32 devices in a mesh: grp: 16 (over z, y, x), blk: 2 (over core).
Axes of the slice: x: 2, y: 2, z: 4, core: 2. Of those that a mesh axis runs over, the one named last changes fastest.
Arguments:
- image: bfloat16 [256, 1024], P(('blk', 'grp')), may hold values from -16 to 16
- text: bfloat16 [256, 1024], P(('grp', 'blk')), may hold values from -16 to 16
- mimage: bfloat16 [256, 1024], P(('blk', 'grp')), may hold values from -16 to 16
- mtext: bfloat16 [256, 1024], P(('grp', 'blk')), may hold values from -16 to 16
Outputs:
- grad_image: float32 [256, 1024], P(('blk', 'grp'))
- grad_text: float32 [256, 1024], P(('grp', 'blk'))
- loss: float32 [], replicated
The draws below stay inside these ranges and needn't reach their ends.
All inputs are finite; a program needn't handle non-finite values.
Results may differ from the reference program's by a relative error of at most 0.0037.
Values may be sent and summed in bfloat16 or wider, within the bound.
A program may use at most 64 MiB of HBM per device.

```python
import math
import jax
import jax.numpy as jnp
from jax import lax

D = 1024
BATCH = 256


def make_pairs(key):
    keys = [jax.random.fold_in(key, 101 + number) for number in range(10)]
    shape = (BATCH, D)
    base_image = jnp.clip(jax.random.normal(keys[0], shape, jnp.float32), -3.0, 3.0)
    base_text = jnp.clip(jax.random.normal(keys[1], shape, jnp.float32), -3.0, 3.0)
    noise_image = jnp.clip(jax.random.normal(keys[2], shape, jnp.float32), -3.0, 3.0)
    noise_text = jnp.clip(jax.random.normal(keys[3], shape, jnp.float32), -3.0, 3.0)
    scale_image = jnp.exp(jax.random.uniform(keys[4], (BATCH, 1), jnp.float32, 0.0, math.log(3.0)))
    scale_text = jnp.exp(jax.random.uniform(keys[5], (BATCH, 1), jnp.float32, 0.0, math.log(3.0)))
    image_out = base_image * scale_image
    text_out = base_text * scale_text
    mimage_out = 0.8 * image_out + 0.6 * noise_image * scale_image
    mtext_out = 0.8 * text_out + 0.6 * noise_text * scale_text
    return (image_out, text_out, mimage_out, mtext_out)


def draw_image(key, part):
    return make_pairs(key)[0].astype(jnp.bfloat16)


def draw_text(key, part):
    return make_pairs(key)[1].astype(jnp.bfloat16)


def draw_mimage(key, part):
    return make_pairs(key)[2].astype(jnp.bfloat16)


def draw_mtext(key, part):
    return make_pairs(key)[3].astype(jnp.bfloat16)


def setup_inputs(seed: int = 0) -> dict:
    key_list = jax.random.split(jax.random.key(seed), 5)
    return {
        "image": draw_image(jax.random.fold_in(key_list[4], 71), 0),
        "text": draw_text(jax.random.fold_in(key_list[4], 71), 0),
        "mimage": draw_mimage(jax.random.fold_in(key_list[4], 71), 0),
        "mtext": draw_mtext(jax.random.fold_in(key_list[4], 71), 0),
    }


mix_weight = 0.4
very_low = -1.0e30


def reference(image, text, mimage, mtext):
    scale_factor = D ** -0.5
    image_all = image.astype(jnp.float32)
    text_all = text.astype(jnp.float32)
    mimage_all = mimage.astype(jnp.float32)
    mtext_all = mtext.astype(jnp.float32)
    block_rows = math.gcd(BATCH, 512)
    block_count = BATCH // block_rows
    column_ids = lax.iota(jnp.int32, BATCH)

    def scores_of(block_index):
        first_row = (block_index * block_rows).astype(jnp.int32)
        image_block = lax.dynamic_slice_in_dim(image_all, first_row, block_rows, 0)
        mimage_block = lax.dynamic_slice_in_dim(mimage_all, first_row, block_rows, 0)
        score_on = jnp.dot(image_block, text_all.T, precision=lax.Precision.HIGHEST) * scale_factor
        score_mom = jnp.dot(mimage_block, mtext_all.T, precision=lax.Precision.HIGHEST) * scale_factor
        return first_row, image_block, score_on, score_mom

    def fold_columns(run_max, run_total, scores):
        new_max = jnp.maximum(run_max, jnp.max(scores, axis=0))
        new_total = run_total * jnp.exp(run_max - new_max) + jnp.sum(jnp.exp(scores - new_max[None, :]), axis=0)
        return new_max, new_total

    def row_lse(scores):
        top_row = jnp.max(scores, axis=1)
        return top_row + jnp.log(jnp.sum(jnp.exp(scores - top_row[:, None]), axis=1))

    def first_pass(carry, block_index):
        cmax_on, csum_on, cmax_mom, csum_mom = carry
        first_row, image_block, score_on, score_mom = scores_of(block_index)
        cmax_on, csum_on = fold_columns(cmax_on, csum_on, score_on)
        cmax_mom, csum_mom = fold_columns(cmax_mom, csum_mom, score_mom)
        return (cmax_on, csum_on, cmax_mom, csum_mom), (row_lse(score_on), row_lse(score_mom))

    low_cols = jnp.full((BATCH,), very_low, jnp.float32)
    zero_cols = jnp.zeros((BATCH,), jnp.float32)
    blocks = jnp.arange(block_count, dtype=jnp.int32)
    col_stats, row_parts = lax.scan(first_pass, (low_cols, zero_cols, low_cols, zero_cols), blocks)
    col_online = col_stats[0] + jnp.log(col_stats[1])
    col_momentum = col_stats[2] + jnp.log(col_stats[3])
    row_online = row_parts[0].reshape(BATCH)
    row_momentum = row_parts[1].reshape(BATCH)

    def second_pass(carry, block_index):
        grad_text_acc, cross_term = carry
        first_row, image_block, score_on, score_mom = scores_of(block_index)
        row_on = lax.dynamic_slice_in_dim(row_online, first_row, block_rows, 0)
        row_mom = lax.dynamic_slice_in_dim(row_momentum, first_row, block_rows, 0)
        row_ids = first_row + lax.iota(jnp.int32, block_rows)
        diagonal = (row_ids[:, None] == column_ids[None, :]).astype(jnp.float32)
        prob_row = jnp.exp(score_on - row_on[:, None])
        prob_col = jnp.exp(score_on - col_online[None, :])
        target_row = mix_weight * jnp.exp(score_mom - row_mom[:, None]) + (1.0 - mix_weight) * diagonal
        target_col = mix_weight * jnp.exp(score_mom - col_momentum[None, :]) + (1.0 - mix_weight) * diagonal
        grad_tile = 0.5 * ((prob_row - target_row) + (prob_col - target_col))
        grad_round = lax.optimization_barrier(grad_tile.astype(jnp.bfloat16)).astype(jnp.float32)
        grad_rows = jnp.dot(grad_round, text_all, precision=lax.Precision.HIGHEST)
        grad_text_acc = grad_text_acc + jnp.dot(grad_round.T, image_block, precision=lax.Precision.HIGHEST)
        cross_term = cross_term + jnp.sum((target_row + target_col) * score_on)
        return (grad_text_acc, cross_term), grad_rows

    start_carry = (jnp.zeros((BATCH, D), jnp.float32), jnp.zeros((), jnp.float32))
    final_carry, grad_blocks = lax.scan(second_pass, start_carry, blocks)
    grad_image = grad_blocks.reshape(BATCH, D)
    grad_text = final_carry[0]
    loss = (jnp.sum(row_online) + jnp.sum(col_online) - final_carry[1]) / (2.0 * BATCH)
    return grad_image, grad_text, loss
```

```python
import functools

import jax
import jax.numpy as jnp
from jax import lax
from jax.experimental import pallas as pl
from jax.experimental.pallas import tpu as pltpu
from jax.sharding import PartitionSpec as P

mix_weight = 0.4
very_low = -1e30
MESH = pl.DeviceIdType.MESH
f32 = jnp.float32
bf16 = jnp.bfloat16


def lines_of(grp, blk):
    fine = 1
    while fine * blk < grp // fine and grp % (2 * fine) == 0:
        fine *= 2
    return fine


def split_index(index, size):
    if size & (size - 1) == 0:
        return index >> (size.bit_length() - 1), index & (size - 1)
    return lax.div(index, size), lax.rem(index, size)


def kernel(
    grp, blk, fine, rows,
    image_ref, text_ref, mimage_ref, mtext_ref,
    grad_image_ref, grad_text_ref, loss_ref,
    images, texts, image_stats, text_stats, partial, image_out, text_out,
    image_in, text_in, plane_loss_out, line_loss_out, plane_loss, line_loss,
    plane_send, plane_recv, line_send, line_recv,
):
    n_plane, n_line = fine * blk, grp // fine
    width = image_ref.shape[1]
    half = width // 2
    lanes = images.shape[0] * images.shape[1]
    text_rows = n_line * rows
    text_lanes = text_stats.shape[2]
    my_grp, my_blk = lax.axis_index("grp"), lax.axis_index("blk")
    my_line, my_fine = lax.div(my_grp, fine), lax.rem(my_grp, fine)
    my_plane = my_fine * blk + my_blk

    def plane_peer(step):
        rank = lax.rem(my_plane + step, n_plane)
        return rank, (my_line * fine + lax.div(rank, blk), lax.rem(rank, blk))

    def line_peer(step):
        rank = lax.rem(my_line + step, n_line)
        return rank, (rank * fine + my_fine, my_blk)

    plane_peers = [plane_peer(step) for step in range(1, n_plane)]
    line_peers = [line_peer(step) for step in range(1, n_line)]

    def to_plane(phase, step, source, target):
        return pltpu.make_async_remote_copy(
            src_ref=source, dst_ref=target,
            send_sem=plane_send.at[phase, step], recv_sem=plane_recv.at[phase, step],
            device_id=plane_peers[step][1], device_id_type=MESH,
        )

    def to_line(phase, step, source, target):
        return pltpu.make_async_remote_copy(
            src_ref=source, dst_ref=target,
            send_sem=line_send.at[phase, step], recv_sem=line_recv.at[phase, step],
            device_id=line_peers[step][1], device_id_type=MESH,
        )

    def start(copies):
        for copy in copies:
            copy.start()

    def arrived(copies):
        for copy in copies:
            copy.wait_recv()

    barrier = pltpu.get_barrier_semaphore()
    for _, peer in plane_peers + line_peers:
        pl.semaphore_signal(barrier, inc=1, device_id=peer, device_id_type=MESH)

    def pair(first, second):
        return jnp.concatenate([first.astype(f32), second.astype(f32)], axis=0).astype(bf16)

    images[my_plane] = pair(image_ref[...], mimage_ref[...])
    texts[my_line] = pair(text_ref[...], mtext_ref[...])
    pl.semaphore_wait(barrier, n_plane + n_line - 2)

    image_copies = [
        to_plane(0, s, images.at[my_plane], images.at[my_plane]) for s in range(n_plane - 1)
    ]
    text_copies = [to_line(0, s, texts.at[my_line], texts.at[my_line]) for s in range(n_line - 1)]
    start(text_copies)
    start(image_copies)

    shape = (text_rows, lanes)
    text_slot, text_sub = split_index(lax.broadcasted_iota(jnp.int32, shape, 0), rows)
    lane_slot, lane_sub = split_index(lax.broadcasted_iota(jnp.int32, shape, 1), 2 * rows)
    online = lane_sub < rows
    lane_fine, lane_blk = split_index(lane_slot, blk)
    image_tile = lane_blk * grp + my_line * fine + lane_fine
    text_tile = (text_slot * fine + my_fine) * blk + my_blk
    same = (image_tile == text_tile) & (lane_sub == text_sub)
    diagonal = jnp.where(same, 1.0, 0.0)
    square = (text_rows, text_lanes)
    eye = lax.broadcasted_iota(jnp.int32, square, 0) == lax.broadcasted_iota(jnp.int32, square, 1)

    def to_lanes(column):
        return jnp.sum(jnp.where(eye, column, 0.0), axis=0, keepdims=True)

    def to_column(row):
        return jnp.sum(jnp.where(eye, row, 0.0), axis=1, keepdims=True)

    arrived(text_copies)
    arrived(image_copies)
    scores = lax.dot_general(
        texts[...].reshape(n_line * 2 * rows, width), images[...].reshape(lanes, width),
        (((1,), (1,)), ((), ())), preferred_element_type=f32,
    ) * (width ** -0.5)
    scores = scores.reshape(n_line, 2, rows, lanes)
    score_on = scores[:, 0].reshape(shape)
    score_mom = pltpu.roll(scores[:, 1].reshape(shape), lanes - rows, 1)
    masked_on = jnp.where(online, score_on, very_low)
    masked_mom = jnp.where(online, score_mom, very_low)

    def stats(on, mom, axis):
        top_on = jnp.max(on, axis=axis, keepdims=True)
        top_mom = jnp.max(mom, axis=axis, keepdims=True)
        spread = jnp.exp(mom - top_mom)
        return (
            top_on, jnp.sum(jnp.exp(on - top_on), axis=axis, keepdims=True),
            top_mom, jnp.sum(spread, axis=axis, keepdims=True),
            jnp.sum(spread * score_on, axis=axis, keepdims=True),
        )

    def message(top_on, sum_on, top_mom, sum_mom, cross, diag):
        line = lax.broadcasted_iota(jnp.int32, (8, top_on.shape[1]), 0)
        tops = jnp.where(line == 0, top_on, jnp.where((line == 1) | (line == 2), top_mom, 0.0))
        sums = jnp.where(line == 0, sum_on, jnp.where(line == 1, sum_mom, 1.0))
        sums = jnp.where(line == 2, cross, jnp.where(line == 3, diag, sums))
        return jnp.concatenate([tops, sums], axis=0)

    def joined(held, count):
        top = held[0, :8]
        for k in range(1, count):
            top = jnp.maximum(top, held[k, :8])
        total = held[0, 8:] * jnp.exp(held[0, :8] - top)
        for k in range(1, count):
            total = total + held[k, 8:] * jnp.exp(held[k, :8] - top)
        return top + jnp.log(total), total

    text_part = [to_lanes(column) for column in stats(masked_on, masked_mom, 1)]
    in_text = lax.broadcasted_iota(jnp.int32, (1, text_lanes), 1) < text_rows
    for k in (1, 3):
        text_part[k] = jnp.where(in_text, text_part[k], 1.0)
    text_stats[my_line] = message(*text_part, jnp.zeros((1, text_lanes), f32))
    text_copies_1 = [
        to_line(1, s, text_stats.at[my_line], text_stats.at[my_line]) for s in range(n_line - 1)
    ]
    start(text_copies_1)
    diag = jnp.sum(diagonal * score_on, axis=0, keepdims=True)
    image_stats[my_plane] = message(*stats(score_on, score_mom, 0), diag)
    image_copies_1 = [
        to_plane(1, s, image_stats.at[my_plane], image_stats.at[my_plane])
        for s in range(n_plane - 1)
    ]
    start(image_copies_1)
    arrived(text_copies_1)
    text_lse, text_total = joined(text_stats, n_line)
    col_on, col_mom = to_column(text_lse[0:1]), to_column(text_lse[1:2])
    prob_col = jnp.exp(masked_on - col_on)
    target_col = mix_weight * jnp.exp(masked_mom - col_mom) + (1.0 - mix_weight) * diagonal
    arrived(image_copies_1)
    image_lse, image_total = joined(image_stats, n_plane)
    prob_row = jnp.exp(score_on - image_lse[0:1])
    target_row = (
        mix_weight * jnp.exp(score_mom - image_lse[1:2]) + (1.0 - mix_weight) * diagonal
    )
    grad = 0.5 * ((prob_row - target_row) + (prob_col - target_col))
    grad = jnp.where(online, grad, 0.0)

    spaced = jnp.concatenate(
        [grad.reshape(n_line, 1, rows, lanes), jnp.zeros((n_line, 1, rows, lanes), f32)], axis=1
    ).reshape(n_line * 2 * rows, lanes)
    partial[...] = lax.dot_general(
        spaced.astype(bf16), texts[...].reshape(n_line * 2 * rows, width),
        (((0,), (0,)), ((), ())), preferred_element_type=f32,
    ).reshape(n_plane, 2 * rows, width)

    def folded(value):
        return jnp.concatenate([value[:, :half], value[:, half:]], axis=0).astype(bf16)

    image_copies_2 = []
    for s in range(n_plane - 1):
        image_out[s] = folded(partial[plane_peers[s][0], :rows, :])
        copy = to_plane(2, s, image_out.at[s], image_in.at[s])
        copy.start()
        image_copies_2.append(copy)

    text_share = jnp.dot(
        grad.astype(bf16), images[...].reshape(lanes, width), preferred_element_type=f32
    )
    own_image = partial[my_plane, :rows, :]
    partial[pl.ds(0, n_line), :rows, :] = text_share.reshape(n_line, rows, width)
    text_copies_2 = []
    for s in range(n_line - 1):
        text_out[s] = folded(partial[line_peers[s][0], :rows, :])
        copy = to_line(2, s, text_out.at[s], text_in.at[s])
        copy.start()
        text_copies_2.append(copy)
    own_text = partial[my_line, :rows, :]

    def shares(lse, total, valid):
        share = lse[0:1] - mix_weight * (total[2:3] / total[1:2])
        return jnp.where(valid, share, 0.0)

    image_share = shares(image_lse, image_total, online[0:1])
    image_share = image_share - jnp.where(
        online[0:1], 2.0 * (1.0 - mix_weight) * image_total[3:4], 0.0
    )
    text_loss = shares(text_lse, text_total, in_text)
    line = lax.broadcasted_iota(jnp.int32, (8, lanes), 0)
    line_loss_out[...] = jnp.where(line == 0, image_share, 0.0)
    line = lax.broadcasted_iota(jnp.int32, (8, text_lanes), 0)
    plane_loss_out[...] = jnp.where(line == 0, text_loss, 0.0)
    line_copies_3 = [
        to_line(3, s, line_loss_out, line_loss.at[s]) for s in range(n_line - 1)
    ]
    plane_copies_3 = [
        to_plane(3, s, plane_loss_out, plane_loss.at[s]) for s in range(n_plane - 1)
    ]
    start(line_copies_3)
    start(plane_copies_3)

    def gathered(own, held, count):
        total = jnp.concatenate([own[:, :half], own[:, half:]], axis=0)
        for s in range(count):
            total = total + held[s].astype(f32)
        return jnp.concatenate([total[:rows], total[rows:]], axis=1)

    arrived(image_copies_2)
    grad_image_ref[...] = gathered(own_image, image_in, n_plane - 1)
    arrived(text_copies_2)
    grad_text_ref[...] = gathered(own_text, text_in, n_line - 1)
    arrived(line_copies_3)
    arrived(plane_copies_3)
    image_loss = line_loss_out[...]
    for s in range(n_line - 1):
        image_loss = image_loss + line_loss[s]
    text_loss = plane_loss_out[...]
    for s in range(n_plane - 1):
        text_loss = text_loss + plane_loss[s]
    total = jnp.sum(image_loss, keepdims=True) + jnp.sum(text_loss, keepdims=True)
    loss_ref[...] = total / (2.0 * rows * grp * blk)

    for copy in (
        image_copies + text_copies + image_copies_1 + text_copies_1
        + image_copies_2 + text_copies_2 + line_copies_3 + plane_copies_3
    ):
        copy.wait_send()


def local(grp, blk, image, text, mimage, mtext):
    rows, width = image.shape
    fine = lines_of(grp, blk)
    n_plane, n_line = fine * blk, grp // fine
    lanes = n_plane * 2 * rows
    text_lanes = -(-n_line * rows // 128) * 128
    in_vmem = pl.BlockSpec(memory_space=pltpu.VMEM)
    grad_image, grad_text, loss = pl.pallas_call(
        functools.partial(kernel, grp, blk, fine, rows),
        out_shape=(
            jax.ShapeDtypeStruct((rows, width), f32),
            jax.ShapeDtypeStruct((rows, width), f32),
            jax.ShapeDtypeStruct((1, 1), f32),
        ),
        in_specs=[in_vmem] * 4,
        out_specs=(in_vmem, in_vmem, in_vmem),
        scratch_shapes=[
            pltpu.VMEM((n_plane, 2 * rows, width), bf16),
            pltpu.VMEM((n_line, 2 * rows, width), bf16),
            pltpu.VMEM((n_plane, 16, lanes), f32),
            pltpu.VMEM((n_line, 16, text_lanes), f32),
            pltpu.VMEM((max(n_plane, n_line), 2 * rows, width), f32),
            pltpu.VMEM((n_plane - 1, 2 * rows, width // 2), bf16),
            pltpu.VMEM((n_line - 1, 2 * rows, width // 2), bf16),
            pltpu.VMEM((n_plane - 1, 2 * rows, width // 2), bf16),
            pltpu.VMEM((n_line - 1, 2 * rows, width // 2), bf16),
            pltpu.VMEM((8, text_lanes), f32),
            pltpu.VMEM((8, lanes), f32),
            pltpu.VMEM((n_plane - 1, 8, text_lanes), f32),
            pltpu.VMEM((n_line - 1, 8, lanes), f32),
            pltpu.SemaphoreType.DMA((4, n_plane - 1)),
            pltpu.SemaphoreType.DMA((4, n_plane - 1)),
            pltpu.SemaphoreType.DMA((4, n_line - 1)),
            pltpu.SemaphoreType.DMA((4, n_line - 1)),
        ],
        compiler_params=pltpu.CompilerParams(
            collective_id=0, has_side_effects=True, vmem_limit_bytes=32 * 1024 * 1024
        ),
    )(image, text, mimage, mtext)
    return grad_image, grad_text, loss.reshape(())


def solution(mesh):
    in_specs = (
        P(("blk", "grp"), None),
        P(("grp", "blk"), None),
        P(("blk", "grp"), None),
        P(("grp", "blk"), None),
    )
    out_specs = (P(("blk", "grp"), None), P(("grp", "blk"), None), P())
    run = functools.partial(local, mesh.shape["grp"], mesh.shape["blk"])
    return jax.shard_map(run, mesh=mesh, in_specs=in_specs, out_specs=out_specs, check_vma=False)
```

```python
import functools

import jax
import jax.numpy as jnp
from jax import lax
from jax.experimental import pallas as pl
from jax.experimental.pallas import tpu as pltpu
from jax.sharding import PartitionSpec as P

mix_weight = 0.4
very_low = -1e30
MESH = pl.DeviceIdType.MESH
f32 = jnp.float32
bf16 = jnp.bfloat16


def lines_of(grp, blk):
    fine = 1
    while fine * blk < grp // fine and grp % (2 * fine) == 0:
        fine *= 2
    return fine


def split_index(index, size):
    if size & (size - 1) == 0:
        return index >> (size.bit_length() - 1), index & (size - 1)
    return lax.div(index, size), lax.rem(index, size)


def kernel(
    grp, blk, fine, rows,
    image_ref, text_ref, mimage_ref, mtext_ref,
    grad_image_ref, grad_text_ref, loss_ref,
    images, texts, image_stats, text_stats, plane_partial, line_partial, image_out, text_out,
    image_in, text_in, plane_loss_out, line_loss_out, plane_loss, line_loss,
    plane_send, plane_recv, line_send, line_recv, fetched, fetch_sem,
):
    fetches = [
        pltpu.make_async_copy(ref, fetched.at[k], fetch_sem.at[k])
        for k, ref in enumerate((text_ref, mtext_ref, image_ref, mimage_ref))
    ]
    for copy in fetches:
        copy.start()
    n_plane, n_line = fine * blk, grp // fine
    width = image_ref.shape[1]
    half = width // 2
    lanes = images.shape[0] * images.shape[1]
    text_rows = n_line * rows
    text_lanes = text_stats.shape[2]
    my_grp, my_blk = lax.axis_index("grp"), lax.axis_index("blk")
    my_line, my_fine = lax.div(my_grp, fine), lax.rem(my_grp, fine)
    my_plane = my_fine * blk + my_blk

    def plane_peer(step):
        rank = lax.rem(my_plane + step, n_plane)
        return rank, (my_line * fine + lax.div(rank, blk), lax.rem(rank, blk))

    def line_peer(step):
        rank = lax.rem(my_line + step, n_line)
        return rank, (rank * fine + my_fine, my_blk)

    plane_peers = [plane_peer(step) for step in range(1, n_plane)]
    line_peers = [line_peer(step) for step in range(1, n_line)]

    def to_plane(phase, step, source, target):
        return pltpu.make_async_remote_copy(
            src_ref=source, dst_ref=target,
            send_sem=plane_send.at[phase, step], recv_sem=plane_recv.at[phase, step],
            device_id=plane_peers[step][1], device_id_type=MESH,
        )

    def to_line(phase, step, source, target):
        return pltpu.make_async_remote_copy(
            src_ref=source, dst_ref=target,
            send_sem=line_send.at[phase, step], recv_sem=line_recv.at[phase, step],
            device_id=line_peers[step][1], device_id_type=MESH,
        )

    def start(copies):
        for copy in copies:
            copy.start()

    def arrived(copies):
        for copy in copies:
            copy.wait_recv()

    barrier = pltpu.get_barrier_semaphore()
    for _, peer in plane_peers + line_peers:
        pl.semaphore_signal(barrier, inc=1, device_id=peer, device_id_type=MESH)

    def pair(first, second):
        return jnp.concatenate([first.astype(f32), second.astype(f32)], axis=0).astype(bf16)

    for copy in fetches:
        copy.wait()
    texts[my_line] = pair(fetched[0], fetched[1])
    images[my_plane] = pair(fetched[2], fetched[3])
    pl.semaphore_wait(barrier, n_plane + n_line - 2)

    image_copies = [
        to_plane(0, s, images.at[my_plane], images.at[my_plane]) for s in range(n_plane - 1)
    ]
    text_copies = [to_line(0, s, texts.at[my_line], texts.at[my_line]) for s in range(n_line - 1)]
    start(text_copies)
    start(image_copies)

    shape = (text_rows, lanes)
    text_slot, text_sub = split_index(lax.broadcasted_iota(jnp.int32, shape, 0), rows)
    lane_slot, lane_sub = split_index(lax.broadcasted_iota(jnp.int32, shape, 1), 2 * rows)
    online = lane_sub < rows
    lane_fine, lane_blk = split_index(lane_slot, blk)
    image_tile = lane_blk * grp + my_line * fine + lane_fine
    text_tile = (text_slot * fine + my_fine) * blk + my_blk
    same = (image_tile == text_tile) & (lane_sub == text_sub)
    diagonal = jnp.where(same, 1.0, 0.0)
    square = (text_rows, text_lanes)
    eye = lax.broadcasted_iota(jnp.int32, square, 0) == lax.broadcasted_iota(jnp.int32, square, 1)

    def to_lanes(column):
        return jnp.sum(jnp.where(eye, column, 0.0), axis=0, keepdims=True)

    def to_column(row):
        return jnp.sum(jnp.where(eye, row, 0.0), axis=1, keepdims=True)

    arrived(text_copies)
    arrived(image_copies)
    scores = lax.dot_general(
        texts[...].reshape(n_line * 2 * rows, width), images[...].reshape(lanes, width),
        (((1,), (1,)), ((), ())), preferred_element_type=f32,
    ) * (width ** -0.5)
    scores = scores.reshape(n_line, 2, rows, lanes)
    score_on = scores[:, 0].reshape(shape)
    score_mom = pltpu.roll(scores[:, 1].reshape(shape), lanes - rows, 1)
    masked_on = jnp.where(online, score_on, very_low)
    masked_mom = jnp.where(online, score_mom, very_low)

    def stats(on, mom, axis):
        top_on = jnp.max(on, axis=axis, keepdims=True)
        top_mom = jnp.max(mom, axis=axis, keepdims=True)
        spread = jnp.exp(mom - top_mom)
        return (
            top_on, jnp.sum(jnp.exp(on - top_on), axis=axis, keepdims=True),
            top_mom, jnp.sum(spread, axis=axis, keepdims=True),
            jnp.sum(spread * score_on, axis=axis, keepdims=True),
        )

    def message(top_on, sum_on, top_mom, sum_mom, cross, diag):
        line = lax.broadcasted_iota(jnp.int32, (8, top_on.shape[1]), 0)
        tops = jnp.where(line == 0, top_on, jnp.where((line == 1) | (line == 2), top_mom, 0.0))
        sums = jnp.where(line == 0, sum_on, jnp.where(line == 1, sum_mom, 1.0))
        sums = jnp.where(line == 2, cross, jnp.where(line == 3, diag, sums))
        return jnp.concatenate([tops, sums], axis=0)

    def joined(held, count):
        top = held[0, :8]
        for k in range(1, count):
            top = jnp.maximum(top, held[k, :8])
        total = held[0, 8:] * jnp.exp(held[0, :8] - top)
        for k in range(1, count):
            total = total + held[k, 8:] * jnp.exp(held[k, :8] - top)
        return top + jnp.log(total), total

    text_part = [to_lanes(column) for column in stats(masked_on, masked_mom, 1)]
    in_text = lax.broadcasted_iota(jnp.int32, (1, text_lanes), 1) < text_rows
    for k in (1, 3):
        text_part[k] = jnp.where(in_text, text_part[k], 1.0)
    text_stats[my_line] = message(*text_part, jnp.zeros((1, text_lanes), f32))
    text_copies_1 = [
        to_line(1, s, text_stats.at[my_line], text_stats.at[my_line]) for s in range(n_line - 1)
    ]
    start(text_copies_1)
    diag = jnp.sum(diagonal * score_on, axis=0, keepdims=True)
    image_stats[my_plane] = message(*stats(score_on, score_mom, 0), diag)
    image_copies_1 = [
        to_plane(1, s, image_stats.at[my_plane], image_stats.at[my_plane])
        for s in range(n_plane - 1)
    ]
    start(image_copies_1)
    arrived(text_copies_1)
    text_lse, text_total = joined(text_stats, n_line)
    col_on, col_mom = to_column(text_lse[0:1]), to_column(text_lse[1:2])
    prob_col = jnp.exp(masked_on - col_on)
    target_col = mix_weight * jnp.exp(masked_mom - col_mom) + (1.0 - mix_weight) * diagonal
    arrived(image_copies_1)
    image_lse, image_total = joined(image_stats, n_plane)
    prob_row = jnp.exp(score_on - image_lse[0:1])
    target_row = (
        mix_weight * jnp.exp(score_mom - image_lse[1:2]) + (1.0 - mix_weight) * diagonal
    )
    grad = 0.5 * ((prob_row - target_row) + (prob_col - target_col))
    grad = jnp.where(online, grad, 0.0)

    def folded(value):
        return jnp.concatenate([value[:, :half], value[:, half:]], axis=0).astype(bf16)

    line_partial[...] = jnp.dot(
        grad.astype(bf16), images[...].reshape(lanes, width), preferred_element_type=f32
    ).reshape(n_line, rows, width)
    text_copies_2 = []
    for s in range(n_line - 1):
        text_out[s] = folded(line_partial[line_peers[s][0]])
        copy = to_line(2, s, text_out.at[s], text_in.at[s])
        copy.start()
        text_copies_2.append(copy)
    spaced = jnp.concatenate(
        [grad.reshape(n_line, 1, rows, lanes), jnp.zeros((n_line, 1, rows, lanes), f32)], axis=1
    ).reshape(n_line * 2 * rows, lanes)
    plane_partial[...] = lax.dot_general(
        spaced.astype(bf16), texts[...].reshape(n_line * 2 * rows, width),
        (((0,), (0,)), ((), ())), preferred_element_type=f32,
    ).reshape(n_plane, 2 * rows, width)
    image_copies_2 = []
    for s in range(n_plane - 1):
        image_out[s] = folded(plane_partial[plane_peers[s][0], :rows, :])
        copy = to_plane(2, s, image_out.at[s], image_in.at[s])
        copy.start()
        image_copies_2.append(copy)

    def shares(lse, total, valid):
        share = lse[0:1] - mix_weight * (total[2:3] / total[1:2])
        return jnp.where(valid, share, 0.0)

    image_share = shares(image_lse, image_total, online[0:1])
    image_share = image_share - jnp.where(
        online[0:1], 2.0 * (1.0 - mix_weight) * image_total[3:4], 0.0
    )
    text_loss = shares(text_lse, text_total, in_text)
    line = lax.broadcasted_iota(jnp.int32, (8, lanes), 0)
    line_loss_out[...] = jnp.where(line == 0, image_share, 0.0)
    line = lax.broadcasted_iota(jnp.int32, (8, text_lanes), 0)
    plane_loss_out[...] = jnp.where(line == 0, text_loss, 0.0)
    line_copies_3 = [
        to_line(3, s, line_loss_out, line_loss.at[s]) for s in range(n_line - 1)
    ]
    plane_copies_3 = [
        to_plane(3, s, plane_loss_out, plane_loss.at[s]) for s in range(n_plane - 1)
    ]
    start(line_copies_3)
    start(plane_copies_3)

    def gathered(own, held, count):
        total = jnp.concatenate([own[:, :half], own[:, half:]], axis=0)
        for s in range(count):
            total = total + held[s].astype(f32)
        return jnp.concatenate([total[:rows], total[rows:]], axis=1)

    arrived(text_copies_2)
    grad_text_ref[...] = gathered(line_partial[my_line], text_in, n_line - 1)
    arrived(image_copies_2)
    grad_image_ref[...] = gathered(plane_partial[my_plane, :rows, :], image_in, n_plane - 1)
    arrived(line_copies_3)
    arrived(plane_copies_3)
    image_loss = line_loss_out[...]
    for s in range(n_line - 1):
        image_loss = image_loss + line_loss[s]
    text_loss = plane_loss_out[...]
    for s in range(n_plane - 1):
        text_loss = text_loss + plane_loss[s]
    total = jnp.sum(image_loss, keepdims=True) + jnp.sum(text_loss, keepdims=True)
    loss_ref[...] = total / (2.0 * rows * grp * blk)

    for copy in (
        image_copies + text_copies + image_copies_1 + text_copies_1
        + image_copies_2 + text_copies_2 + line_copies_3 + plane_copies_3
    ):
        copy.wait_send()


def local(grp, blk, image, text, mimage, mtext):
    rows, width = image.shape
    fine = lines_of(grp, blk)
    n_plane, n_line = fine * blk, grp // fine
    lanes = n_plane * 2 * rows
    text_lanes = -(-n_line * rows // 128) * 128
    in_vmem = pl.BlockSpec(memory_space=pltpu.VMEM)
    grad_image, grad_text, loss = pl.pallas_call(
        functools.partial(kernel, grp, blk, fine, rows),
        out_shape=(
            jax.ShapeDtypeStruct((rows, width), f32),
            jax.ShapeDtypeStruct((rows, width), f32),
            jax.ShapeDtypeStruct((1, 1), f32),
        ),
        in_specs=[pl.BlockSpec(memory_space=pltpu.HBM)] * 4,
        out_specs=(in_vmem, in_vmem, in_vmem),
        scratch_shapes=[
            pltpu.VMEM((n_plane, 2 * rows, width), bf16),
            pltpu.VMEM((n_line, 2 * rows, width), bf16),
            pltpu.VMEM((n_plane, 16, lanes), f32),
            pltpu.VMEM((n_line, 16, text_lanes), f32),
            pltpu.VMEM((n_plane, 2 * rows, width), f32),
            pltpu.VMEM((n_line, rows, width), f32),
            pltpu.VMEM((n_plane - 1, 2 * rows, width // 2), bf16),
            pltpu.VMEM((n_line - 1, 2 * rows, width // 2), bf16),
            pltpu.VMEM((n_plane - 1, 2 * rows, width // 2), bf16),
            pltpu.VMEM((n_line - 1, 2 * rows, width // 2), bf16),
            pltpu.VMEM((8, text_lanes), f32),
            pltpu.VMEM((8, lanes), f32),
            pltpu.VMEM((n_plane - 1, 8, text_lanes), f32),
            pltpu.VMEM((n_line - 1, 8, lanes), f32),
            pltpu.SemaphoreType.DMA((4, n_plane - 1)),
            pltpu.SemaphoreType.DMA((4, n_plane - 1)),
            pltpu.SemaphoreType.DMA((4, n_line - 1)),
            pltpu.SemaphoreType.DMA((4, n_line - 1)),
            pltpu.VMEM((4, rows, width), bf16),
            pltpu.SemaphoreType.DMA((4,)),
        ],
        compiler_params=pltpu.CompilerParams(
            collective_id=0, has_side_effects=True, vmem_limit_bytes=32 * 1024 * 1024
        ),
    )(image, text, mimage, mtext)
    return grad_image, grad_text, loss.reshape(())


def solution(mesh):
    in_specs = (
        P(("blk", "grp"), None),
        P(("grp", "blk"), None),
        P(("blk", "grp"), None),
        P(("grp", "blk"), None),
    )
    out_specs = (P(("blk", "grp"), None), P(("grp", "blk"), None), P())
    run = functools.partial(local, mesh.shape["grp"], mesh.shape["blk"])
    return jax.shard_map(run, mesh=mesh, in_specs=in_specs, out_specs=out_specs, check_vma=False)
```

```python
import functools

import jax
import jax.numpy as jnp
from jax import lax
from jax.experimental import pallas as pl
from jax.experimental.pallas import tpu as pltpu
from jax.sharding import PartitionSpec as P

mix_weight = 0.4
very_low = -1e30
MESH = pl.DeviceIdType.MESH
f32 = jnp.float32
bf16 = jnp.bfloat16


def lines_of(grp, blk):
    fine = 1
    while fine * blk < grp // fine and grp % (2 * fine) == 0:
        fine *= 2
    return fine


def split_index(index, size):
    if size & (size - 1) == 0:
        return index >> (size.bit_length() - 1), index & (size - 1)
    return lax.div(index, size), lax.rem(index, size)


def kernel(
    grp, blk, fine, rows,
    image_ref, text_ref, mimage_ref, mtext_ref,
    grad_image_ref, grad_text_ref, loss_ref,
    images, texts, image_stats, text_stats, plane_partial, line_partial, image_out, text_out,
    image_in, text_in, plane_loss_out, line_loss_out, plane_loss, line_loss,
    plane_send, plane_recv, line_send, line_recv, fetched, fetch_sem, result, result_sem,
):
    fetches = [
        pltpu.make_async_copy(ref, fetched.at[k], fetch_sem.at[k])
        for k, ref in enumerate((text_ref, mtext_ref, image_ref, mimage_ref))
    ]
    for copy in fetches:
        copy.start()
    n_plane, n_line = fine * blk, grp // fine
    width = image_ref.shape[1]
    half = width // 2
    lanes = images.shape[0] * images.shape[1]
    text_rows = n_line * rows
    text_lanes = text_stats.shape[2]
    my_grp, my_blk = lax.axis_index("grp"), lax.axis_index("blk")
    my_line, my_fine = lax.div(my_grp, fine), lax.rem(my_grp, fine)
    my_plane = my_fine * blk + my_blk

    def plane_peer(step):
        rank = lax.rem(my_plane + step, n_plane)
        return rank, (my_line * fine + lax.div(rank, blk), lax.rem(rank, blk))

    def line_peer(step):
        rank = lax.rem(my_line + step, n_line)
        return rank, (rank * fine + my_fine, my_blk)

    plane_peers = [plane_peer(step) for step in range(1, n_plane)]
    line_peers = [line_peer(step) for step in range(1, n_line)]

    def to_plane(phase, step, source, target):
        return pltpu.make_async_remote_copy(
            src_ref=source, dst_ref=target,
            send_sem=plane_send.at[phase, step], recv_sem=plane_recv.at[phase, step],
            device_id=plane_peers[step][1], device_id_type=MESH,
        )

    def to_line(phase, step, source, target):
        return pltpu.make_async_remote_copy(
            src_ref=source, dst_ref=target,
            send_sem=line_send.at[phase, step], recv_sem=line_recv.at[phase, step],
            device_id=line_peers[step][1], device_id_type=MESH,
        )

    def start(copies):
        for copy in copies:
            copy.start()

    def arrived(copies):
        for copy in copies:
            copy.wait_recv()

    barrier = pltpu.get_barrier_semaphore()
    for _, peer in plane_peers + line_peers:
        pl.semaphore_signal(barrier, inc=1, device_id=peer, device_id_type=MESH)

    def pair(first, second):
        return jnp.concatenate([first.astype(f32), second.astype(f32)], axis=0).astype(bf16)

    for copy in fetches:
        copy.wait()
    texts[my_line] = pair(fetched[0], fetched[1])
    images[my_plane] = pair(fetched[2], fetched[3])
    pl.semaphore_wait(barrier, n_plane + n_line - 2)

    image_copies = [
        to_plane(0, s, images.at[my_plane], images.at[my_plane]) for s in range(n_plane - 1)
    ]
    text_copies = [to_line(0, s, texts.at[my_line], texts.at[my_line]) for s in range(n_line - 1)]
    start(text_copies)
    start(image_copies)

    shape = (text_rows, lanes)
    text_slot, text_sub = split_index(lax.broadcasted_iota(jnp.int32, shape, 0), rows)
    lane_slot, lane_sub = split_index(lax.broadcasted_iota(jnp.int32, shape, 1), 2 * rows)
    online = lane_sub < rows
    lane_fine, lane_blk = split_index(lane_slot, blk)
    image_tile = lane_blk * grp + my_line * fine + lane_fine
    text_tile = (text_slot * fine + my_fine) * blk + my_blk
    same = (image_tile == text_tile) & (lane_sub == text_sub)
    diagonal = jnp.where(same, 1.0, 0.0)
    square = (text_rows, text_lanes)
    eye = lax.broadcasted_iota(jnp.int32, square, 0) == lax.broadcasted_iota(jnp.int32, square, 1)

    def to_lanes(column):
        return jnp.sum(jnp.where(eye, column, 0.0), axis=0, keepdims=True)

    def to_column(row):
        return jnp.sum(jnp.where(eye, row, 0.0), axis=1, keepdims=True)

    arrived(text_copies)
    arrived(image_copies)
    scores = lax.dot_general(
        texts[...].reshape(n_line * 2 * rows, width), images[...].reshape(lanes, width),
        (((1,), (1,)), ((), ())), preferred_element_type=f32,
    ) * (width ** -0.5)
    scores = scores.reshape(n_line, 2, rows, lanes)
    score_on = scores[:, 0].reshape(shape)
    score_mom = pltpu.roll(scores[:, 1].reshape(shape), lanes - rows, 1)
    masked_on = jnp.where(online, score_on, very_low)
    masked_mom = jnp.where(online, score_mom, very_low)

    def stats(on, mom, axis):
        top_on = jnp.max(on, axis=axis, keepdims=True)
        top_mom = jnp.max(mom, axis=axis, keepdims=True)
        spread = jnp.exp(mom - top_mom)
        return (
            top_on, jnp.sum(jnp.exp(on - top_on), axis=axis, keepdims=True),
            top_mom, jnp.sum(spread, axis=axis, keepdims=True),
            jnp.sum(spread * score_on, axis=axis, keepdims=True),
        )

    def message(top_on, sum_on, top_mom, sum_mom, cross, diag):
        line = lax.broadcasted_iota(jnp.int32, (8, top_on.shape[1]), 0)
        tops = jnp.where(line == 0, top_on, jnp.where((line == 1) | (line == 2), top_mom, 0.0))
        sums = jnp.where(line == 0, sum_on, jnp.where(line == 1, sum_mom, 1.0))
        sums = jnp.where(line == 2, cross, jnp.where(line == 3, diag, sums))
        return jnp.concatenate([tops, sums], axis=0)

    def joined(held, count):
        top = held[0, :8]
        for k in range(1, count):
            top = jnp.maximum(top, held[k, :8])
        total = held[0, 8:] * jnp.exp(held[0, :8] - top)
        for k in range(1, count):
            total = total + held[k, 8:] * jnp.exp(held[k, :8] - top)
        return top + jnp.log(total), total

    text_part = [to_lanes(column) for column in stats(masked_on, masked_mom, 1)]
    in_text = lax.broadcasted_iota(jnp.int32, (1, text_lanes), 1) < text_rows
    for k in (1, 3):
        text_part[k] = jnp.where(in_text, text_part[k], 1.0)
    text_stats[my_line] = message(*text_part, jnp.zeros((1, text_lanes), f32))
    text_copies_1 = [
        to_line(1, s, text_stats.at[my_line], text_stats.at[my_line]) for s in range(n_line - 1)
    ]
    start(text_copies_1)
    diag = jnp.sum(diagonal * score_on, axis=0, keepdims=True)
    image_stats[my_plane] = message(*stats(score_on, score_mom, 0), diag)
    image_copies_1 = [
        to_plane(1, s, image_stats.at[my_plane], image_stats.at[my_plane])
        for s in range(n_plane - 1)
    ]
    start(image_copies_1)
    arrived(text_copies_1)
    text_lse, text_total = joined(text_stats, n_line)
    col_on, col_mom = to_column(text_lse[0:1]), to_column(text_lse[1:2])
    prob_col = jnp.exp(masked_on - col_on)
    target_col = mix_weight * jnp.exp(masked_mom - col_mom) + (1.0 - mix_weight) * diagonal
    arrived(image_copies_1)
    image_lse, image_total = joined(image_stats, n_plane)
    prob_row = jnp.exp(score_on - image_lse[0:1])
    target_row = (
        mix_weight * jnp.exp(score_mom - image_lse[1:2]) + (1.0 - mix_weight) * diagonal
    )
    grad = 0.5 * ((prob_row - target_row) + (prob_col - target_col))
    grad = jnp.where(online, grad, 0.0)

    def folded(value):
        return jnp.concatenate([value[:, :half], value[:, half:]], axis=0).astype(bf16)

    line_partial[...] = jnp.dot(
        grad.astype(bf16), images[...].reshape(lanes, width), preferred_element_type=f32
    ).reshape(n_line, rows, width)
    text_copies_2 = []
    for s in range(n_line - 1):
        text_out[s] = folded(line_partial[line_peers[s][0]])
        copy = to_line(2, s, text_out.at[s], text_in.at[s])
        copy.start()
        text_copies_2.append(copy)
    spaced = jnp.concatenate(
        [grad.reshape(n_line, 1, rows, lanes), jnp.zeros((n_line, 1, rows, lanes), f32)], axis=1
    ).reshape(n_line * 2 * rows, lanes)
    plane_partial[...] = lax.dot_general(
        spaced.astype(bf16), texts[...].reshape(n_line * 2 * rows, width),
        (((0,), (0,)), ((), ())), preferred_element_type=f32,
    ).reshape(n_plane, 2 * rows, width)
    image_copies_2 = []
    for s in range(n_plane - 1):
        image_out[s] = folded(plane_partial[plane_peers[s][0], :rows, :])
        copy = to_plane(2, s, image_out.at[s], image_in.at[s])
        copy.start()
        image_copies_2.append(copy)

    def shares(lse, total, valid):
        share = lse[0:1] - mix_weight * (total[2:3] / total[1:2])
        return jnp.where(valid, share, 0.0)

    image_share = shares(image_lse, image_total, online[0:1])
    image_share = image_share - jnp.where(
        online[0:1], 2.0 * (1.0 - mix_weight) * image_total[3:4], 0.0
    )
    text_loss = shares(text_lse, text_total, in_text)
    line = lax.broadcasted_iota(jnp.int32, (8, lanes), 0)
    line_loss_out[...] = jnp.where(line == 0, image_share, 0.0)
    line = lax.broadcasted_iota(jnp.int32, (8, text_lanes), 0)
    plane_loss_out[...] = jnp.where(line == 0, text_loss, 0.0)
    line_copies_3 = [
        to_line(3, s, line_loss_out, line_loss.at[s]) for s in range(n_line - 1)
    ]
    plane_copies_3 = [
        to_plane(3, s, plane_loss_out, plane_loss.at[s]) for s in range(n_plane - 1)
    ]
    start(line_copies_3)
    start(plane_copies_3)

    def gathered(own, held, count):
        total = jnp.concatenate([own[:, :half], own[:, half:]], axis=0)
        for s in range(count):
            total = total + held[s].astype(f32)
        return jnp.concatenate([total[:rows], total[rows:]], axis=1)

    arrived(text_copies_2)
    result[0] = gathered(line_partial[my_line], text_in, n_line - 1)
    results = [
        pltpu.make_async_copy(result.at[0], grad_text_ref, result_sem.at[0]),
        pltpu.make_async_copy(result.at[1], grad_image_ref, result_sem.at[1]),
    ]
    results[0].start()
    arrived(image_copies_2)
    result[1] = gathered(plane_partial[my_plane, :rows, :], image_in, n_plane - 1)
    results[1].start()
    arrived(line_copies_3)
    arrived(plane_copies_3)
    image_loss = line_loss_out[...]
    for s in range(n_line - 1):
        image_loss = image_loss + line_loss[s]
    text_loss = plane_loss_out[...]
    for s in range(n_plane - 1):
        text_loss = text_loss + plane_loss[s]
    total = jnp.sum(image_loss, keepdims=True) + jnp.sum(text_loss, keepdims=True)
    loss_ref[...] = total / (2.0 * rows * grp * blk)

    for copy in (
        image_copies + text_copies + image_copies_1 + text_copies_1
        + image_copies_2 + text_copies_2 + line_copies_3 + plane_copies_3
    ):
        copy.wait_send()
    for copy in results:
        copy.wait()


def local(grp, blk, image, text, mimage, mtext):
    rows, width = image.shape
    fine = lines_of(grp, blk)
    n_plane, n_line = fine * blk, grp // fine
    lanes = n_plane * 2 * rows
    text_lanes = -(-n_line * rows // 128) * 128
    in_hbm = pl.BlockSpec(memory_space=pltpu.HBM)
    in_vmem = pl.BlockSpec(memory_space=pltpu.VMEM)
    grad_image, grad_text, loss = pl.pallas_call(
        functools.partial(kernel, grp, blk, fine, rows),
        out_shape=(
            jax.ShapeDtypeStruct((rows, width), f32),
            jax.ShapeDtypeStruct((rows, width), f32),
            jax.ShapeDtypeStruct((1, 1), f32),
        ),
        in_specs=[in_hbm] * 4,
        out_specs=(in_hbm, in_hbm, in_vmem),
        scratch_shapes=[
            pltpu.VMEM((n_plane, 2 * rows, width), bf16),
            pltpu.VMEM((n_line, 2 * rows, width), bf16),
            pltpu.VMEM((n_plane, 16, lanes), f32),
            pltpu.VMEM((n_line, 16, text_lanes), f32),
            pltpu.VMEM((n_plane, 2 * rows, width), f32),
            pltpu.VMEM((n_line, rows, width), f32),
            pltpu.VMEM((n_plane - 1, 2 * rows, width // 2), bf16),
            pltpu.VMEM((n_line - 1, 2 * rows, width // 2), bf16),
            pltpu.VMEM((n_plane - 1, 2 * rows, width // 2), bf16),
            pltpu.VMEM((n_line - 1, 2 * rows, width // 2), bf16),
            pltpu.VMEM((8, text_lanes), f32),
            pltpu.VMEM((8, lanes), f32),
            pltpu.VMEM((n_plane - 1, 8, text_lanes), f32),
            pltpu.VMEM((n_line - 1, 8, lanes), f32),
            pltpu.SemaphoreType.DMA((4, n_plane - 1)),
            pltpu.SemaphoreType.DMA((4, n_plane - 1)),
            pltpu.SemaphoreType.DMA((4, n_line - 1)),
            pltpu.SemaphoreType.DMA((4, n_line - 1)),
            pltpu.VMEM((4, rows, width), bf16),
            pltpu.SemaphoreType.DMA((4,)),
            pltpu.VMEM((2, rows, width), f32),
            pltpu.SemaphoreType.DMA((2,)),
        ],
        compiler_params=pltpu.CompilerParams(
            collective_id=0, has_side_effects=True, vmem_limit_bytes=60 * 1024 * 1024
        ),
    )(image, text, mimage, mtext)
    return grad_image, grad_text, loss.reshape(())


def solution(mesh):
    in_specs = (
        P(("blk", "grp"), None),
        P(("grp", "blk"), None),
        P(("blk", "grp"), None),
        P(("grp", "blk"), None),
    )
    out_specs = (P(("blk", "grp"), None), P(("grp", "blk"), None), P())
    run = functools.partial(local, mesh.shape["grp"], mesh.shape["blk"])
    return jax.shard_map(run, mesh=mesh, in_specs=in_specs, out_specs=out_specs, check_vma=False)
```

```python
import functools

import jax
import jax.numpy as jnp
from jax import lax
from jax.experimental import pallas as pl
from jax.experimental.pallas import tpu as pltpu
from jax.sharding import PartitionSpec as P

mix_weight = 0.4
very_low = -1e30
MESH = pl.DeviceIdType.MESH
f32 = jnp.float32
bf16 = jnp.bfloat16


def lines_of(grp, blk):
    fine = 1
    while fine * blk < grp // fine and grp % (2 * fine) == 0:
        fine *= 2
    return fine


def split_index(index, size):
    if size & (size - 1) == 0:
        return index >> (size.bit_length() - 1), index & (size - 1)
    return lax.div(index, size), lax.rem(index, size)


def kernel(
    grp, blk, fine, rows,
    image_ref, text_ref, mimage_ref, mtext_ref,
    grad_image_ref, grad_text_ref, loss_ref,
    images, texts, image_stats, text_stats, plane_partial, line_partial, image_out, text_out,
    image_in, text_in, plane_loss_out, line_loss_out, plane_loss, line_loss,
    plane_send, plane_recv, line_send, line_recv, fetched, fetch_sem, result, result_sem,
):
    n_plane, n_line = fine * blk, grp // fine
    width = image_ref.shape[1]
    half = width // 2
    lanes = images.shape[0] * images.shape[1]
    text_rows = n_line * rows
    text_lanes = text_stats.shape[2]
    my_grp, my_blk = lax.axis_index("grp"), lax.axis_index("blk")
    my_line, my_fine = lax.div(my_grp, fine), lax.rem(my_grp, fine)
    my_plane = my_fine * blk + my_blk

    def plane_peer(step):
        rank = lax.rem(my_plane + step, n_plane)
        return rank, (my_line * fine + lax.div(rank, blk), lax.rem(rank, blk))

    def line_peer(step):
        rank = lax.rem(my_line + step, n_line)
        return rank, (rank * fine + my_fine, my_blk)

    def send_all(peer_of, count, sems, phase, ends):
        send_sem, recv_sem = sems

        def step(s, carry):
            rank, peer = peer_of(s + 1)
            source, target = ends(s, rank)
            pltpu.make_async_remote_copy(
                src_ref=source, dst_ref=target,
                send_sem=send_sem.at[phase], recv_sem=recv_sem.at[phase],
                device_id=peer, device_id_type=MESH,
            ).start()
            return carry

        lax.fori_loop(0, count - 1, step, 0)

    def wait_all(sem, phase, span):
        pltpu.make_async_copy(span, span, sem.at[phase]).wait()

    plane_sems, line_sems = (plane_send, plane_recv), (line_send, line_recv)

    def to_plane(phase, ends):
        send_all(plane_peer, n_plane, plane_sems, phase, ends)

    def to_line(phase, ends):
        send_all(line_peer, n_line, line_sems, phase, ends)

    other_planes, other_lines = pl.ds(0, n_plane - 1), pl.ds(0, n_line - 1)
    plane_spans = [
        images.at[other_planes], image_stats.at[other_planes], image_in, plane_loss,
    ]
    line_spans = [texts.at[other_lines], text_stats.at[other_lines], text_in, line_loss]

    barrier = pltpu.get_barrier_semaphore()

    def greet(peer_of, count):
        def step(s, carry):
            pl.semaphore_signal(
                barrier, inc=1, device_id=peer_of(s + 1)[1], device_id_type=MESH
            )
            return carry

        lax.fori_loop(0, count - 1, step, 0)

    greet(line_peer, n_line)
    greet(plane_peer, n_plane)
    fetches = [
        pltpu.make_async_copy(ref, fetched.at[k], fetch_sem.at[k])
        for k, ref in enumerate((text_ref, mtext_ref, image_ref, mimage_ref))
    ]
    for copy in fetches:
        copy.start()

    def pair(first, second):
        return jnp.concatenate([first.astype(f32), second.astype(f32)], axis=0).astype(bf16)

    for copy in fetches:
        copy.wait()
    texts[my_line] = pair(fetched[0], fetched[1])
    images[my_plane] = pair(fetched[2], fetched[3])
    pl.semaphore_wait(barrier, n_plane + n_line - 2)

    to_line(0, lambda s, rank: (texts.at[my_line], texts.at[my_line]))
    to_plane(0, lambda s, rank: (images.at[my_plane], images.at[my_plane]))

    shape = (text_rows, lanes)
    text_slot, text_sub = split_index(lax.broadcasted_iota(jnp.int32, shape, 0), rows)
    lane_slot, lane_sub = split_index(lax.broadcasted_iota(jnp.int32, shape, 1), 2 * rows)
    online = lane_sub < rows
    lane_fine, lane_blk = split_index(lane_slot, blk)
    image_tile = lane_blk * grp + my_line * fine + lane_fine
    text_tile = (text_slot * fine + my_fine) * blk + my_blk
    same = (image_tile == text_tile) & (lane_sub == text_sub)
    diagonal = jnp.where(same, 1.0, 0.0)
    square = (text_rows, text_lanes)
    eye = lax.broadcasted_iota(jnp.int32, square, 0) == lax.broadcasted_iota(jnp.int32, square, 1)

    def to_lanes(column):
        return jnp.sum(jnp.where(eye, column, 0.0), axis=0, keepdims=True)

    def to_column(row):
        return jnp.sum(jnp.where(eye, row, 0.0), axis=1, keepdims=True)

    wait_all(line_recv, 0, line_spans[0])
    wait_all(plane_recv, 0, plane_spans[0])
    scores = lax.dot_general(
        texts[...].reshape(n_line * 2 * rows, width), images[...].reshape(lanes, width),
        (((1,), (1,)), ((), ())), preferred_element_type=f32,
    ) * (width ** -0.5)
    scores = scores.reshape(n_line, 2, rows, lanes)
    score_on = scores[:, 0].reshape(shape)
    score_mom = pltpu.roll(scores[:, 1].reshape(shape), lanes - rows, 1)
    masked_on = jnp.where(online, score_on, very_low)
    masked_mom = jnp.where(online, score_mom, very_low)

    def stats(on, mom, axis):
        top_on = jnp.max(on, axis=axis, keepdims=True)
        top_mom = jnp.max(mom, axis=axis, keepdims=True)
        spread = jnp.exp(mom - top_mom)
        return (
            top_on, jnp.sum(jnp.exp(on - top_on), axis=axis, keepdims=True),
            top_mom, jnp.sum(spread, axis=axis, keepdims=True),
            jnp.sum(spread * score_on, axis=axis, keepdims=True),
        )

    def message(top_on, sum_on, top_mom, sum_mom, cross, diag):
        line = lax.broadcasted_iota(jnp.int32, (8, top_on.shape[1]), 0)
        tops = jnp.where(line == 0, top_on, jnp.where((line == 1) | (line == 2), top_mom, 0.0))
        sums = jnp.where(line == 0, sum_on, jnp.where(line == 1, sum_mom, 1.0))
        sums = jnp.where(line == 2, cross, jnp.where(line == 3, diag, sums))
        return jnp.concatenate([tops, sums], axis=0)

    def joined(held, count):
        top = held[0, :8]
        for k in range(1, count):
            top = jnp.maximum(top, held[k, :8])
        total = held[0, 8:] * jnp.exp(held[0, :8] - top)
        for k in range(1, count):
            total = total + held[k, 8:] * jnp.exp(held[k, :8] - top)
        return top + jnp.log(total), total

    text_part = [to_lanes(column) for column in stats(masked_on, masked_mom, 1)]
    in_text = lax.broadcasted_iota(jnp.int32, (1, text_lanes), 1) < text_rows
    for k in (1, 3):
        text_part[k] = jnp.where(in_text, text_part[k], 1.0)
    text_stats[my_line] = message(*text_part, jnp.zeros((1, text_lanes), f32))
    to_line(1, lambda s, rank: (text_stats.at[my_line], text_stats.at[my_line]))
    diag = jnp.sum(diagonal * score_on, axis=0, keepdims=True)
    image_stats[my_plane] = message(*stats(score_on, score_mom, 0), diag)
    to_plane(1, lambda s, rank: (image_stats.at[my_plane], image_stats.at[my_plane]))
    wait_all(line_recv, 1, line_spans[1])
    text_lse, text_total = joined(text_stats, n_line)
    col_on, col_mom = to_column(text_lse[0:1]), to_column(text_lse[1:2])
    prob_col = jnp.exp(masked_on - col_on)
    target_col = mix_weight * jnp.exp(masked_mom - col_mom) + (1.0 - mix_weight) * diagonal
    wait_all(plane_recv, 1, plane_spans[1])
    image_lse, image_total = joined(image_stats, n_plane)
    prob_row = jnp.exp(score_on - image_lse[0:1])
    target_row = (
        mix_weight * jnp.exp(score_mom - image_lse[1:2]) + (1.0 - mix_weight) * diagonal
    )
    grad = 0.5 * ((prob_row - target_row) + (prob_col - target_col))
    grad = jnp.where(online, grad, 0.0)

    def folded(value):
        return jnp.concatenate([value[:, :half], value[:, half:]], axis=0).astype(bf16)

    line_partial[...] = jnp.dot(
        grad.astype(bf16), images[...].reshape(lanes, width), preferred_element_type=f32
    ).reshape(n_line, rows, width)

    def text_ends(s, rank):
        text_out[s] = folded(line_partial[rank])
        return text_out.at[s], text_in.at[s]

    to_line(2, text_ends)
    spaced = jnp.concatenate(
        [grad.reshape(n_line, 1, rows, lanes), jnp.zeros((n_line, 1, rows, lanes), f32)], axis=1
    ).reshape(n_line * 2 * rows, lanes)
    plane_partial[...] = lax.dot_general(
        spaced.astype(bf16), texts[...].reshape(n_line * 2 * rows, width),
        (((0,), (0,)), ((), ())), preferred_element_type=f32,
    ).reshape(n_plane, 2 * rows, width)

    def image_ends(s, rank):
        image_out[s] = folded(plane_partial[rank, :rows, :])
        return image_out.at[s], image_in.at[s]

    to_plane(2, image_ends)

    def shares(lse, total, valid):
        share = lse[0:1] - mix_weight * (total[2:3] / total[1:2])
        return jnp.where(valid, share, 0.0)

    image_share = shares(image_lse, image_total, online[0:1])
    image_share = image_share - jnp.where(
        online[0:1], 2.0 * (1.0 - mix_weight) * image_total[3:4], 0.0
    )
    text_loss = shares(text_lse, text_total, in_text)
    line = lax.broadcasted_iota(jnp.int32, (8, lanes), 0)
    line_loss_out[...] = jnp.where(line == 0, image_share, 0.0)
    line = lax.broadcasted_iota(jnp.int32, (8, text_lanes), 0)
    plane_loss_out[...] = jnp.where(line == 0, text_loss, 0.0)
    to_line(3, lambda s, rank: (line_loss_out, line_loss.at[s]))
    to_plane(3, lambda s, rank: (plane_loss_out, plane_loss.at[s]))

    def gathered(own, held, count):
        total = jnp.concatenate([own[:, :half], own[:, half:]], axis=0)
        for s in range(count):
            total = total + held[s].astype(f32)
        return jnp.concatenate([total[:rows], total[rows:]], axis=1)

    wait_all(line_recv, 2, line_spans[2])
    result[0] = gathered(line_partial[my_line], text_in, n_line - 1)
    results = [
        pltpu.make_async_copy(result.at[0], grad_text_ref, result_sem.at[0]),
        pltpu.make_async_copy(result.at[1], grad_image_ref, result_sem.at[1]),
    ]
    results[0].start()
    wait_all(plane_recv, 2, plane_spans[2])
    result[1] = gathered(plane_partial[my_plane, :rows, :], image_in, n_plane - 1)
    results[1].start()
    wait_all(line_recv, 3, line_spans[3])
    wait_all(plane_recv, 3, plane_spans[3])
    image_loss = line_loss_out[...]
    for s in range(n_line - 1):
        image_loss = image_loss + line_loss[s]
    text_loss = plane_loss_out[...]
    for s in range(n_plane - 1):
        text_loss = text_loss + plane_loss[s]
    total = jnp.sum(image_loss, keepdims=True) + jnp.sum(text_loss, keepdims=True)
    loss_ref[...] = total / (2.0 * rows * grp * blk)

    for phase in range(4):
        wait_all(line_send, phase, line_spans[phase])
        wait_all(plane_send, phase, plane_spans[phase])
    for copy in results:
        copy.wait()


def local(grp, blk, image, text, mimage, mtext):
    rows, width = image.shape
    fine = lines_of(grp, blk)
    n_plane, n_line = fine * blk, grp // fine
    lanes = n_plane * 2 * rows
    text_lanes = -(-n_line * rows // 128) * 128
    in_hbm = pl.BlockSpec(memory_space=pltpu.HBM)
    in_vmem = pl.BlockSpec(memory_space=pltpu.VMEM)
    grad_image, grad_text, loss = pl.pallas_call(
        functools.partial(kernel, grp, blk, fine, rows),
        out_shape=(
            jax.ShapeDtypeStruct((rows, width), f32),
            jax.ShapeDtypeStruct((rows, width), f32),
            jax.ShapeDtypeStruct((1, 1), f32),
        ),
        in_specs=[in_hbm] * 4,
        out_specs=(in_hbm, in_hbm, in_vmem),
        scratch_shapes=[
            pltpu.VMEM((n_plane, 2 * rows, width), bf16),
            pltpu.VMEM((n_line, 2 * rows, width), bf16),
            pltpu.VMEM((n_plane, 16, lanes), f32),
            pltpu.VMEM((n_line, 16, text_lanes), f32),
            pltpu.VMEM((n_plane, 2 * rows, width), f32),
            pltpu.VMEM((n_line, rows, width), f32),
            pltpu.VMEM((n_plane - 1, 2 * rows, width // 2), bf16),
            pltpu.VMEM((n_line - 1, 2 * rows, width // 2), bf16),
            pltpu.VMEM((n_plane - 1, 2 * rows, width // 2), bf16),
            pltpu.VMEM((n_line - 1, 2 * rows, width // 2), bf16),
            pltpu.VMEM((8, text_lanes), f32),
            pltpu.VMEM((8, lanes), f32),
            pltpu.VMEM((n_plane - 1, 8, text_lanes), f32),
            pltpu.VMEM((n_line - 1, 8, lanes), f32),
            pltpu.SemaphoreType.DMA((4,)),
            pltpu.SemaphoreType.DMA((4,)),
            pltpu.SemaphoreType.DMA((4,)),
            pltpu.SemaphoreType.DMA((4,)),
            pltpu.VMEM((4, rows, width), bf16),
            pltpu.SemaphoreType.DMA((4,)),
            pltpu.VMEM((2, rows, width), f32),
            pltpu.SemaphoreType.DMA((2,)),
        ],
        compiler_params=pltpu.CompilerParams(
            collective_id=0, has_side_effects=True, vmem_limit_bytes=60 * 1024 * 1024
        ),
    )(image, text, mimage, mtext)
    return grad_image, grad_text, loss.reshape(())


def solution(mesh):
    in_specs = (
        P(("blk", "grp"), None),
        P(("grp", "blk"), None),
        P(("blk", "grp"), None),
        P(("grp", "blk"), None),
    )
    out_specs = (P(("blk", "grp"), None), P(("grp", "blk"), None), P())
    run = functools.partial(local, mesh.shape["grp"], mesh.shape["blk"])
    return jax.shard_map(run, mesh=mesh, in_specs=in_specs, out_specs=out_specs, check_vma=False)
```

```python
import functools

import jax
import jax.numpy as jnp
from jax import lax
from jax.experimental import pallas as pl
from jax.experimental.pallas import tpu as pltpu
from jax.sharding import PartitionSpec as P

mix_weight = 0.4
very_low = -1e30
MESH = pl.DeviceIdType.MESH
f32 = jnp.float32
bf16 = jnp.bfloat16


def lines_of(grp, blk):
    fine = 1
    while fine * blk < grp // fine and grp % (2 * fine) == 0:
        fine *= 2
    return fine


def split_index(index, size):
    if size & (size - 1) == 0:
        return index >> (size.bit_length() - 1), index & (size - 1)
    return lax.div(index, size), lax.rem(index, size)


def kernel(
    grp, blk, fine, rows,
    image_ref, text_ref, mimage_ref, mtext_ref,
    grad_image_ref, grad_text_ref, loss_ref,
    images, texts, image_stats, text_stats, plane_partial, line_partial, image_out, text_out,
    image_in, text_in, plane_loss_out, line_loss_out, plane_loss, line_loss,
    plane_send, plane_recv, line_send, line_recv, fetched, fetch_sem, result, result_sem,
):
    n_plane, n_line = fine * blk, grp // fine
    width = image_ref.shape[1]
    half = width // 2
    lanes = images.shape[0] * images.shape[1]
    text_rows = n_line * rows
    text_lanes = text_stats.shape[2]
    my_grp, my_blk = lax.axis_index("grp"), lax.axis_index("blk")
    my_line, my_fine = lax.div(my_grp, fine), lax.rem(my_grp, fine)
    my_plane = my_fine * blk + my_blk

    def plane_peer(step):
        rank = lax.rem(my_plane + step, n_plane)
        return rank, (my_line * fine + lax.div(rank, blk), lax.rem(rank, blk))

    def line_peer(step):
        rank = lax.rem(my_line + step, n_line)
        return rank, (rank * fine + my_fine, my_blk)

    def send_all(peer_of, count, sems, phase, ends):
        send_sem, recv_sem = sems

        def step(s, carry):
            rank, peer = peer_of(s + 1)
            source, target = ends(s, rank)
            pltpu.make_async_remote_copy(
                src_ref=source, dst_ref=target,
                send_sem=send_sem.at[phase], recv_sem=recv_sem.at[phase],
                device_id=peer, device_id_type=MESH,
            ).start()
            return carry

        lax.fori_loop(0, count - 1, step, 0)

    def wait_all(sem, phase, span):
        pltpu.make_async_copy(span, span, sem.at[phase]).wait()

    plane_sems, line_sems = (plane_send, plane_recv), (line_send, line_recv)

    def to_plane(phase, ends):
        send_all(plane_peer, n_plane, plane_sems, phase, ends)

    def to_line(phase, ends):
        send_all(line_peer, n_line, line_sems, phase, ends)

    other_planes, other_lines = pl.ds(0, n_plane - 1), pl.ds(0, n_line - 1)
    plane_spans = [
        images.at[other_planes], image_stats.at[other_planes], image_in, plane_loss,
    ]
    line_spans = [texts.at[other_lines], text_stats.at[other_lines], text_in, line_loss]

    barrier = pltpu.get_barrier_semaphore()

    def greet(peer_of, count):
        def step(s, carry):
            pl.semaphore_signal(
                barrier, inc=1, device_id=peer_of(s + 1)[1], device_id_type=MESH
            )
            return carry

        lax.fori_loop(0, count - 1, step, 0)

    greet(line_peer, n_line)
    greet(plane_peer, n_plane)
    fetches = [
        pltpu.make_async_copy(ref, fetched.at[k], fetch_sem.at[k])
        for k, ref in enumerate((text_ref, mtext_ref, image_ref, mimage_ref))
    ]
    for copy in fetches:
        copy.start()

    def pair(first, second):
        return jnp.concatenate([first.astype(f32), second.astype(f32)], axis=0).astype(bf16)

    for copy in fetches:
        copy.wait()
    texts[my_line] = pair(fetched[0], fetched[1])
    images[my_plane] = pair(fetched[2], fetched[3])
    pl.semaphore_wait(barrier, n_plane + n_line - 2)

    to_line(0, lambda s, rank: (texts.at[my_line], texts.at[my_line]))
    to_plane(0, lambda s, rank: (images.at[my_plane], images.at[my_plane]))

    shape = (text_rows, lanes)
    text_slot, text_sub = split_index(lax.broadcasted_iota(jnp.int32, shape, 0), rows)
    lane_slot, lane_sub = split_index(lax.broadcasted_iota(jnp.int32, shape, 1), 2 * rows)
    online = lane_sub < rows
    lane_fine, lane_blk = split_index(lane_slot, blk)
    image_tile = lane_blk * grp + my_line * fine + lane_fine
    text_tile = (text_slot * fine + my_fine) * blk + my_blk
    same = (image_tile == text_tile) & (lane_sub == text_sub)
    diagonal = jnp.where(same, 1.0, 0.0)
    square = (text_rows, text_lanes)
    eye = lax.broadcasted_iota(jnp.int32, square, 0) == lax.broadcasted_iota(jnp.int32, square, 1)

    def to_lanes(column):
        return jnp.sum(jnp.where(eye, column, 0.0), axis=0, keepdims=True)

    def to_column(row):
        return jnp.sum(jnp.where(eye, row, 0.0), axis=1, keepdims=True)

    wait_all(line_recv, 0, line_spans[0])
    wait_all(plane_recv, 0, plane_spans[0])
    scores = lax.dot_general(
        texts[...].reshape(n_line * 2 * rows, width), images[...].reshape(lanes, width),
        (((1,), (1,)), ((), ())), preferred_element_type=f32,
    ) * (width ** -0.5)
    scores = scores.reshape(n_line, 2, rows, lanes)
    score_on = scores[:, 0].reshape(shape)
    score_mom = pltpu.roll(scores[:, 1].reshape(shape), lanes - rows, 1)
    masked_on = jnp.where(online, score_on, very_low)
    masked_mom = jnp.where(online, score_mom, very_low)

    def stats(on, mom, axis):
        top_on = jnp.max(on, axis=axis, keepdims=True)
        top_mom = jnp.max(mom, axis=axis, keepdims=True)
        spread = jnp.exp(mom - top_mom)
        return (
            top_on, jnp.sum(jnp.exp(on - top_on), axis=axis, keepdims=True),
            top_mom, jnp.sum(spread, axis=axis, keepdims=True),
            jnp.sum(spread * score_on, axis=axis, keepdims=True),
        )

    def message(top_on, sum_on, top_mom, sum_mom, cross, diag):
        line = lax.broadcasted_iota(jnp.int32, (8, top_on.shape[1]), 0)
        tops = jnp.where(line == 0, top_on, jnp.where((line == 1) | (line == 2), top_mom, 0.0))
        sums = jnp.where(line == 0, sum_on, jnp.where(line == 1, sum_mom, 1.0))
        sums = jnp.where(line == 2, cross, jnp.where(line == 3, diag, sums))
        return jnp.concatenate([tops, sums], axis=0)

    def joined(held, count):
        top = held[0, :8]
        for k in range(1, count):
            top = jnp.maximum(top, held[k, :8])
        total = held[0, 8:] * jnp.exp(held[0, :8] - top)
        for k in range(1, count):
            total = total + held[k, 8:] * jnp.exp(held[k, :8] - top)
        return top + jnp.log(total), total

    text_part = [to_lanes(column) for column in stats(masked_on, masked_mom, 1)]
    in_text = lax.broadcasted_iota(jnp.int32, (1, text_lanes), 1) < text_rows
    for k in (1, 3):
        text_part[k] = jnp.where(in_text, text_part[k], 1.0)
    text_stats[my_line] = message(*text_part, jnp.zeros((1, text_lanes), f32))
    to_line(1, lambda s, rank: (text_stats.at[my_line], text_stats.at[my_line]))
    diag = jnp.sum(diagonal * score_on, axis=0, keepdims=True)
    image_stats[my_plane] = message(*stats(score_on, score_mom, 0), diag)
    to_plane(1, lambda s, rank: (image_stats.at[my_plane], image_stats.at[my_plane]))
    wait_all(line_recv, 1, line_spans[1])
    text_lse, text_total = joined(text_stats, n_line)
    col_on, col_mom = to_column(text_lse[0:1]), to_column(text_lse[1:2])
    prob_col = jnp.exp(masked_on - col_on)
    target_col = mix_weight * jnp.exp(masked_mom - col_mom) + (1.0 - mix_weight) * diagonal
    wait_all(plane_recv, 1, plane_spans[1])
    image_lse, image_total = joined(image_stats, n_plane)
    prob_row = jnp.exp(score_on - image_lse[0:1])
    target_row = (
        mix_weight * jnp.exp(score_mom - image_lse[1:2]) + (1.0 - mix_weight) * diagonal
    )
    grad = 0.5 * ((prob_row - target_row) + (prob_col - target_col))
    grad = jnp.where(online, grad, 0.0)

    def folded(value):
        return jnp.concatenate([value[:, :half], value[:, half:]], axis=0).astype(bf16)

    line_partial[...] = jnp.dot(
        grad.astype(bf16), images[...].reshape(lanes, width), preferred_element_type=f32
    ).reshape(n_line, rows, width)

    def text_ends(s, rank):
        text_out[s] = folded(line_partial[rank])
        return text_out.at[s], text_in.at[s]

    to_line(2, text_ends)
    spaced = jnp.concatenate(
        [grad.reshape(n_line, 1, rows, lanes), jnp.zeros((n_line, 1, rows, lanes), f32)], axis=1
    ).reshape(n_line * 2 * rows, lanes)
    plane_partial[...] = lax.dot_general(
        spaced.astype(bf16), texts[...].reshape(n_line * 2 * rows, width),
        (((0,), (0,)), ((), ())), preferred_element_type=f32,
    ).reshape(n_plane, 2 * rows, width)

    def image_ends(s, rank):
        image_out[s] = folded(plane_partial[rank, :rows, :])
        return image_out.at[s], image_in.at[s]

    to_plane(2, image_ends)

    def shares(lse, total, valid):
        share = lse[0:1] - mix_weight * (total[2:3] / total[1:2])
        return jnp.where(valid, share, 0.0)

    image_share = shares(image_lse, image_total, online[0:1])
    image_share = image_share - jnp.where(
        online[0:1], 2.0 * (1.0 - mix_weight) * image_total[3:4], 0.0
    )
    text_loss = shares(text_lse, text_total, in_text)
    line = lax.broadcasted_iota(jnp.int32, (8, lanes), 0)
    line_loss_out[...] = jnp.where(line == 0, image_share, 0.0)
    line = lax.broadcasted_iota(jnp.int32, (8, text_lanes), 0)
    plane_loss_out[...] = jnp.where(line == 0, text_loss, 0.0)
    to_line(3, lambda s, rank: (line_loss_out, line_loss.at[s]))
    to_plane(3, lambda s, rank: (plane_loss_out, plane_loss.at[s]))

    def gathered(own, held, count):
        total = jnp.concatenate([own[:, :half], own[:, half:]], axis=0)
        for s in range(count):
            total = total + held[s].astype(f32)
        return jnp.concatenate([total[:rows], total[rows:]], axis=1)

    wait_all(line_recv, 2, line_spans[2])
    result[0] = gathered(line_partial[my_line], text_in, n_line - 1)
    results = [
        pltpu.make_async_copy(result.at[0], grad_text_ref, result_sem.at[0]),
        pltpu.make_async_copy(result.at[1], grad_image_ref, result_sem.at[1]),
    ]
    results[0].start()
    wait_all(plane_recv, 2, plane_spans[2])
    result[1] = gathered(plane_partial[my_plane, :rows, :], image_in, n_plane - 1)
    results[1].start()
    wait_all(line_recv, 3, line_spans[3])
    wait_all(plane_recv, 3, plane_spans[3])
    image_loss = line_loss_out[...]
    for s in range(n_line - 1):
        image_loss = image_loss + line_loss[s]
    text_loss = plane_loss_out[...]
    for s in range(n_plane - 1):
        text_loss = text_loss + plane_loss[s]
    total = jnp.sum(image_loss, keepdims=True) + jnp.sum(text_loss, keepdims=True)
    loss_ref[...] = total / (2.0 * rows * grp * blk)

    for phase in range(4):
        wait_all(line_send, phase, line_spans[phase])
        wait_all(plane_send, phase, plane_spans[phase])
    for copy in results:
        copy.wait()


def hand_over(image_in, text_in, loss_in, image_out, text_out, loss_out, sems):
    copies = [
        pltpu.make_async_copy(image_in, image_out, sems.at[0]),
        pltpu.make_async_copy(text_in, text_out, sems.at[1]),
        pltpu.make_async_copy(loss_in, loss_out, sems.at[2]),
    ]
    for copy in copies:
        copy.start()
    for copy in copies:
        copy.wait()


def local(grp, blk, image, text, mimage, mtext):
    rows, width = image.shape
    fine = lines_of(grp, blk)
    n_plane, n_line = fine * blk, grp // fine
    lanes = n_plane * 2 * rows
    text_lanes = -(-n_line * rows // 128) * 128
    in_hbm = pl.BlockSpec(memory_space=pltpu.HBM)
    in_vmem = pl.BlockSpec(memory_space=pltpu.VMEM)
    grad_image, grad_text, loss = pl.pallas_call(
        functools.partial(kernel, grp, blk, fine, rows),
        out_shape=(
            jax.ShapeDtypeStruct((rows, width), f32),
            jax.ShapeDtypeStruct((rows, width), f32),
            jax.ShapeDtypeStruct((1, 1), f32),
        ),
        in_specs=[in_hbm] * 4,
        out_specs=(in_hbm, in_hbm, in_vmem),
        scratch_shapes=[
            pltpu.VMEM((n_plane, 2 * rows, width), bf16),
            pltpu.VMEM((n_line, 2 * rows, width), bf16),
            pltpu.VMEM((n_plane, 16, lanes), f32),
            pltpu.VMEM((n_line, 16, text_lanes), f32),
            pltpu.VMEM((n_plane, 2 * rows, width), f32),
            pltpu.VMEM((n_line, rows, width), f32),
            pltpu.VMEM((n_plane - 1, 2 * rows, width // 2), bf16),
            pltpu.VMEM((n_line - 1, 2 * rows, width // 2), bf16),
            pltpu.VMEM((n_plane - 1, 2 * rows, width // 2), bf16),
            pltpu.VMEM((n_line - 1, 2 * rows, width // 2), bf16),
            pltpu.VMEM((8, text_lanes), f32),
            pltpu.VMEM((8, lanes), f32),
            pltpu.VMEM((n_plane - 1, 8, text_lanes), f32),
            pltpu.VMEM((n_line - 1, 8, lanes), f32),
            pltpu.SemaphoreType.DMA((4,)),
            pltpu.SemaphoreType.DMA((4,)),
            pltpu.SemaphoreType.DMA((4,)),
            pltpu.SemaphoreType.DMA((4,)),
            pltpu.VMEM((4, rows, width), bf16),
            pltpu.SemaphoreType.DMA((4,)),
            pltpu.VMEM((2, rows, width), f32),
            pltpu.SemaphoreType.DMA((2,)),
        ],
        compiler_params=pltpu.CompilerParams(
            collective_id=0, has_side_effects=True, vmem_limit_bytes=60 * 1024 * 1024
        ),
    )(image, text, mimage, mtext)
    found = (grad_image, grad_text, loss)
    grad_image, grad_text, loss = pl.pallas_call(
        hand_over,
        out_shape=tuple(jax.ShapeDtypeStruct(value.shape, value.dtype) for value in found),
        in_specs=[in_hbm] * 3,
        out_specs=(in_hbm,) * 3,
        scratch_shapes=[pltpu.SemaphoreType.DMA((3,))],
        compiler_params=pltpu.CompilerParams(vmem_limit_bytes=60 * 1024 * 1024),
    )(*found)
    return grad_image, grad_text, loss.reshape(())


def solution(mesh):
    in_specs = (
        P(("blk", "grp"), None),
        P(("grp", "blk"), None),
        P(("blk", "grp"), None),
        P(("grp", "blk"), None),
    )
    out_specs = (P(("blk", "grp"), None), P(("grp", "blk"), None), P())
    run = functools.partial(local, mesh.shape["grp"], mesh.shape["blk"])
    return jax.shard_map(run, mesh=mesh, in_specs=in_specs, out_specs=out_specs, check_vma=False)
```

```python
import functools

import jax
import jax.numpy as jnp
from jax import lax
from jax.experimental import pallas as pl
from jax.experimental.pallas import tpu as pltpu
from jax.sharding import PartitionSpec as P

mix_weight = 0.4
very_low = -1e30
MESH = pl.DeviceIdType.MESH
f32 = jnp.float32
bf16 = jnp.bfloat16


def lines_of(grp, blk):
    fine = 1
    while fine * blk < grp // fine and grp % (2 * fine) == 0:
        fine *= 2
    return fine


def split_index(index, size):
    if size & (size - 1) == 0:
        return index >> (size.bit_length() - 1), index & (size - 1)
    return lax.div(index, size), lax.rem(index, size)


def kernel(
    grp, blk, fine, rows,
    image_ref, text_ref, mimage_ref, mtext_ref,
    grad_image_ref, grad_text_ref, loss_ref,
    images, texts, image_stats, text_stats, plane_partial, line_partial, image_out, text_out,
    image_in, text_in, plane_loss_out, line_loss_out, plane_loss, line_loss,
    plane_send, plane_recv, line_send, line_recv, fetched, fetch_sem, result, loss_held, result_sem,
):
    n_plane, n_line = fine * blk, grp // fine
    width = image_ref.shape[1]
    half = width // 2
    lanes = images.shape[0] * images.shape[1]
    text_rows = n_line * rows
    text_lanes = text_stats.shape[2]
    my_grp, my_blk = lax.axis_index("grp"), lax.axis_index("blk")
    my_line, my_fine = lax.div(my_grp, fine), lax.rem(my_grp, fine)
    my_plane = my_fine * blk + my_blk

    def plane_peer(step):
        rank = lax.rem(my_plane + step, n_plane)
        return rank, (my_line * fine + lax.div(rank, blk), lax.rem(rank, blk))

    def line_peer(step):
        rank = lax.rem(my_line + step, n_line)
        return rank, (rank * fine + my_fine, my_blk)

    def send_all(peer_of, count, sems, phase, ends):
        send_sem, recv_sem = sems

        def step(s, carry):
            rank, peer = peer_of(s + 1)
            source, target = ends(s, rank)
            pltpu.make_async_remote_copy(
                src_ref=source, dst_ref=target,
                send_sem=send_sem.at[phase], recv_sem=recv_sem.at[phase],
                device_id=peer, device_id_type=MESH,
            ).start()
            return carry

        lax.fori_loop(0, count - 1, step, 0)

    def wait_all(sem, phase, span):
        pltpu.make_async_copy(span, span, sem.at[phase]).wait()

    plane_sems, line_sems = (plane_send, plane_recv), (line_send, line_recv)

    def to_plane(phase, ends):
        send_all(plane_peer, n_plane, plane_sems, phase, ends)

    def to_line(phase, ends):
        send_all(line_peer, n_line, line_sems, phase, ends)

    other_planes, other_lines = pl.ds(0, n_plane - 1), pl.ds(0, n_line - 1)
    plane_spans = [
        images.at[other_planes], image_stats.at[other_planes], image_in, plane_loss,
    ]
    line_spans = [texts.at[other_lines], text_stats.at[other_lines], text_in, line_loss]

    barrier = pltpu.get_barrier_semaphore()

    def greet(peer_of, count):
        def step(s, carry):
            pl.semaphore_signal(
                barrier, inc=1, device_id=peer_of(s + 1)[1], device_id_type=MESH
            )
            return carry

        lax.fori_loop(0, count - 1, step, 0)

    greet(line_peer, n_line)
    greet(plane_peer, n_plane)
    fetches = [
        pltpu.make_async_copy(ref, fetched.at[k], fetch_sem.at[k])
        for k, ref in enumerate((text_ref, mtext_ref, image_ref, mimage_ref))
    ]
    for copy in fetches:
        copy.start()

    def pair(first, second):
        return jnp.concatenate([first.astype(f32), second.astype(f32)], axis=0).astype(bf16)

    for copy in fetches:
        copy.wait()
    texts[my_line] = pair(fetched[0], fetched[1])
    images[my_plane] = pair(fetched[2], fetched[3])
    pl.semaphore_wait(barrier, n_plane + n_line - 2)

    to_line(0, lambda s, rank: (texts.at[my_line], texts.at[my_line]))
    to_plane(0, lambda s, rank: (images.at[my_plane], images.at[my_plane]))

    shape = (text_rows, lanes)
    text_slot, text_sub = split_index(lax.broadcasted_iota(jnp.int32, shape, 0), rows)
    lane_slot, lane_sub = split_index(lax.broadcasted_iota(jnp.int32, shape, 1), 2 * rows)
    online = lane_sub < rows
    lane_fine, lane_blk = split_index(lane_slot, blk)
    image_tile = lane_blk * grp + my_line * fine + lane_fine
    text_tile = (text_slot * fine + my_fine) * blk + my_blk
    same = (image_tile == text_tile) & (lane_sub == text_sub)
    diagonal = jnp.where(same, 1.0, 0.0)
    square = (text_rows, text_lanes)
    eye = lax.broadcasted_iota(jnp.int32, square, 0) == lax.broadcasted_iota(jnp.int32, square, 1)

    def to_lanes(column):
        return jnp.sum(jnp.where(eye, column, 0.0), axis=0, keepdims=True)

    def to_column(row):
        return jnp.sum(jnp.where(eye, row, 0.0), axis=1, keepdims=True)

    wait_all(line_recv, 0, line_spans[0])
    wait_all(plane_recv, 0, plane_spans[0])
    scores = lax.dot_general(
        texts[...].reshape(n_line * 2 * rows, width), images[...].reshape(lanes, width),
        (((1,), (1,)), ((), ())), preferred_element_type=f32,
    ) * (width ** -0.5)
    scores = scores.reshape(n_line, 2, rows, lanes)
    score_on = scores[:, 0].reshape(shape)
    score_mom = pltpu.roll(scores[:, 1].reshape(shape), lanes - rows, 1)
    masked_on = jnp.where(online, score_on, very_low)
    masked_mom = jnp.where(online, score_mom, very_low)

    def stats(on, mom, axis):
        top_on = jnp.max(on, axis=axis, keepdims=True)
        top_mom = jnp.max(mom, axis=axis, keepdims=True)
        spread = jnp.exp(mom - top_mom)
        return (
            top_on, jnp.sum(jnp.exp(on - top_on), axis=axis, keepdims=True),
            top_mom, jnp.sum(spread, axis=axis, keepdims=True),
            jnp.sum(spread * score_on, axis=axis, keepdims=True),
        )

    def message(top_on, sum_on, top_mom, sum_mom, cross, diag):
        line = lax.broadcasted_iota(jnp.int32, (8, top_on.shape[1]), 0)
        tops = jnp.where(line == 0, top_on, jnp.where((line == 1) | (line == 2), top_mom, 0.0))
        sums = jnp.where(line == 0, sum_on, jnp.where(line == 1, sum_mom, 1.0))
        sums = jnp.where(line == 2, cross, jnp.where(line == 3, diag, sums))
        return jnp.concatenate([tops, sums], axis=0)

    def joined(held, count):
        top = held[0, :8]
        for k in range(1, count):
            top = jnp.maximum(top, held[k, :8])
        total = held[0, 8:] * jnp.exp(held[0, :8] - top)
        for k in range(1, count):
            total = total + held[k, 8:] * jnp.exp(held[k, :8] - top)
        return top + jnp.log(total), total

    text_part = [to_lanes(column) for column in stats(masked_on, masked_mom, 1)]
    in_text = lax.broadcasted_iota(jnp.int32, (1, text_lanes), 1) < text_rows
    for k in (1, 3):
        text_part[k] = jnp.where(in_text, text_part[k], 1.0)
    text_stats[my_line] = message(*text_part, jnp.zeros((1, text_lanes), f32))
    to_line(1, lambda s, rank: (text_stats.at[my_line], text_stats.at[my_line]))
    diag = jnp.sum(diagonal * score_on, axis=0, keepdims=True)
    image_stats[my_plane] = message(*stats(score_on, score_mom, 0), diag)
    to_plane(1, lambda s, rank: (image_stats.at[my_plane], image_stats.at[my_plane]))
    wait_all(line_recv, 1, line_spans[1])
    text_lse, text_total = joined(text_stats, n_line)
    col_on, col_mom = to_column(text_lse[0:1]), to_column(text_lse[1:2])
    prob_col = jnp.exp(masked_on - col_on)
    target_col = mix_weight * jnp.exp(masked_mom - col_mom) + (1.0 - mix_weight) * diagonal
    wait_all(plane_recv, 1, plane_spans[1])
    image_lse, image_total = joined(image_stats, n_plane)
    prob_row = jnp.exp(score_on - image_lse[0:1])
    target_row = (
        mix_weight * jnp.exp(score_mom - image_lse[1:2]) + (1.0 - mix_weight) * diagonal
    )
    grad = 0.5 * ((prob_row - target_row) + (prob_col - target_col))
    grad = jnp.where(online, grad, 0.0)

    def folded(value):
        return jnp.concatenate([value[:, :half], value[:, half:]], axis=0).astype(bf16)

    line_partial[...] = jnp.dot(
        grad.astype(bf16), images[...].reshape(lanes, width), preferred_element_type=f32
    ).reshape(n_line, rows, width)

    def text_ends(s, rank):
        text_out[s] = folded(line_partial[rank])
        return text_out.at[s], text_in.at[s]

    to_line(2, text_ends)
    spaced = jnp.concatenate(
        [grad.reshape(n_line, 1, rows, lanes), jnp.zeros((n_line, 1, rows, lanes), f32)], axis=1
    ).reshape(n_line * 2 * rows, lanes)
    plane_partial[...] = lax.dot_general(
        spaced.astype(bf16), texts[...].reshape(n_line * 2 * rows, width),
        (((0,), (0,)), ((), ())), preferred_element_type=f32,
    ).reshape(n_plane, 2 * rows, width)

    def image_ends(s, rank):
        image_out[s] = folded(plane_partial[rank, :rows, :])
        return image_out.at[s], image_in.at[s]

    to_plane(2, image_ends)

    def shares(lse, total, valid):
        share = lse[0:1] - mix_weight * (total[2:3] / total[1:2])
        return jnp.where(valid, share, 0.0)

    image_share = shares(image_lse, image_total, online[0:1])
    image_share = image_share - jnp.where(
        online[0:1], 2.0 * (1.0 - mix_weight) * image_total[3:4], 0.0
    )
    text_loss = shares(text_lse, text_total, in_text)
    line = lax.broadcasted_iota(jnp.int32, (8, lanes), 0)
    line_loss_out[...] = jnp.where(line == 0, image_share, 0.0)
    line = lax.broadcasted_iota(jnp.int32, (8, text_lanes), 0)
    plane_loss_out[...] = jnp.where(line == 0, text_loss, 0.0)
    to_line(3, lambda s, rank: (line_loss_out, line_loss.at[s]))
    to_plane(3, lambda s, rank: (plane_loss_out, plane_loss.at[s]))

    def gathered(own, held, count):
        total = jnp.concatenate([own[:, :half], own[:, half:]], axis=0)
        for s in range(count):
            total = total + held[s].astype(f32)
        return jnp.concatenate([total[:rows], total[rows:]], axis=1)

    wait_all(line_recv, 2, line_spans[2])
    result[0] = gathered(line_partial[my_line], text_in, n_line - 1)
    results = [
        pltpu.make_async_copy(result.at[0], grad_text_ref, result_sem.at[0]),
        pltpu.make_async_copy(result.at[1], grad_image_ref, result_sem.at[1]),
        pltpu.make_async_copy(loss_held, loss_ref, result_sem.at[2]),
    ]
    results[0].start()
    wait_all(plane_recv, 2, plane_spans[2])
    result[1] = gathered(plane_partial[my_plane, :rows, :], image_in, n_plane - 1)
    results[1].start()
    wait_all(line_recv, 3, line_spans[3])
    wait_all(plane_recv, 3, plane_spans[3])
    image_loss = line_loss_out[...]
    for s in range(n_line - 1):
        image_loss = image_loss + line_loss[s]
    text_loss = plane_loss_out[...]
    for s in range(n_plane - 1):
        text_loss = text_loss + plane_loss[s]
    total = jnp.sum(image_loss, keepdims=True) + jnp.sum(text_loss, keepdims=True)
    loss_held[...] = total / (2.0 * rows * grp * blk)
    results[2].start()

    for phase in range(4):
        wait_all(line_send, phase, line_spans[phase])
        wait_all(plane_send, phase, plane_spans[phase])
    for copy in results:
        copy.wait()


def hand_over(*refs):
    found, results, held = refs[:3], refs[3:6], refs[6:9]
    in_sems, out_sems = refs[9:]
    fetches = [
        pltpu.make_async_copy(found[k], held[k], in_sems.at[k]) for k in range(3)
    ]
    writes = [
        pltpu.make_async_copy(held[k], results[k], out_sems.at[k]) for k in range(3)
    ]
    for copy in fetches:
        copy.start()
    for fetch, write in zip(fetches, writes):
        fetch.wait()
        write.start()
    for copy in writes:
        copy.wait()


def local(grp, blk, image, text, mimage, mtext):
    rows, width = image.shape
    fine = lines_of(grp, blk)
    n_plane, n_line = fine * blk, grp // fine
    lanes = n_plane * 2 * rows
    text_lanes = -(-n_line * rows // 128) * 128
    in_hbm = pl.BlockSpec(memory_space=pltpu.HBM)
    grad_image, grad_text, loss = pl.pallas_call(
        functools.partial(kernel, grp, blk, fine, rows),
        out_shape=(
            jax.ShapeDtypeStruct((rows, width), f32),
            jax.ShapeDtypeStruct((rows, width), f32),
            jax.ShapeDtypeStruct((1, 1), f32),
        ),
        in_specs=[in_hbm] * 4,
        out_specs=(in_hbm,) * 3,
        scratch_shapes=[
            pltpu.VMEM((n_plane, 2 * rows, width), bf16),
            pltpu.VMEM((n_line, 2 * rows, width), bf16),
            pltpu.VMEM((n_plane, 16, lanes), f32),
            pltpu.VMEM((n_line, 16, text_lanes), f32),
            pltpu.VMEM((n_plane, 2 * rows, width), f32),
            pltpu.VMEM((n_line, rows, width), f32),
            pltpu.VMEM((n_plane - 1, 2 * rows, width // 2), bf16),
            pltpu.VMEM((n_line - 1, 2 * rows, width // 2), bf16),
            pltpu.VMEM((n_plane - 1, 2 * rows, width // 2), bf16),
            pltpu.VMEM((n_line - 1, 2 * rows, width // 2), bf16),
            pltpu.VMEM((8, text_lanes), f32),
            pltpu.VMEM((8, lanes), f32),
            pltpu.VMEM((n_plane - 1, 8, text_lanes), f32),
            pltpu.VMEM((n_line - 1, 8, lanes), f32),
            pltpu.SemaphoreType.DMA((4,)),
            pltpu.SemaphoreType.DMA((4,)),
            pltpu.SemaphoreType.DMA((4,)),
            pltpu.SemaphoreType.DMA((4,)),
            pltpu.VMEM((4, rows, width), bf16),
            pltpu.SemaphoreType.DMA((4,)),
            pltpu.VMEM((2, rows, width), f32),
            pltpu.VMEM((1, 1), f32),
            pltpu.SemaphoreType.DMA((3,)),
        ],
        compiler_params=pltpu.CompilerParams(
            collective_id=0, has_side_effects=True, vmem_limit_bytes=60 * 1024 * 1024
        ),
    )(image, text, mimage, mtext)
    found = (grad_image, grad_text, loss)
    grad_image, grad_text, loss = pl.pallas_call(
        hand_over,
        out_shape=tuple(jax.ShapeDtypeStruct(value.shape, value.dtype) for value in found),
        in_specs=[in_hbm] * 3,
        out_specs=(in_hbm,) * 3,
        scratch_shapes=[
            *(pltpu.VMEM(value.shape, value.dtype) for value in found),
            pltpu.SemaphoreType.DMA((3,)),
            pltpu.SemaphoreType.DMA((3,)),
        ],
        compiler_params=pltpu.CompilerParams(vmem_limit_bytes=60 * 1024 * 1024),
    )(*found)
    return grad_image, grad_text, loss.reshape(())


def solution(mesh):
    in_specs = (
        P(("blk", "grp"), None),
        P(("grp", "blk"), None),
        P(("blk", "grp"), None),
        P(("grp", "blk"), None),
    )
    out_specs = (P(("blk", "grp"), None), P(("grp", "blk"), None), P())
    run = functools.partial(local, mesh.shape["grp"], mesh.shape["blk"])
    return jax.shard_map(run, mesh=mesh, in_specs=in_specs, out_specs=out_specs, check_vma=False)
```

```python
import functools

import jax
import jax.numpy as jnp
from jax import lax
from jax.experimental import pallas as pl
from jax.experimental.pallas import tpu as pltpu
from jax.sharding import PartitionSpec as P

mix_weight = 0.4
very_low = -1e30
MESH = pl.DeviceIdType.MESH
f32 = jnp.float32
bf16 = jnp.bfloat16


def lines_of(grp, blk):
    fine = 1
    while fine * blk < grp // fine and grp % (2 * fine) == 0:
        fine *= 2
    return fine


def split_index(index, size):
    if size & (size - 1) == 0:
        return index >> (size.bit_length() - 1), index & (size - 1)
    return lax.div(index, size), lax.rem(index, size)


def kernel(
    grp, blk, fine, rows,
    image_ref, text_ref, mimage_ref, mtext_ref,
    grad_image_ref, grad_text_ref, loss_ref,
    images, texts, image_stats, text_stats, plane_partial, line_partial, image_out, text_out,
    image_in, text_in, plane_loss_out, line_loss_out, plane_loss, line_loss,
    plane_send, plane_recv, line_send, line_recv, fetched, fetch_sem,
):
    n_plane, n_line = fine * blk, grp // fine
    width = image_ref.shape[1]
    half = width // 2
    lanes = images.shape[0] * images.shape[1]
    text_rows = n_line * rows
    text_lanes = text_stats.shape[2]
    my_grp, my_blk = lax.axis_index("grp"), lax.axis_index("blk")
    my_line, my_fine = lax.div(my_grp, fine), lax.rem(my_grp, fine)
    my_plane = my_fine * blk + my_blk

    def plane_peer(step):
        rank = lax.rem(my_plane + step, n_plane)
        return rank, (my_line * fine + lax.div(rank, blk), lax.rem(rank, blk))

    def line_peer(step):
        rank = lax.rem(my_line + step, n_line)
        return rank, (rank * fine + my_fine, my_blk)

    def send_all(peer_of, count, sems, phase, ends):
        send_sem, recv_sem = sems

        def step(s, carry):
            rank, peer = peer_of(s + 1)
            source, target = ends(s, rank)
            pltpu.make_async_remote_copy(
                src_ref=source, dst_ref=target,
                send_sem=send_sem.at[phase], recv_sem=recv_sem.at[phase],
                device_id=peer, device_id_type=MESH,
            ).start()
            return carry

        lax.fori_loop(0, count - 1, step, 0)

    def wait_all(sem, phase, span):
        pltpu.make_async_copy(span, span, sem.at[phase]).wait()

    plane_sems, line_sems = (plane_send, plane_recv), (line_send, line_recv)

    def to_plane(phase, ends):
        send_all(plane_peer, n_plane, plane_sems, phase, ends)

    def to_line(phase, ends):
        send_all(line_peer, n_line, line_sems, phase, ends)

    other_planes, other_lines = pl.ds(0, n_plane - 1), pl.ds(0, n_line - 1)
    plane_spans = [
        images.at[other_planes], image_stats.at[other_planes], image_in, plane_loss,
    ]
    line_spans = [texts.at[other_lines], text_stats.at[other_lines], text_in, line_loss]

    barrier = pltpu.get_barrier_semaphore()

    def greet(peer_of, count):
        def step(s, carry):
            pl.semaphore_signal(
                barrier, inc=1, device_id=peer_of(s + 1)[1], device_id_type=MESH
            )
            return carry

        lax.fori_loop(0, count - 1, step, 0)

    greet(line_peer, n_line)
    greet(plane_peer, n_plane)
    fetches = [
        pltpu.make_async_copy(ref, fetched.at[k], fetch_sem.at[k])
        for k, ref in enumerate((text_ref, mtext_ref, image_ref, mimage_ref))
    ]
    for copy in fetches:
        copy.start()

    def pair(first, second):
        return jnp.concatenate([first.astype(f32), second.astype(f32)], axis=0).astype(bf16)

    for copy in fetches:
        copy.wait()
    texts[my_line] = pair(fetched[0], fetched[1])
    images[my_plane] = pair(fetched[2], fetched[3])
    pl.semaphore_wait(barrier, n_plane + n_line - 2)

    to_line(0, lambda s, rank: (texts.at[my_line], texts.at[my_line]))
    to_plane(0, lambda s, rank: (images.at[my_plane], images.at[my_plane]))

    shape = (text_rows, lanes)
    text_slot, text_sub = split_index(lax.broadcasted_iota(jnp.int32, shape, 0), rows)
    lane_slot, lane_sub = split_index(lax.broadcasted_iota(jnp.int32, shape, 1), 2 * rows)
    online = lane_sub < rows
    lane_fine, lane_blk = split_index(lane_slot, blk)
    image_tile = lane_blk * grp + my_line * fine + lane_fine
    text_tile = (text_slot * fine + my_fine) * blk + my_blk
    same = (image_tile == text_tile) & (lane_sub == text_sub)
    diagonal = jnp.where(same, 1.0, 0.0)
    square = (text_rows, text_lanes)
    eye = lax.broadcasted_iota(jnp.int32, square, 0) == lax.broadcasted_iota(jnp.int32, square, 1)

    def to_lanes(column):
        return jnp.sum(jnp.where(eye, column, 0.0), axis=0, keepdims=True)

    def to_column(row):
        return jnp.sum(jnp.where(eye, row, 0.0), axis=1, keepdims=True)

    wait_all(line_recv, 0, line_spans[0])
    wait_all(plane_recv, 0, plane_spans[0])
    scores = lax.dot_general(
        texts[...].reshape(n_line * 2 * rows, width), images[...].reshape(lanes, width),
        (((1,), (1,)), ((), ())), preferred_element_type=f32,
    ) * (width ** -0.5)
    scores = scores.reshape(n_line, 2, rows, lanes)
    score_on = scores[:, 0].reshape(shape)
    score_mom = pltpu.roll(scores[:, 1].reshape(shape), lanes - rows, 1)
    masked_on = jnp.where(online, score_on, very_low)
    masked_mom = jnp.where(online, score_mom, very_low)

    def stats(on, mom, axis):
        top_on = jnp.max(on, axis=axis, keepdims=True)
        top_mom = jnp.max(mom, axis=axis, keepdims=True)
        spread = jnp.exp(mom - top_mom)
        return (
            top_on, jnp.sum(jnp.exp(on - top_on), axis=axis, keepdims=True),
            top_mom, jnp.sum(spread, axis=axis, keepdims=True),
            jnp.sum(spread * score_on, axis=axis, keepdims=True),
        )

    def message(top_on, sum_on, top_mom, sum_mom, cross, diag):
        line = lax.broadcasted_iota(jnp.int32, (8, top_on.shape[1]), 0)
        tops = jnp.where(line == 0, top_on, jnp.where((line == 1) | (line == 2), top_mom, 0.0))
        sums = jnp.where(line == 0, sum_on, jnp.where(line == 1, sum_mom, 1.0))
        sums = jnp.where(line == 2, cross, jnp.where(line == 3, diag, sums))
        return jnp.concatenate([tops, sums], axis=0)

    def joined(held, count):
        top = held[0, :8]
        for k in range(1, count):
            top = jnp.maximum(top, held[k, :8])
        total = held[0, 8:] * jnp.exp(held[0, :8] - top)
        for k in range(1, count):
            total = total + held[k, 8:] * jnp.exp(held[k, :8] - top)
        return top + jnp.log(total), total

    text_part = [to_lanes(column) for column in stats(masked_on, masked_mom, 1)]
    in_text = lax.broadcasted_iota(jnp.int32, (1, text_lanes), 1) < text_rows
    for k in (1, 3):
        text_part[k] = jnp.where(in_text, text_part[k], 1.0)
    text_stats[my_line] = message(*text_part, jnp.zeros((1, text_lanes), f32))
    to_line(1, lambda s, rank: (text_stats.at[my_line], text_stats.at[my_line]))
    diag = jnp.sum(diagonal * score_on, axis=0, keepdims=True)
    image_stats[my_plane] = message(*stats(score_on, score_mom, 0), diag)
    to_plane(1, lambda s, rank: (image_stats.at[my_plane], image_stats.at[my_plane]))
    wait_all(line_recv, 1, line_spans[1])
    text_lse, text_total = joined(text_stats, n_line)
    col_on, col_mom = to_column(text_lse[0:1]), to_column(text_lse[1:2])
    prob_col = jnp.exp(masked_on - col_on)
    target_col = mix_weight * jnp.exp(masked_mom - col_mom) + (1.0 - mix_weight) * diagonal
    wait_all(plane_recv, 1, plane_spans[1])
    image_lse, image_total = joined(image_stats, n_plane)
    prob_row = jnp.exp(score_on - image_lse[0:1])
    target_row = (
        mix_weight * jnp.exp(score_mom - image_lse[1:2]) + (1.0 - mix_weight) * diagonal
    )
    grad = 0.5 * ((prob_row - target_row) + (prob_col - target_col))
    grad = jnp.where(online, grad, 0.0)

    def folded(value):
        return jnp.concatenate([value[:, :half], value[:, half:]], axis=0).astype(bf16)

    line_partial[...] = jnp.dot(
        grad.astype(bf16), images[...].reshape(lanes, width), preferred_element_type=f32
    ).reshape(n_line, rows, width)

    def text_ends(s, rank):
        text_out[s] = folded(line_partial[rank])
        return text_out.at[s], text_in.at[s]

    to_line(2, text_ends)
    spaced = jnp.concatenate(
        [grad.reshape(n_line, 1, rows, lanes), jnp.zeros((n_line, 1, rows, lanes), f32)], axis=1
    ).reshape(n_line * 2 * rows, lanes)
    plane_partial[...] = lax.dot_general(
        spaced.astype(bf16), texts[...].reshape(n_line * 2 * rows, width),
        (((0,), (0,)), ((), ())), preferred_element_type=f32,
    ).reshape(n_plane, 2 * rows, width)

    def image_ends(s, rank):
        image_out[s] = folded(plane_partial[rank, :rows, :])
        return image_out.at[s], image_in.at[s]

    to_plane(2, image_ends)

    def shares(lse, total, valid):
        share = lse[0:1] - mix_weight * (total[2:3] / total[1:2])
        return jnp.where(valid, share, 0.0)

    image_share = shares(image_lse, image_total, online[0:1])
    image_share = image_share - jnp.where(
        online[0:1], 2.0 * (1.0 - mix_weight) * image_total[3:4], 0.0
    )
    text_loss = shares(text_lse, text_total, in_text)
    line = lax.broadcasted_iota(jnp.int32, (8, lanes), 0)
    line_loss_out[...] = jnp.where(line == 0, image_share, 0.0)
    line = lax.broadcasted_iota(jnp.int32, (8, text_lanes), 0)
    plane_loss_out[...] = jnp.where(line == 0, text_loss, 0.0)
    to_line(3, lambda s, rank: (line_loss_out, line_loss.at[s]))
    to_plane(3, lambda s, rank: (plane_loss_out, plane_loss.at[s]))

    def gathered(own, held, count):
        total = jnp.concatenate([own[:, :half], own[:, half:]], axis=0)
        for s in range(count):
            total = total + held[s].astype(f32)
        return jnp.concatenate([total[:rows], total[rows:]], axis=1)

    wait_all(line_recv, 2, line_spans[2])
    grad_text_ref[...] = gathered(line_partial[my_line], text_in, n_line - 1)
    wait_all(plane_recv, 2, plane_spans[2])
    grad_image_ref[...] = gathered(plane_partial[my_plane, :rows, :], image_in, n_plane - 1)
    wait_all(line_recv, 3, line_spans[3])
    wait_all(plane_recv, 3, plane_spans[3])
    image_loss = line_loss_out[...]
    for s in range(n_line - 1):
        image_loss = image_loss + line_loss[s]
    text_loss = plane_loss_out[...]
    for s in range(n_plane - 1):
        text_loss = text_loss + plane_loss[s]
    loss_ref[...] = sum(
        value[:, first:first + 128]
        for value in (image_loss, text_loss)
        for first in range(0, value.shape[1], 128)
    )

    for phase in range(4):
        wait_all(line_send, phase, line_spans[phase])
        wait_all(plane_send, phase, plane_spans[phase])


def hand_over(pairs, image_in, text_in, loss_in, image_out, text_out, loss_out, loss, sems):
    copies = [
        pltpu.make_async_copy(image_in, image_out, sems.at[0]),
        pltpu.make_async_copy(text_in, text_out, sems.at[1]),
        pltpu.make_async_copy(loss, loss_out, sems.at[2]),
    ]
    copies[0].start()
    copies[1].start()
    loss[...] = jnp.sum(loss_in[...], keepdims=True) / (2.0 * pairs)
    copies[2].start()
    for copy in copies:
        copy.wait()


def local(grp, blk, image, text, mimage, mtext):
    rows, width = image.shape
    fine = lines_of(grp, blk)
    n_plane, n_line = fine * blk, grp // fine
    lanes = n_plane * 2 * rows
    text_lanes = -(-n_line * rows // 128) * 128
    operands = [
        pltpu.with_memory_space_constraint(value, pltpu.HBM)
        for value in (image, text, mimage, mtext)
    ]
    in_hbm = pl.BlockSpec(memory_space=pltpu.HBM)
    in_vmem = pl.BlockSpec(memory_space=pltpu.VMEM)
    grad_image, grad_text, loss = pl.pallas_call(
        functools.partial(kernel, grp, blk, fine, rows),
        out_shape=(
            jax.ShapeDtypeStruct((rows, width), f32),
            jax.ShapeDtypeStruct((rows, width), f32),
            jax.ShapeDtypeStruct((8, 128), f32),
        ),
        in_specs=[in_hbm] * 4,
        out_specs=(in_vmem,) * 3,
        scratch_shapes=[
            pltpu.VMEM((n_plane, 2 * rows, width), bf16),
            pltpu.VMEM((n_line, 2 * rows, width), bf16),
            pltpu.VMEM((n_plane, 16, lanes), f32),
            pltpu.VMEM((n_line, 16, text_lanes), f32),
            pltpu.VMEM((n_plane, 2 * rows, width), f32),
            pltpu.VMEM((n_line, rows, width), f32),
            pltpu.VMEM((n_plane - 1, 2 * rows, width // 2), bf16),
            pltpu.VMEM((n_line - 1, 2 * rows, width // 2), bf16),
            pltpu.VMEM((n_plane - 1, 2 * rows, width // 2), bf16),
            pltpu.VMEM((n_line - 1, 2 * rows, width // 2), bf16),
            pltpu.VMEM((8, text_lanes), f32),
            pltpu.VMEM((8, lanes), f32),
            pltpu.VMEM((n_plane - 1, 8, text_lanes), f32),
            pltpu.VMEM((n_line - 1, 8, lanes), f32),
            pltpu.SemaphoreType.DMA((4,)),
            pltpu.SemaphoreType.DMA((4,)),
            pltpu.SemaphoreType.DMA((4,)),
            pltpu.SemaphoreType.DMA((4,)),
            pltpu.VMEM((4, rows, width), bf16),
            pltpu.SemaphoreType.DMA((4,)),
        ],
        compiler_params=pltpu.CompilerParams(
            collective_id=0, has_side_effects=True, vmem_limit_bytes=32 * 1024 * 1024
        ),
    )(*operands)
    grad_image, grad_text, loss = pl.pallas_call(
        functools.partial(hand_over, rows * grp * blk),
        out_shape=(
            jax.ShapeDtypeStruct((rows, width), f32),
            jax.ShapeDtypeStruct((rows, width), f32),
            jax.ShapeDtypeStruct((1, 1), f32),
        ),
        in_specs=[in_vmem] * 3,
        out_specs=(in_hbm,) * 3,
        scratch_shapes=[pltpu.VMEM((1, 1), f32), pltpu.SemaphoreType.DMA((3,))],
        compiler_params=pltpu.CompilerParams(vmem_limit_bytes=32 * 1024 * 1024),
    )(grad_image, grad_text, loss)
    return grad_image, grad_text, loss.reshape(())


def solution(mesh):
    in_specs = (
        P(("blk", "grp"), None),
        P(("grp", "blk"), None),
        P(("blk", "grp"), None),
        P(("grp", "blk"), None),
    )
    out_specs = (P(("blk", "grp"), None), P(("grp", "blk"), None), P())
    run = functools.partial(local, mesh.shape["grp"], mesh.shape["blk"])
    return jax.shard_map(run, mesh=mesh, in_specs=in_specs, out_specs=out_specs, check_vma=False)
```

```python
import functools

import jax
import jax.numpy as jnp
from jax import lax
from jax.experimental import pallas as pl
from jax.experimental.pallas import tpu as pltpu
from jax.sharding import PartitionSpec as P

mix_weight = 0.4
very_low = -1e30
MESH = pl.DeviceIdType.MESH
f32 = jnp.float32
bf16 = jnp.bfloat16


def lines_of(grp, blk):
    fine = 1
    while fine * blk < grp // fine and grp % (2 * fine) == 0:
        fine *= 2
    return fine


def split_index(index, size):
    if size & (size - 1) == 0:
        return index >> (size.bit_length() - 1), index & (size - 1)
    return lax.div(index, size), lax.rem(index, size)


def kernel(
    grp, blk, fine, rows,
    image_ref, text_ref, mimage_ref, mtext_ref,
    grad_image_ref, grad_text_ref, loss_ref,
    images, texts, image_stats, text_stats, plane_partial, line_partial, image_out, text_out,
    image_in, text_in,
    plane_send, plane_recv, line_send, line_recv, fetched, fetch_sem,
):
    n_plane, n_line = fine * blk, grp // fine
    width = image_ref.shape[1]
    half = width // 2
    lanes = images.shape[0] * images.shape[1]
    text_rows = n_line * rows
    text_lanes = text_stats.shape[2]
    my_grp, my_blk = lax.axis_index("grp"), lax.axis_index("blk")
    my_line, my_fine = lax.div(my_grp, fine), lax.rem(my_grp, fine)
    my_plane = my_fine * blk + my_blk

    def plane_peer(step):
        rank = lax.rem(my_plane + step, n_plane)
        return rank, (my_line * fine + lax.div(rank, blk), lax.rem(rank, blk))

    def line_peer(step):
        rank = lax.rem(my_line + step, n_line)
        return rank, (rank * fine + my_fine, my_blk)

    def send_all(peer_of, count, sems, phase, ends):
        send_sem, recv_sem = sems

        def step(s, carry):
            rank, peer = peer_of(s + 1)
            source, target = ends(s, rank)
            pltpu.make_async_remote_copy(
                src_ref=source, dst_ref=target,
                send_sem=send_sem.at[phase], recv_sem=recv_sem.at[phase],
                device_id=peer, device_id_type=MESH,
            ).start()
            return carry

        lax.fori_loop(0, count - 1, step, 0)

    def wait_all(sem, phase, span):
        pltpu.make_async_copy(span, span, sem.at[phase]).wait()

    plane_sems, line_sems = (plane_send, plane_recv), (line_send, line_recv)

    def to_plane(phase, ends):
        send_all(plane_peer, n_plane, plane_sems, phase, ends)

    def to_line(phase, ends):
        send_all(line_peer, n_line, line_sems, phase, ends)

    other_planes, other_lines = pl.ds(0, n_plane - 1), pl.ds(0, n_line - 1)
    plane_spans = [
        images.at[other_planes], image_stats.at[other_planes], image_in,
    ]
    line_spans = [texts.at[other_lines], text_stats.at[other_lines], text_in]

    barrier = pltpu.get_barrier_semaphore()

    def greet(peer_of, count):
        def step(s, carry):
            pl.semaphore_signal(
                barrier, inc=1, device_id=peer_of(s + 1)[1], device_id_type=MESH
            )
            return carry

        lax.fori_loop(0, count - 1, step, 0)

    greet(line_peer, n_line)
    greet(plane_peer, n_plane)
    fetches = [
        pltpu.make_async_copy(ref, fetched.at[k], fetch_sem.at[k])
        for k, ref in enumerate((text_ref, mtext_ref, image_ref, mimage_ref))
    ]
    for copy in fetches:
        copy.start()

    def pair(first, second):
        return jnp.concatenate([first.astype(f32), second.astype(f32)], axis=0).astype(bf16)

    for copy in fetches:
        copy.wait()
    texts[my_line] = pair(fetched[0], fetched[1])
    images[my_plane] = pair(fetched[2], fetched[3])
    pl.semaphore_wait(barrier, n_plane + n_line - 2)

    to_line(0, lambda s, rank: (texts.at[my_line], texts.at[my_line]))
    to_plane(0, lambda s, rank: (images.at[my_plane], images.at[my_plane]))

    shape = (text_rows, lanes)
    text_slot, text_sub = split_index(lax.broadcasted_iota(jnp.int32, shape, 0), rows)
    lane_slot, lane_sub = split_index(lax.broadcasted_iota(jnp.int32, shape, 1), 2 * rows)
    online = lane_sub < rows
    lane_fine, lane_blk = split_index(lane_slot, blk)
    image_tile = lane_blk * grp + my_line * fine + lane_fine
    text_tile = (text_slot * fine + my_fine) * blk + my_blk
    same = (image_tile == text_tile) & (lane_sub == text_sub)
    diagonal = jnp.where(same, 1.0, 0.0)
    square = (text_rows, text_lanes)
    eye = lax.broadcasted_iota(jnp.int32, square, 0) == lax.broadcasted_iota(jnp.int32, square, 1)

    def to_lanes(column):
        return jnp.sum(jnp.where(eye, column, 0.0), axis=0, keepdims=True)

    def to_column(row):
        return jnp.sum(jnp.where(eye, row, 0.0), axis=1, keepdims=True)

    wait_all(line_recv, 0, line_spans[0])
    wait_all(plane_recv, 0, plane_spans[0])
    scores = lax.dot_general(
        texts[...].reshape(n_line * 2 * rows, width), images[...].reshape(lanes, width),
        (((1,), (1,)), ((), ())), preferred_element_type=f32,
    ) * (width ** -0.5)
    scores = scores.reshape(n_line, 2, rows, lanes)
    score_on = scores[:, 0].reshape(shape)
    score_mom = pltpu.roll(scores[:, 1].reshape(shape), lanes - rows, 1)
    masked_on = jnp.where(online, score_on, very_low)
    masked_mom = jnp.where(online, score_mom, very_low)

    def stats(on, mom, axis):
        top_on = jnp.max(on, axis=axis, keepdims=True)
        top_mom = jnp.max(mom, axis=axis, keepdims=True)
        spread = jnp.exp(mom - top_mom)
        return (
            top_on, jnp.sum(jnp.exp(on - top_on), axis=axis, keepdims=True),
            top_mom, jnp.sum(spread, axis=axis, keepdims=True),
            jnp.sum(spread * score_on, axis=axis, keepdims=True),
        )

    def message(top_on, sum_on, top_mom, sum_mom, cross, diag):
        line = lax.broadcasted_iota(jnp.int32, (8, top_on.shape[1]), 0)
        tops = jnp.where(line == 0, top_on, jnp.where((line == 1) | (line == 2), top_mom, 0.0))
        sums = jnp.where(line == 0, sum_on, jnp.where(line == 1, sum_mom, 1.0))
        sums = jnp.where(line == 2, cross, jnp.where(line == 3, diag, sums))
        return jnp.concatenate([tops, sums], axis=0)

    def joined(held, count):
        top = held[0, :8]
        for k in range(1, count):
            top = jnp.maximum(top, held[k, :8])
        total = held[0, 8:] * jnp.exp(held[0, :8] - top)
        for k in range(1, count):
            total = total + held[k, 8:] * jnp.exp(held[k, :8] - top)
        return top + jnp.log(total), total

    text_part = [to_lanes(column) for column in stats(masked_on, masked_mom, 1)]
    in_text = lax.broadcasted_iota(jnp.int32, (1, text_lanes), 1) < text_rows
    for k in (1, 3):
        text_part[k] = jnp.where(in_text, text_part[k], 1.0)
    text_stats[my_line] = message(*text_part, jnp.zeros((1, text_lanes), f32))
    to_line(1, lambda s, rank: (text_stats.at[my_line], text_stats.at[my_line]))
    diag = jnp.sum(diagonal * score_on, axis=0, keepdims=True)
    image_stats[my_plane] = message(*stats(score_on, score_mom, 0), diag)
    to_plane(1, lambda s, rank: (image_stats.at[my_plane], image_stats.at[my_plane]))
    wait_all(line_recv, 1, line_spans[1])
    text_lse, text_total = joined(text_stats, n_line)
    col_on, col_mom = to_column(text_lse[0:1]), to_column(text_lse[1:2])
    prob_col = jnp.exp(masked_on - col_on)
    target_col = mix_weight * jnp.exp(masked_mom - col_mom) + (1.0 - mix_weight) * diagonal
    wait_all(plane_recv, 1, plane_spans[1])
    image_lse, image_total = joined(image_stats, n_plane)
    prob_row = jnp.exp(score_on - image_lse[0:1])
    target_row = (
        mix_weight * jnp.exp(score_mom - image_lse[1:2]) + (1.0 - mix_weight) * diagonal
    )
    grad = 0.5 * ((prob_row - target_row) + (prob_col - target_col))
    grad = jnp.where(online, grad, 0.0)

    def shares(lse, total, valid):
        share = lse[0:1] - mix_weight * (total[2:3] / total[1:2])
        return jnp.where(valid, share, 0.0)

    image_share = shares(image_lse, image_total, online[0:1])
    image_share = image_share - jnp.where(
        online[0:1], 2.0 * (1.0 - mix_weight) * image_total[3:4], 0.0
    )
    text_loss = shares(text_lse, text_total, in_text)
    def narrow(share):
        return sum(share[:, first:first + 128] for first in range(0, share.shape[1], 128))

    image_share, text_loss = narrow(image_share), narrow(text_loss)

    def rider(share):
        head = share.astype(bf16).astype(f32)
        middle = (share - head).astype(bf16).astype(f32)
        tail = share - head - middle
        line = lax.broadcasted_iota(jnp.int32, (2 * rows, 128), 0)
        return jnp.where(
            line == 0, head, jnp.where(line == 1, middle, jnp.where(line == 2, tail, 0.0))
        )

    image_rider, text_rider = rider(image_share), rider(text_loss)

    def folded(value):
        return jnp.concatenate([value[:, :half], value[:, half:]], axis=0)

    def put(target, value, extra):
        target[:, :half] = folded(value).astype(bf16)
        target[:, half:] = extra.astype(bf16)

    line_partial[...] = jnp.dot(
        grad.astype(bf16), images[...].reshape(lanes, width), preferred_element_type=f32
    ).reshape(n_line, rows, width)

    def text_ends(s, rank):
        put(text_out.at[s], line_partial[rank], image_rider)
        return text_out.at[s], text_in.at[s]

    to_line(2, text_ends)
    spaced = jnp.concatenate(
        [grad.reshape(n_line, 1, rows, lanes), jnp.zeros((n_line, 1, rows, lanes), f32)], axis=1
    ).reshape(n_line * 2 * rows, lanes)
    plane_partial[...] = lax.dot_general(
        spaced.astype(bf16), texts[...].reshape(n_line * 2 * rows, width),
        (((0,), (0,)), ((), ())), preferred_element_type=f32,
    ).reshape(n_plane, 2 * rows, width)

    def image_ends(s, rank):
        put(image_out.at[s], plane_partial[rank, :rows, :], text_rider)
        return image_out.at[s], image_in.at[s]

    to_plane(2, image_ends)

    def gathered(own, held, count, extra):
        total, share = folded(own), extra
        for s in range(count):
            total = total + held[s, :, :half].astype(f32)
            share = share + held[s, :, half:].astype(f32)
        return jnp.concatenate([total[:rows], total[rows:]], axis=1), share

    wait_all(line_recv, 2, line_spans[2])
    grad_text_ref[...], image_loss = gathered(
        line_partial[my_line], text_in, n_line - 1, image_rider
    )
    wait_all(plane_recv, 2, plane_spans[2])
    grad_image_ref[...], text_loss = gathered(
        plane_partial[my_plane, :rows, :], image_in, n_plane - 1, text_rider
    )
    loss_ref[...] = image_loss + text_loss

    for phase in range(3):
        wait_all(line_send, phase, line_spans[phase])
        wait_all(plane_send, phase, plane_spans[phase])


def hand_over(pairs, image_in, text_in, loss_in, image_out, text_out, loss_out, loss, sems):
    copies = [
        pltpu.make_async_copy(image_in, image_out, sems.at[0]),
        pltpu.make_async_copy(text_in, text_out, sems.at[1]),
        pltpu.make_async_copy(loss, loss_out, sems.at[2]),
    ]
    copies[0].start()
    copies[1].start()
    loss[...] = jnp.sum(loss_in[...], keepdims=True) / (2.0 * pairs)
    copies[2].start()
    for copy in copies:
        copy.wait()


def local(grp, blk, image, text, mimage, mtext):
    rows, width = image.shape
    fine = lines_of(grp, blk)
    n_plane, n_line = fine * blk, grp // fine
    lanes = n_plane * 2 * rows
    text_lanes = -(-n_line * rows // 128) * 128
    operands = [
        pltpu.with_memory_space_constraint(value, pltpu.HBM)
        for value in (image, text, mimage, mtext)
    ]
    in_hbm = pl.BlockSpec(memory_space=pltpu.HBM)
    in_vmem = pl.BlockSpec(memory_space=pltpu.VMEM)
    grad_image, grad_text, loss = pl.pallas_call(
        functools.partial(kernel, grp, blk, fine, rows),
        out_shape=(
            jax.ShapeDtypeStruct((rows, width), f32),
            jax.ShapeDtypeStruct((rows, width), f32),
            jax.ShapeDtypeStruct((2 * rows, 128), f32),
        ),
        in_specs=[in_hbm] * 4,
        out_specs=(in_vmem,) * 3,
        scratch_shapes=[
            pltpu.VMEM((n_plane, 2 * rows, width), bf16),
            pltpu.VMEM((n_line, 2 * rows, width), bf16),
            pltpu.VMEM((n_plane, 16, lanes), f32),
            pltpu.VMEM((n_line, 16, text_lanes), f32),
            pltpu.VMEM((n_plane, 2 * rows, width), f32),
            pltpu.VMEM((n_line, rows, width), f32),
            pltpu.VMEM((n_plane - 1, 2 * rows, width // 2 + 128), bf16),
            pltpu.VMEM((n_line - 1, 2 * rows, width // 2 + 128), bf16),
            pltpu.VMEM((n_plane - 1, 2 * rows, width // 2 + 128), bf16),
            pltpu.VMEM((n_line - 1, 2 * rows, width // 2 + 128), bf16),
            pltpu.SemaphoreType.DMA((3,)),
            pltpu.SemaphoreType.DMA((3,)),
            pltpu.SemaphoreType.DMA((3,)),
            pltpu.SemaphoreType.DMA((3,)),
            pltpu.VMEM((4, rows, width), bf16),
            pltpu.SemaphoreType.DMA((4,)),
        ],
        compiler_params=pltpu.CompilerParams(
            collective_id=0, has_side_effects=True, vmem_limit_bytes=32 * 1024 * 1024
        ),
    )(*operands)
    grad_image, grad_text, loss = pl.pallas_call(
        functools.partial(hand_over, rows * grp * blk),
        out_shape=(
            jax.ShapeDtypeStruct((rows, width), f32),
            jax.ShapeDtypeStruct((rows, width), f32),
            jax.ShapeDtypeStruct((1, 1), f32),
        ),
        in_specs=[in_vmem] * 3,
        out_specs=(in_hbm,) * 3,
        scratch_shapes=[pltpu.VMEM((1, 1), f32), pltpu.SemaphoreType.DMA((3,))],
        compiler_params=pltpu.CompilerParams(vmem_limit_bytes=32 * 1024 * 1024),
    )(grad_image, grad_text, loss)
    return grad_image, grad_text, loss.reshape(())


def solution(mesh):
    in_specs = (
        P(("blk", "grp"), None),
        P(("grp", "blk"), None),
        P(("blk", "grp"), None),
        P(("grp", "blk"), None),
    )
    out_specs = (P(("blk", "grp"), None), P(("grp", "blk"), None), P())
    run = functools.partial(local, mesh.shape["grp"], mesh.shape["blk"])
    return jax.shard_map(run, mesh=mesh, in_specs=in_specs, out_specs=out_specs, check_vma=False)
```

```python
import functools

import jax
import jax.numpy as jnp
from jax import lax
from jax.experimental import pallas as pl
from jax.experimental.pallas import tpu as pltpu
from jax.sharding import PartitionSpec as P

mix_weight = 0.4
very_low = -1e30
MESH = pl.DeviceIdType.MESH
f32 = jnp.float32
bf16 = jnp.bfloat16


def lines_of(grp, blk):
    fine = 1
    while fine * blk < grp // fine and grp % (2 * fine) == 0:
        fine *= 2
    return fine


def split_index(index, size):
    if size & (size - 1) == 0:
        return index >> (size.bit_length() - 1), index & (size - 1)
    return lax.div(index, size), lax.rem(index, size)


def kernel(
    grp, blk, fine, rows,
    image_ref, text_ref, mimage_ref, mtext_ref,
    grad_image_ref, grad_text_ref, loss_ref,
    images, texts, image_stats, text_stats, plane_partial, line_partial, image_out, text_out,
    image_in, text_in,
    plane_send, plane_recv, line_send, line_recv, fetched, fetch_sem,
):
    n_plane, n_line = fine * blk, grp // fine
    width = image_ref.shape[1]
    half = width // 2
    lanes = images.shape[0] * images.shape[1]
    text_rows = n_line * rows
    text_lanes = text_stats.shape[2]
    my_grp, my_blk = lax.axis_index("grp"), lax.axis_index("blk")
    my_line, my_fine = lax.div(my_grp, fine), lax.rem(my_grp, fine)
    my_plane = my_fine * blk + my_blk

    def plane_peer(step):
        rank = lax.rem(my_plane + step, n_plane)
        return rank, (my_line * fine + lax.div(rank, blk), lax.rem(rank, blk))

    def line_peer(step):
        rank = lax.rem(my_line + step, n_line)
        return rank, (rank * fine + my_fine, my_blk)

    def send_all(peer_of, count, sems, phase, ends):
        send_sem, recv_sem = sems

        def step(s, carry):
            rank, peer = peer_of(s + 1)
            source, target = ends(s, rank)
            pltpu.make_async_remote_copy(
                src_ref=source, dst_ref=target,
                send_sem=send_sem.at[phase], recv_sem=recv_sem.at[phase],
                device_id=peer, device_id_type=MESH,
            ).start()
            return carry

        lax.fori_loop(0, count - 1, step, 0)

    def wait_all(sem, phase, span):
        pltpu.make_async_copy(span, span, sem.at[phase]).wait()

    plane_sems, line_sems = (plane_send, plane_recv), (line_send, line_recv)

    def to_plane(phase, ends):
        send_all(plane_peer, n_plane, plane_sems, phase, ends)

    def to_line(phase, ends):
        send_all(line_peer, n_line, line_sems, phase, ends)

    other_planes, other_lines = pl.ds(0, n_plane - 1), pl.ds(0, n_line - 1)
    plane_spans = [
        images.at[other_planes], image_stats.at[other_planes], image_in,
    ]
    line_spans = [texts.at[other_lines], text_stats.at[other_lines], text_in]

    barrier = pltpu.get_barrier_semaphore()

    def greet(peer_of, count):
        def step(s, carry):
            pl.semaphore_signal(
                barrier, inc=1, device_id=peer_of(s + 1)[1], device_id_type=MESH
            )
            return carry

        lax.fori_loop(0, count - 1, step, 0)

    greet(line_peer, n_line)
    greet(plane_peer, n_plane)
    fetches = [
        pltpu.make_async_copy(ref, fetched.at[k], fetch_sem.at[k])
        for k, ref in enumerate((text_ref, mtext_ref, image_ref, mimage_ref))
    ]
    for copy in fetches:
        copy.start()

    def pair(first, second):
        return jnp.concatenate([first.astype(f32), second.astype(f32)], axis=0).astype(bf16)

    for copy in fetches:
        copy.wait()
    texts[my_line] = pair(fetched[0], fetched[1])
    images[my_plane] = pair(fetched[2], fetched[3])
    pl.semaphore_wait(barrier, n_plane + n_line - 2)

    to_line(0, lambda s, rank: (texts.at[my_line], texts.at[my_line]))
    to_plane(0, lambda s, rank: (images.at[my_plane], images.at[my_plane]))

    shape = (text_rows, lanes)
    text_slot, text_sub = split_index(lax.broadcasted_iota(jnp.int32, shape, 0), rows)
    lane_slot, lane_sub = split_index(lax.broadcasted_iota(jnp.int32, shape, 1), 2 * rows)
    online = lane_sub < rows
    lane_fine, lane_blk = split_index(lane_slot, blk)
    image_tile = lane_blk * grp + my_line * fine + lane_fine
    text_tile = (text_slot * fine + my_fine) * blk + my_blk
    same = (image_tile == text_tile) & (lane_sub == text_sub)
    diagonal = jnp.where(same, 1.0, 0.0)
    square = (text_rows, text_lanes)
    eye = lax.broadcasted_iota(jnp.int32, square, 0) == lax.broadcasted_iota(jnp.int32, square, 1)

    def to_lanes(column):
        return jnp.sum(jnp.where(eye, column, 0.0), axis=0, keepdims=True)

    def to_column(row):
        return jnp.sum(jnp.where(eye, row, 0.0), axis=1, keepdims=True)

    wait_all(line_recv, 0, line_spans[0])
    wait_all(plane_recv, 0, plane_spans[0])
    scores = lax.dot_general(
        texts[...].reshape(n_line * 2 * rows, width), images[...].reshape(lanes, width),
        (((1,), (1,)), ((), ())), preferred_element_type=f32,
    ) * (width ** -0.5)
    scores = scores.reshape(n_line, 2, rows, lanes)
    score_on = scores[:, 0].reshape(shape)
    score_mom = pltpu.roll(scores[:, 1].reshape(shape), lanes - rows, 1)
    masked_on = jnp.where(online, score_on, very_low)
    masked_mom = jnp.where(online, score_mom, very_low)

    def stats(on, mom, axis):
        top_on = jnp.max(on, axis=axis, keepdims=True)
        top_mom = jnp.max(mom, axis=axis, keepdims=True)
        spread = jnp.exp(mom - top_mom)
        return (
            top_on, jnp.sum(jnp.exp(on - top_on), axis=axis, keepdims=True),
            top_mom, jnp.sum(spread, axis=axis, keepdims=True),
            jnp.sum(spread * score_on, axis=axis, keepdims=True),
        )

    def message(top_on, sum_on, top_mom, sum_mom, cross, diag):
        line = lax.broadcasted_iota(jnp.int32, (8, top_on.shape[1]), 0)
        tile = diag
        for row, part in enumerate((top_on, top_mom, sum_on, sum_mom, cross)):
            tile = jnp.where(line == row, part, tile)
        return tile

    def joined(held, count):
        line = lax.broadcasted_iota(jnp.int32, held.shape[1:], 0)
        tiles = [held[k] for k in range(count)]
        tops = [
            jnp.where(line == 2, tile[0:1], jnp.where((line == 3) | (line == 4), tile[1:2], 0.0))
            for tile in tiles
        ]
        top = functools.reduce(jnp.maximum, tops)
        total = sum(tile * jnp.exp(mine - top) for tile, mine in zip(tiles, tops))
        return top[2:4] + jnp.log(total[2:4]), total

    text_part = [to_lanes(column) for column in stats(masked_on, masked_mom, 1)]
    in_text = lax.broadcasted_iota(jnp.int32, (1, text_lanes), 1) < text_rows
    for k in (1, 3):
        text_part[k] = jnp.where(in_text, text_part[k], 1.0)
    text_stats[my_line] = message(*text_part, jnp.zeros((1, text_lanes), f32))
    to_line(1, lambda s, rank: (text_stats.at[my_line], text_stats.at[my_line]))
    diag = jnp.sum(diagonal * score_on, axis=0, keepdims=True)
    image_stats[my_plane] = message(*stats(score_on, score_mom, 0), diag)
    to_plane(1, lambda s, rank: (image_stats.at[my_plane], image_stats.at[my_plane]))
    wait_all(line_recv, 1, line_spans[1])
    text_lse, text_total = joined(text_stats, n_line)
    col_on, col_mom = to_column(text_lse[0:1]), to_column(text_lse[1:2])
    prob_col = jnp.exp(masked_on - col_on)
    target_col = mix_weight * jnp.exp(masked_mom - col_mom) + (1.0 - mix_weight) * diagonal
    wait_all(plane_recv, 1, plane_spans[1])
    image_lse, image_total = joined(image_stats, n_plane)
    prob_row = jnp.exp(score_on - image_lse[0:1])
    target_row = (
        mix_weight * jnp.exp(score_mom - image_lse[1:2]) + (1.0 - mix_weight) * diagonal
    )
    grad = 0.5 * ((prob_row - target_row) + (prob_col - target_col))
    grad = jnp.where(online, grad, 0.0)

    def shares(lse, total, valid):
        share = lse[0:1] - mix_weight * (total[4:5] / total[3:4])
        return jnp.where(valid, share, 0.0)

    image_share = shares(image_lse, image_total, online[0:1])
    image_share = image_share - jnp.where(
        online[0:1], 2.0 * (1.0 - mix_weight) * image_total[5:6], 0.0
    )
    text_loss = shares(text_lse, text_total, in_text)

    def narrow(share):
        return sum(share[:, first:first + 128] for first in range(0, share.shape[1], 128))

    image_share, text_loss = narrow(image_share), narrow(text_loss)

    def rider(share):
        head = share.astype(bf16).astype(f32)
        middle = (share - head).astype(bf16).astype(f32)
        tail = share - head - middle
        line = lax.broadcasted_iota(jnp.int32, (2 * rows, 128), 0)
        return jnp.where(
            line == 0, head, jnp.where(line == 1, middle, jnp.where(line == 2, tail, 0.0))
        )

    image_rider, text_rider = rider(image_share), rider(text_loss)

    def folded(value):
        return jnp.concatenate([value[:, :half], value[:, half:]], axis=0)

    def put(target, value, extra):
        target[:, :half] = folded(value).astype(bf16)
        target[:, half:] = extra.astype(bf16)

    line_partial[...] = jnp.dot(
        grad.astype(bf16), images[...].reshape(lanes, width), preferred_element_type=f32
    ).reshape(n_line, rows, width)

    def text_ends(s, rank):
        put(text_out.at[s], line_partial[rank], image_rider)
        return text_out.at[s], text_in.at[s]

    to_line(2, text_ends)
    spaced = jnp.concatenate(
        [grad.reshape(n_line, 1, rows, lanes), jnp.zeros((n_line, 1, rows, lanes), f32)], axis=1
    ).reshape(n_line * 2 * rows, lanes)
    plane_partial[...] = lax.dot_general(
        spaced.astype(bf16), texts[...].reshape(n_line * 2 * rows, width),
        (((0,), (0,)), ((), ())), preferred_element_type=f32,
    ).reshape(n_plane, 2 * rows, width)

    def image_ends(s, rank):
        put(image_out.at[s], plane_partial[rank, :rows, :], text_rider)
        return image_out.at[s], image_in.at[s]

    to_plane(2, image_ends)

    def gathered(own, held, count, extra):
        total, share = folded(own), extra
        for s in range(count):
            total = total + held[s, :, :half].astype(f32)
            share = share + held[s, :, half:].astype(f32)
        return jnp.concatenate([total[:rows], total[rows:]], axis=1), share

    wait_all(line_recv, 2, line_spans[2])
    grad_text_ref[...], image_loss = gathered(
        line_partial[my_line], text_in, n_line - 1, image_rider
    )
    wait_all(plane_recv, 2, plane_spans[2])
    grad_image_ref[...], text_loss = gathered(
        plane_partial[my_plane, :rows, :], image_in, n_plane - 1, text_rider
    )
    loss_ref[...] = image_loss + text_loss

    for phase in range(3):
        wait_all(line_send, phase, line_spans[phase])
        wait_all(plane_send, phase, plane_spans[phase])


def hand_over(pairs, image_in, text_in, loss_in, image_out, text_out, loss_out, loss, sems):
    copies = [
        pltpu.make_async_copy(image_in, image_out, sems.at[0]),
        pltpu.make_async_copy(text_in, text_out, sems.at[1]),
        pltpu.make_async_copy(loss, loss_out, sems.at[2]),
    ]
    copies[0].start()
    copies[1].start()
    loss[...] = jnp.sum(loss_in[...], keepdims=True) / (2.0 * pairs)
    copies[2].start()
    for copy in copies:
        copy.wait()


def local(grp, blk, image, text, mimage, mtext):
    rows, width = image.shape
    fine = lines_of(grp, blk)
    n_plane, n_line = fine * blk, grp // fine
    lanes = n_plane * 2 * rows
    text_lanes = -(-n_line * rows // 128) * 128
    operands = [
        pltpu.with_memory_space_constraint(value, pltpu.HBM)
        for value in (image, text, mimage, mtext)
    ]
    in_hbm = pl.BlockSpec(memory_space=pltpu.HBM)
    in_vmem = pl.BlockSpec(memory_space=pltpu.VMEM)
    grad_image, grad_text, loss = pl.pallas_call(
        functools.partial(kernel, grp, blk, fine, rows),
        out_shape=(
            jax.ShapeDtypeStruct((rows, width), f32),
            jax.ShapeDtypeStruct((rows, width), f32),
            jax.ShapeDtypeStruct((2 * rows, 128), f32),
        ),
        in_specs=[in_hbm] * 4,
        out_specs=(in_vmem,) * 3,
        scratch_shapes=[
            pltpu.VMEM((n_plane, 2 * rows, width), bf16),
            pltpu.VMEM((n_line, 2 * rows, width), bf16),
            pltpu.VMEM((n_plane, 8, lanes), f32),
            pltpu.VMEM((n_line, 8, text_lanes), f32),
            pltpu.VMEM((n_plane, 2 * rows, width), f32),
            pltpu.VMEM((n_line, rows, width), f32),
            pltpu.VMEM((n_plane - 1, 2 * rows, width // 2 + 128), bf16),
            pltpu.VMEM((n_line - 1, 2 * rows, width // 2 + 128), bf16),
            pltpu.VMEM((n_plane - 1, 2 * rows, width // 2 + 128), bf16),
            pltpu.VMEM((n_line - 1, 2 * rows, width // 2 + 128), bf16),
            pltpu.SemaphoreType.DMA((3,)),
            pltpu.SemaphoreType.DMA((3,)),
            pltpu.SemaphoreType.DMA((3,)),
            pltpu.SemaphoreType.DMA((3,)),
            pltpu.VMEM((4, rows, width), bf16),
            pltpu.SemaphoreType.DMA((4,)),
        ],
        compiler_params=pltpu.CompilerParams(
            collective_id=0, has_side_effects=True, vmem_limit_bytes=32 * 1024 * 1024
        ),
    )(*operands)
    grad_image, grad_text, loss = pl.pallas_call(
        functools.partial(hand_over, rows * grp * blk),
        out_shape=(
            jax.ShapeDtypeStruct((rows, width), f32),
            jax.ShapeDtypeStruct((rows, width), f32),
            jax.ShapeDtypeStruct((1, 1), f32),
        ),
        in_specs=[in_vmem] * 3,
        out_specs=(in_hbm,) * 3,
        scratch_shapes=[pltpu.VMEM((1, 1), f32), pltpu.SemaphoreType.DMA((3,))],
        compiler_params=pltpu.CompilerParams(vmem_limit_bytes=32 * 1024 * 1024),
    )(grad_image, grad_text, loss)
    return grad_image, grad_text, loss.reshape(())


def solution(mesh):
    in_specs = (
        P(("blk", "grp"), None),
        P(("grp", "blk"), None),
        P(("blk", "grp"), None),
        P(("grp", "blk"), None),
    )
    out_specs = (P(("blk", "grp"), None), P(("grp", "blk"), None), P())
    run = functools.partial(local, mesh.shape["grp"], mesh.shape["blk"])
    return jax.shard_map(run, mesh=mesh, in_specs=in_specs, out_specs=out_specs, check_vma=False)
```

```python
import functools

import jax
import jax.numpy as jnp
from jax import lax
from jax.experimental import pallas as pl
from jax.experimental.pallas import tpu as pltpu
from jax.sharding import PartitionSpec as P

mix_weight = 0.4
very_low = -1e30
MESH = pl.DeviceIdType.MESH
f32 = jnp.float32
bf16 = jnp.bfloat16


def lines_of(grp, blk):
    fine = 1
    while fine * blk < grp // fine and grp % (2 * fine) == 0:
        fine *= 2
    return fine


def split_index(index, size):
    if size & (size - 1) == 0:
        return index >> (size.bit_length() - 1), index & (size - 1)
    return lax.div(index, size), lax.rem(index, size)


def kernel(
    grp, blk, fine, rows,
    image_ref, text_ref, mimage_ref, mtext_ref,
    grad_image_ref, grad_text_ref, loss_ref,
    images, texts, image_stats, text_stats, plane_partial, line_partial, image_out, text_out,
    image_in, text_in,
    plane_send, plane_recv, line_send, line_recv, fetched, fetch_sem, chip_recv,
):
    n_plane, n_line = fine * blk, grp // fine
    width = image_ref.shape[1]
    half = width // 2
    lanes = images.shape[0] * images.shape[1]
    text_rows = n_line * rows
    text_lanes = text_stats.shape[2]
    my_grp, my_blk = lax.axis_index("grp"), lax.axis_index("blk")
    my_line, my_fine = lax.div(my_grp, fine), lax.rem(my_grp, fine)
    my_plane = my_fine * blk + my_blk

    def plane_peer(step):
        rank = lax.rem(my_plane + step, n_plane)
        return rank, (my_line * fine + lax.div(rank, blk), lax.rem(rank, blk))

    def line_peer(step):
        rank = lax.rem(my_line + step, n_line)
        return rank, (rank * fine + my_fine, my_blk)

    def send_all(peer_of, count, sems, phase, ends):
        send_sem, recv_sem = sems

        def step(s, carry):
            rank, peer = peer_of(s + 1)
            source, target = ends(s, rank)
            pltpu.make_async_remote_copy(
                src_ref=source, dst_ref=target,
                send_sem=send_sem.at[phase], recv_sem=recv_sem.at[phase],
                device_id=peer, device_id_type=MESH,
            ).start()
            return carry

        lax.fori_loop(0, count - 1, step, 0)

    def wait_all(sem, phase, span):
        pltpu.make_async_copy(span, span, sem.at[phase]).wait()

    plane_sems, line_sems = (plane_send, plane_recv), (line_send, line_recv)

    def to_plane(phase, ends):
        send_all(plane_peer, n_plane, plane_sems, phase, ends)

    def to_line(phase, ends):
        send_all(line_peer, n_line, line_sems, phase, ends)

    other_planes, other_lines = pl.ds(0, n_plane - 1), pl.ds(0, n_line - 1)
    plane_spans = [
        images.at[other_planes], image_stats.at[other_planes], image_in,
    ]
    line_spans = [texts.at[other_lines], text_stats.at[other_lines], text_in]

    barrier = pltpu.get_barrier_semaphore()

    def greet(peer_of, count):
        def step(s, carry):
            pl.semaphore_signal(
                barrier, inc=1, device_id=peer_of(s + 1)[1], device_id_type=MESH
            )
            return carry

        lax.fori_loop(0, count - 1, step, 0)

    greet(line_peer, n_line)
    greet(plane_peer, n_plane)
    fetches = [
        pltpu.make_async_copy(ref, fetched.at[k], fetch_sem.at[k])
        for k, ref in enumerate((text_ref, mtext_ref, image_ref, mimage_ref))
    ]
    for copy in fetches:
        copy.start()

    def pair(first, second):
        return jnp.concatenate([first.astype(f32), second.astype(f32)], axis=0).astype(bf16)

    for copy in fetches:
        copy.wait()
    texts[my_line] = pair(fetched[0], fetched[1])
    images[my_plane] = pair(fetched[2], fetched[3])
    pl.semaphore_wait(barrier, n_plane + n_line - 2)

    to_line(0, lambda s, rank: (texts.at[my_line], texts.at[my_line]))
    chips = n_plane // 2
    core = lax.rem(my_plane, 2)
    sibling = my_plane + 1 - 2 * core

    def peer_at(rank):
        return (my_line * fine + lax.div(rank, blk), lax.rem(rank, blk))

    def pass_on(rank, peer, sem):
        return pltpu.make_async_remote_copy(
            src_ref=images.at[rank], dst_ref=images.at[rank],
            send_sem=plane_send.at[0], recv_sem=sem,
            device_id=peer_at(peer), device_id_type=MESH,
        )

    for d in range(1, chips):
        pass_on(my_plane, lax.rem(my_plane + 2 * d, n_plane), chip_recv.at[d - 1]).start()
    pass_on(my_plane, sibling, plane_recv.at[0]).start()

    shape = (text_rows, lanes)
    text_slot, text_sub = split_index(lax.broadcasted_iota(jnp.int32, shape, 0), rows)
    lane_slot, lane_sub = split_index(lax.broadcasted_iota(jnp.int32, shape, 1), 2 * rows)
    online = lane_sub < rows
    lane_fine, lane_blk = split_index(lane_slot, blk)
    image_tile = lane_blk * grp + my_line * fine + lane_fine
    text_tile = (text_slot * fine + my_fine) * blk + my_blk
    same = (image_tile == text_tile) & (lane_sub == text_sub)
    diagonal = jnp.where(same, 1.0, 0.0)
    square = (text_rows, text_lanes)
    eye = lax.broadcasted_iota(jnp.int32, square, 0) == lax.broadcasted_iota(jnp.int32, square, 1)

    def to_lanes(column):
        return jnp.sum(jnp.where(eye, column, 0.0), axis=0, keepdims=True)

    def to_column(row):
        return jnp.sum(jnp.where(eye, row, 0.0), axis=1, keepdims=True)

    for d in range(1, chips):
        source = lax.rem(my_plane + n_plane - 2 * d, n_plane)
        wait_all(chip_recv, d - 1, images.at[source])
        pass_on(source, sibling, plane_recv.at[0]).start()
    wait_all(line_recv, 0, line_spans[0])
    wait_all(plane_recv, 0, images.at[pl.ds(0, chips)])
    scores = lax.dot_general(
        texts[...].reshape(n_line * 2 * rows, width), images[...].reshape(lanes, width),
        (((1,), (1,)), ((), ())), preferred_element_type=f32,
    ) * (width ** -0.5)
    scores = scores.reshape(n_line, 2, rows, lanes)
    score_on = scores[:, 0].reshape(shape)
    score_mom = pltpu.roll(scores[:, 1].reshape(shape), lanes - rows, 1)
    masked_on = jnp.where(online, score_on, very_low)
    masked_mom = jnp.where(online, score_mom, very_low)

    def stats(on, mom, axis):
        top_on = jnp.max(on, axis=axis, keepdims=True)
        top_mom = jnp.max(mom, axis=axis, keepdims=True)
        spread = jnp.exp(mom - top_mom)
        return (
            top_on, jnp.sum(jnp.exp(on - top_on), axis=axis, keepdims=True),
            top_mom, jnp.sum(spread, axis=axis, keepdims=True),
            jnp.sum(spread * score_on, axis=axis, keepdims=True),
        )

    def message(top_on, sum_on, top_mom, sum_mom, cross, diag):
        line = lax.broadcasted_iota(jnp.int32, (8, top_on.shape[1]), 0)
        tile = diag
        for row, part in enumerate((top_on, top_mom, sum_on, sum_mom, cross)):
            tile = jnp.where(line == row, part, tile)
        return tile

    def joined(held, count):
        line = lax.broadcasted_iota(jnp.int32, held.shape[1:], 0)
        tiles = [held[k] for k in range(count)]
        tops = [
            jnp.where(line == 2, tile[0:1], jnp.where((line == 3) | (line == 4), tile[1:2], 0.0))
            for tile in tiles
        ]
        top = functools.reduce(jnp.maximum, tops)
        total = sum(tile * jnp.exp(mine - top) for tile, mine in zip(tiles, tops))
        return top[2:4] + jnp.log(total[2:4]), total

    text_part = [to_lanes(column) for column in stats(masked_on, masked_mom, 1)]
    in_text = lax.broadcasted_iota(jnp.int32, (1, text_lanes), 1) < text_rows
    for k in (1, 3):
        text_part[k] = jnp.where(in_text, text_part[k], 1.0)
    text_stats[my_line] = message(*text_part, jnp.zeros((1, text_lanes), f32))
    to_line(1, lambda s, rank: (text_stats.at[my_line], text_stats.at[my_line]))
    diag = jnp.sum(diagonal * score_on, axis=0, keepdims=True)
    image_stats[my_plane] = message(*stats(score_on, score_mom, 0), diag)
    to_plane(1, lambda s, rank: (image_stats.at[my_plane], image_stats.at[my_plane]))
    wait_all(line_recv, 1, line_spans[1])
    text_lse, text_total = joined(text_stats, n_line)
    col_on, col_mom = to_column(text_lse[0:1]), to_column(text_lse[1:2])
    prob_col = jnp.exp(masked_on - col_on)
    target_col = mix_weight * jnp.exp(masked_mom - col_mom) + (1.0 - mix_weight) * diagonal
    wait_all(plane_recv, 1, plane_spans[1])
    image_lse, image_total = joined(image_stats, n_plane)
    prob_row = jnp.exp(score_on - image_lse[0:1])
    target_row = (
        mix_weight * jnp.exp(score_mom - image_lse[1:2]) + (1.0 - mix_weight) * diagonal
    )
    grad = 0.5 * ((prob_row - target_row) + (prob_col - target_col))
    grad = jnp.where(online, grad, 0.0)

    def shares(lse, total, valid):
        share = lse[0:1] - mix_weight * (total[4:5] / total[3:4])
        return jnp.where(valid, share, 0.0)

    image_share = shares(image_lse, image_total, online[0:1])
    image_share = image_share - jnp.where(
        online[0:1], 2.0 * (1.0 - mix_weight) * image_total[5:6], 0.0
    )
    text_loss = shares(text_lse, text_total, in_text)

    def narrow(share):
        return sum(share[:, first:first + 128] for first in range(0, share.shape[1], 128))

    image_share, text_loss = narrow(image_share), narrow(text_loss)

    def rider(share):
        head = share.astype(bf16).astype(f32)
        middle = (share - head).astype(bf16).astype(f32)
        tail = share - head - middle
        line = lax.broadcasted_iota(jnp.int32, (2 * rows, 128), 0)
        return jnp.where(
            line == 0, head, jnp.where(line == 1, middle, jnp.where(line == 2, tail, 0.0))
        )

    image_rider, text_rider = rider(image_share), rider(text_loss)

    def folded(value):
        return jnp.concatenate([value[:, :half], value[:, half:]], axis=0)

    def put(target, value, extra):
        target[:, :half] = folded(value).astype(bf16)
        target[:, half:] = extra.astype(bf16)

    line_partial[...] = jnp.dot(
        grad.astype(bf16), images[...].reshape(lanes, width), preferred_element_type=f32
    ).reshape(n_line, rows, width)

    def text_ends(s, rank):
        put(text_out.at[s], line_partial[rank], image_rider)
        return text_out.at[s], text_in.at[s]

    to_line(2, text_ends)
    spaced = jnp.concatenate(
        [grad.reshape(n_line, 1, rows, lanes), jnp.zeros((n_line, 1, rows, lanes), f32)], axis=1
    ).reshape(n_line * 2 * rows, lanes)
    plane_partial[...] = lax.dot_general(
        spaced.astype(bf16), texts[...].reshape(n_line * 2 * rows, width),
        (((0,), (0,)), ((), ())), preferred_element_type=f32,
    ).reshape(n_plane, 2 * rows, width)

    def image_ends(s, rank):
        put(image_out.at[s], plane_partial[rank, :rows, :], text_rider)
        return image_out.at[s], image_in.at[s]

    to_plane(2, image_ends)

    def gathered(own, held, count, extra):
        total, share = folded(own), extra
        for s in range(count):
            total = total + held[s, :, :half].astype(f32)
            share = share + held[s, :, half:].astype(f32)
        return jnp.concatenate([total[:rows], total[rows:]], axis=1), share

    wait_all(line_recv, 2, line_spans[2])
    grad_text_ref[...], image_loss = gathered(
        line_partial[my_line], text_in, n_line - 1, image_rider
    )
    wait_all(plane_recv, 2, plane_spans[2])
    grad_image_ref[...], text_loss = gathered(
        plane_partial[my_plane, :rows, :], image_in, n_plane - 1, text_rider
    )
    loss_ref[...] = image_loss + text_loss

    for phase in range(3):
        wait_all(line_send, phase, line_spans[phase])
        wait_all(plane_send, phase, plane_spans[phase])


def hand_over(pairs, image_in, text_in, loss_in, image_out, text_out, loss_out, loss, sems):
    copies = [
        pltpu.make_async_copy(image_in, image_out, sems.at[0]),
        pltpu.make_async_copy(text_in, text_out, sems.at[1]),
        pltpu.make_async_copy(loss, loss_out, sems.at[2]),
    ]
    copies[0].start()
    copies[1].start()
    loss[...] = jnp.sum(loss_in[...], keepdims=True) / (2.0 * pairs)
    copies[2].start()
    for copy in copies:
        copy.wait()


def local(grp, blk, image, text, mimage, mtext):
    rows, width = image.shape
    fine = lines_of(grp, blk)
    n_plane, n_line = fine * blk, grp // fine
    lanes = n_plane * 2 * rows
    text_lanes = -(-n_line * rows // 128) * 128
    operands = [
        pltpu.with_memory_space_constraint(value, pltpu.HBM)
        for value in (image, text, mimage, mtext)
    ]
    in_hbm = pl.BlockSpec(memory_space=pltpu.HBM)
    in_vmem = pl.BlockSpec(memory_space=pltpu.VMEM)
    grad_image, grad_text, loss = pl.pallas_call(
        functools.partial(kernel, grp, blk, fine, rows),
        out_shape=(
            jax.ShapeDtypeStruct((rows, width), f32),
            jax.ShapeDtypeStruct((rows, width), f32),
            jax.ShapeDtypeStruct((2 * rows, 128), f32),
        ),
        in_specs=[in_hbm] * 4,
        out_specs=(in_vmem,) * 3,
        scratch_shapes=[
            pltpu.VMEM((n_plane, 2 * rows, width), bf16),
            pltpu.VMEM((n_line, 2 * rows, width), bf16),
            pltpu.VMEM((n_plane, 8, lanes), f32),
            pltpu.VMEM((n_line, 8, text_lanes), f32),
            pltpu.VMEM((n_plane, 2 * rows, width), f32),
            pltpu.VMEM((n_line, rows, width), f32),
            pltpu.VMEM((n_plane - 1, 2 * rows, width // 2 + 128), bf16),
            pltpu.VMEM((n_line - 1, 2 * rows, width // 2 + 128), bf16),
            pltpu.VMEM((n_plane - 1, 2 * rows, width // 2 + 128), bf16),
            pltpu.VMEM((n_line - 1, 2 * rows, width // 2 + 128), bf16),
            pltpu.SemaphoreType.DMA((3,)),
            pltpu.SemaphoreType.DMA((3,)),
            pltpu.SemaphoreType.DMA((3,)),
            pltpu.SemaphoreType.DMA((3,)),
            pltpu.VMEM((4, rows, width), bf16),
            pltpu.SemaphoreType.DMA((4,)),
            pltpu.SemaphoreType.DMA((max(n_plane // 2 - 1, 1),)),
        ],
        compiler_params=pltpu.CompilerParams(
            collective_id=0, has_side_effects=True, vmem_limit_bytes=32 * 1024 * 1024
        ),
    )(*operands)
    grad_image, grad_text, loss = pl.pallas_call(
        functools.partial(hand_over, rows * grp * blk),
        out_shape=(
            jax.ShapeDtypeStruct((rows, width), f32),
            jax.ShapeDtypeStruct((rows, width), f32),
            jax.ShapeDtypeStruct((1, 1), f32),
        ),
        in_specs=[in_vmem] * 3,
        out_specs=(in_hbm,) * 3,
        scratch_shapes=[pltpu.VMEM((1, 1), f32), pltpu.SemaphoreType.DMA((3,))],
        compiler_params=pltpu.CompilerParams(vmem_limit_bytes=32 * 1024 * 1024),
    )(grad_image, grad_text, loss)
    return grad_image, grad_text, loss.reshape(())


def solution(mesh):
    in_specs = (
        P(("blk", "grp"), None),
        P(("grp", "blk"), None),
        P(("blk", "grp"), None),
        P(("grp", "blk"), None),
    )
    out_specs = (P(("blk", "grp"), None), P(("grp", "blk"), None), P())
    run = functools.partial(local, mesh.shape["grp"], mesh.shape["blk"])
    return jax.shard_map(run, mesh=mesh, in_specs=in_specs, out_specs=out_specs, check_vma=False)
```

```python
import functools

import jax
import jax.numpy as jnp
from jax import lax
from jax.experimental import pallas as pl
from jax.experimental.pallas import tpu as pltpu
from jax.sharding import PartitionSpec as P

mix_weight = 0.4
very_low = -1e30
MESH = pl.DeviceIdType.MESH
f32 = jnp.float32
bf16 = jnp.bfloat16


def lines_of(grp, blk):
    fine = 1
    while fine * blk < grp // fine and grp % (2 * fine) == 0:
        fine *= 2
    return fine


def split_index(index, size):
    if size & (size - 1) == 0:
        return index >> (size.bit_length() - 1), index & (size - 1)
    return lax.div(index, size), lax.rem(index, size)


def kernel(
    grp, blk, fine, rows,
    image_ref, text_ref, mimage_ref, mtext_ref,
    grad_image_ref, grad_text_ref, loss_ref,
    images, texts, image_stats, text_stats, plane_partial, line_partial, image_out, text_out,
    image_in, text_in,
    plane_send, plane_recv, line_send, line_recv, fetched, fetch_sem,
):
    n_plane, n_line = fine * blk, grp // fine
    width = image_ref.shape[1]
    half = width // 2
    lanes = images.shape[0] * images.shape[1]
    text_rows = n_line * rows
    text_lanes = text_stats.shape[2]
    my_grp, my_blk = lax.axis_index("grp"), lax.axis_index("blk")
    my_line, my_fine = lax.div(my_grp, fine), lax.rem(my_grp, fine)
    my_plane = my_fine * blk + my_blk

    def plane_peer(step):
        rank = lax.rem(my_plane + step, n_plane)
        return rank, (my_line * fine + lax.div(rank, blk), lax.rem(rank, blk))

    def line_peer(step):
        rank = lax.rem(my_line + step, n_line)
        return rank, (rank * fine + my_fine, my_blk)

    def send_all(peer_of, count, sems, phase, ends):
        send_sem, recv_sem = sems

        def step(s, carry):
            rank, peer = peer_of(s + 1)
            source, target = ends(s, rank)
            pltpu.make_async_remote_copy(
                src_ref=source, dst_ref=target,
                send_sem=send_sem.at[phase], recv_sem=recv_sem.at[phase],
                device_id=peer, device_id_type=MESH,
            ).start()
            return carry

        lax.fori_loop(0, count - 1, step, 0)

    def wait_all(sem, phase, span):
        pltpu.make_async_copy(span, span, sem.at[phase]).wait()

    plane_sems, line_sems = (plane_send, plane_recv), (line_send, line_recv)

    def to_plane(phase, ends):
        send_all(plane_peer, n_plane, plane_sems, phase, ends)

    def to_line(phase, ends):
        send_all(line_peer, n_line, line_sems, phase, ends)

    other_planes, other_lines = pl.ds(0, n_plane - 1), pl.ds(0, n_line - 1)
    plane_spans = [
        images.at[other_planes], image_stats.at[other_planes], image_in,
    ]
    line_spans = [texts.at[other_lines], text_stats.at[other_lines], text_in]

    barrier = pltpu.get_barrier_semaphore()

    def greet(peer_of, count):
        def step(s, carry):
            pl.semaphore_signal(
                barrier, inc=1, device_id=peer_of(s + 1)[1], device_id_type=MESH
            )
            return carry

        lax.fori_loop(0, count - 1, step, 0)

    greet(line_peer, n_line)
    greet(plane_peer, n_plane)
    fetches = [
        pltpu.make_async_copy(ref, fetched.at[k], fetch_sem.at[k])
        for k, ref in enumerate((text_ref, mtext_ref, image_ref, mimage_ref))
    ]
    for copy in fetches:
        copy.start()

    def pair(first, second):
        return jnp.concatenate([first.astype(f32), second.astype(f32)], axis=0).astype(bf16)

    fetches[0].wait()
    fetches[1].wait()
    texts[my_line] = pair(fetched[0], fetched[1])
    pl.semaphore_wait(barrier, n_plane + n_line - 2)
    to_line(0, lambda s, rank: (texts.at[my_line], texts.at[my_line]))
    fetches[2].wait()
    fetches[3].wait()
    images[my_plane] = pair(fetched[2], fetched[3])
    to_plane(0, lambda s, rank: (images.at[my_plane], images.at[my_plane]))

    shape = (text_rows, lanes)
    text_slot, text_sub = split_index(lax.broadcasted_iota(jnp.int32, shape, 0), rows)
    lane_slot, lane_sub = split_index(lax.broadcasted_iota(jnp.int32, shape, 1), 2 * rows)
    online = lane_sub < rows
    lane_fine, lane_blk = split_index(lane_slot, blk)
    image_tile = lane_blk * grp + my_line * fine + lane_fine
    text_tile = (text_slot * fine + my_fine) * blk + my_blk
    same = (image_tile == text_tile) & (lane_sub == text_sub)
    diagonal = jnp.where(same, 1.0, 0.0)
    square = (text_rows, text_lanes)
    eye = lax.broadcasted_iota(jnp.int32, square, 0) == lax.broadcasted_iota(jnp.int32, square, 1)

    def to_lanes(column):
        return jnp.sum(jnp.where(eye, column, 0.0), axis=0, keepdims=True)

    def to_column(row):
        return jnp.sum(jnp.where(eye, row, 0.0), axis=1, keepdims=True)

    wait_all(line_recv, 0, line_spans[0])
    wait_all(plane_recv, 0, plane_spans[0])
    scores = lax.dot_general(
        texts[...].reshape(n_line * 2 * rows, width), images[...].reshape(lanes, width),
        (((1,), (1,)), ((), ())), preferred_element_type=f32,
    ) * (width ** -0.5)
    scores = scores.reshape(n_line, 2, rows, lanes)
    score_on = scores[:, 0].reshape(shape)
    score_mom = pltpu.roll(scores[:, 1].reshape(shape), lanes - rows, 1)
    masked_on = jnp.where(online, score_on, very_low)
    masked_mom = jnp.where(online, score_mom, very_low)

    def stats(on, mom, axis):
        top_on = jnp.max(on, axis=axis, keepdims=True)
        top_mom = jnp.max(mom, axis=axis, keepdims=True)
        spread = jnp.exp(mom - top_mom)
        return (
            top_on, jnp.sum(jnp.exp(on - top_on), axis=axis, keepdims=True),
            top_mom, jnp.sum(spread, axis=axis, keepdims=True),
            jnp.sum(spread * score_on, axis=axis, keepdims=True),
        )

    def message(top_on, sum_on, top_mom, sum_mom, cross, diag):
        line = lax.broadcasted_iota(jnp.int32, (8, top_on.shape[1]), 0)
        tile = diag
        for row, part in enumerate((top_on, top_mom, sum_on, sum_mom, cross)):
            tile = jnp.where(line == row, part, tile)
        return tile

    def joined(held, count):
        line = lax.broadcasted_iota(jnp.int32, held.shape[1:], 0)
        tiles = [held[k] for k in range(count)]
        tops = [
            jnp.where(line == 2, tile[0:1], jnp.where((line == 3) | (line == 4), tile[1:2], 0.0))
            for tile in tiles
        ]
        top = functools.reduce(jnp.maximum, tops)
        total = sum(tile * jnp.exp(mine - top) for tile, mine in zip(tiles, tops))
        return top[2:4] + jnp.log(total[2:4]), total

    text_part = [to_lanes(column) for column in stats(masked_on, masked_mom, 1)]
    in_text = lax.broadcasted_iota(jnp.int32, (1, text_lanes), 1) < text_rows
    for k in (1, 3):
        text_part[k] = jnp.where(in_text, text_part[k], 1.0)
    text_stats[my_line] = message(*text_part, jnp.zeros((1, text_lanes), f32))
    to_line(1, lambda s, rank: (text_stats.at[my_line], text_stats.at[my_line]))
    diag = jnp.sum(diagonal * score_on, axis=0, keepdims=True)
    image_stats[my_plane] = message(*stats(score_on, score_mom, 0), diag)
    to_plane(1, lambda s, rank: (image_stats.at[my_plane], image_stats.at[my_plane]))
    wait_all(line_recv, 1, line_spans[1])
    text_lse, text_total = joined(text_stats, n_line)
    col_on, col_mom = to_column(text_lse[0:1]), to_column(text_lse[1:2])
    prob_col = jnp.exp(masked_on - col_on)
    target_col = mix_weight * jnp.exp(masked_mom - col_mom) + (1.0 - mix_weight) * diagonal
    wait_all(plane_recv, 1, plane_spans[1])
    image_lse, image_total = joined(image_stats, n_plane)
    prob_row = jnp.exp(score_on - image_lse[0:1])
    target_row = (
        mix_weight * jnp.exp(score_mom - image_lse[1:2]) + (1.0 - mix_weight) * diagonal
    )
    grad = 0.5 * ((prob_row - target_row) + (prob_col - target_col))
    grad = jnp.where(online, grad, 0.0)

    def shares(lse, total, valid):
        share = lse[0:1] - mix_weight * (total[4:5] / total[3:4])
        return jnp.where(valid, share, 0.0)

    image_share = shares(image_lse, image_total, online[0:1])
    image_share = image_share - jnp.where(
        online[0:1], 2.0 * (1.0 - mix_weight) * image_total[5:6], 0.0
    )
    text_loss = shares(text_lse, text_total, in_text)

    def narrow(share):
        return sum(share[:, first:first + 128] for first in range(0, share.shape[1], 128))

    image_share, text_loss = narrow(image_share), narrow(text_loss)

    def rider(share):
        head = share.astype(bf16).astype(f32)
        middle = (share - head).astype(bf16).astype(f32)
        tail = share - head - middle
        line = lax.broadcasted_iota(jnp.int32, (2 * rows, 128), 0)
        return jnp.where(
            line == 0, head, jnp.where(line == 1, middle, jnp.where(line == 2, tail, 0.0))
        )

    image_rider, text_rider = rider(image_share), rider(text_loss)

    def folded(value):
        return jnp.concatenate([value[:, :half], value[:, half:]], axis=0)

    def put(target, value, extra):
        target[:, :half] = folded(value).astype(bf16)
        target[:, half:] = extra.astype(bf16)

    line_partial[...] = jnp.dot(
        grad.astype(bf16), images[...].reshape(lanes, width), preferred_element_type=f32
    ).reshape(n_line, rows, width)

    def text_ends(s, rank):
        put(text_out.at[s], line_partial[rank], image_rider)
        return text_out.at[s], text_in.at[s]

    to_line(2, text_ends)
    spaced = jnp.concatenate(
        [grad.reshape(n_line, 1, rows, lanes), jnp.zeros((n_line, 1, rows, lanes), f32)], axis=1
    ).reshape(n_line * 2 * rows, lanes)
    plane_partial[...] = lax.dot_general(
        spaced.astype(bf16), texts[...].reshape(n_line * 2 * rows, width),
        (((0,), (0,)), ((), ())), preferred_element_type=f32,
    ).reshape(n_plane, 2 * rows, width)

    def image_ends(s, rank):
        put(image_out.at[s], plane_partial[rank, :rows, :], text_rider)
        return image_out.at[s], image_in.at[s]

    to_plane(2, image_ends)

    def gathered(own, held, count, extra):
        total, share = folded(own), extra
        for s in range(count):
            total = total + held[s, :, :half].astype(f32)
            share = share + held[s, :, half:].astype(f32)
        return jnp.concatenate([total[:rows], total[rows:]], axis=1), share

    wait_all(line_recv, 2, line_spans[2])
    grad_text_ref[...], image_loss = gathered(
        line_partial[my_line], text_in, n_line - 1, image_rider
    )
    wait_all(plane_recv, 2, plane_spans[2])
    grad_image_ref[...], text_loss = gathered(
        plane_partial[my_plane, :rows, :], image_in, n_plane - 1, text_rider
    )
    loss_ref[...] = image_loss + text_loss

    for phase in range(3):
        wait_all(line_send, phase, line_spans[phase])
        wait_all(plane_send, phase, plane_spans[phase])


def hand_over(pairs, image_in, text_in, loss_in, image_out, text_out, loss_out, loss, sems):
    copies = [
        pltpu.make_async_copy(image_in, image_out, sems.at[0]),
        pltpu.make_async_copy(text_in, text_out, sems.at[1]),
        pltpu.make_async_copy(loss, loss_out, sems.at[2]),
    ]
    copies[0].start()
    copies[1].start()
    loss[...] = jnp.sum(loss_in[...], keepdims=True) / (2.0 * pairs)
    copies[2].start()
    for copy in copies:
        copy.wait()


def local(grp, blk, image, text, mimage, mtext):
    rows, width = image.shape
    fine = lines_of(grp, blk)
    n_plane, n_line = fine * blk, grp // fine
    lanes = n_plane * 2 * rows
    text_lanes = -(-n_line * rows // 128) * 128
    operands = [
        pltpu.with_memory_space_constraint(value, pltpu.HBM)
        for value in (image, text, mimage, mtext)
    ]
    in_hbm = pl.BlockSpec(memory_space=pltpu.HBM)
    in_vmem = pl.BlockSpec(memory_space=pltpu.VMEM)
    grad_image, grad_text, loss = pl.pallas_call(
        functools.partial(kernel, grp, blk, fine, rows),
        out_shape=(
            jax.ShapeDtypeStruct((rows, width), f32),
            jax.ShapeDtypeStruct((rows, width), f32),
            jax.ShapeDtypeStruct((2 * rows, 128), f32),
        ),
        in_specs=[in_hbm] * 4,
        out_specs=(in_vmem,) * 3,
        scratch_shapes=[
            pltpu.VMEM((n_plane, 2 * rows, width), bf16),
            pltpu.VMEM((n_line, 2 * rows, width), bf16),
            pltpu.VMEM((n_plane, 8, lanes), f32),
            pltpu.VMEM((n_line, 8, text_lanes), f32),
            pltpu.VMEM((n_plane, 2 * rows, width), f32),
            pltpu.VMEM((n_line, rows, width), f32),
            pltpu.VMEM((n_plane - 1, 2 * rows, width // 2 + 128), bf16),
            pltpu.VMEM((n_line - 1, 2 * rows, width // 2 + 128), bf16),
            pltpu.VMEM((n_plane - 1, 2 * rows, width // 2 + 128), bf16),
            pltpu.VMEM((n_line - 1, 2 * rows, width // 2 + 128), bf16),
            pltpu.SemaphoreType.DMA((3,)),
            pltpu.SemaphoreType.DMA((3,)),
            pltpu.SemaphoreType.DMA((3,)),
            pltpu.SemaphoreType.DMA((3,)),
            pltpu.VMEM((4, rows, width), bf16),
            pltpu.SemaphoreType.DMA((4,)),
        ],
        compiler_params=pltpu.CompilerParams(
            collective_id=0, has_side_effects=True, vmem_limit_bytes=32 * 1024 * 1024
        ),
    )(*operands)
    grad_image, grad_text, loss = pl.pallas_call(
        functools.partial(hand_over, rows * grp * blk),
        out_shape=(
            jax.ShapeDtypeStruct((rows, width), f32),
            jax.ShapeDtypeStruct((rows, width), f32),
            jax.ShapeDtypeStruct((1, 1), f32),
        ),
        in_specs=[in_vmem] * 3,
        out_specs=(in_hbm,) * 3,
        scratch_shapes=[pltpu.VMEM((1, 1), f32), pltpu.SemaphoreType.DMA((3,))],
        compiler_params=pltpu.CompilerParams(vmem_limit_bytes=32 * 1024 * 1024),
    )(grad_image, grad_text, loss)
    return grad_image, grad_text, loss.reshape(())


def solution(mesh):
    in_specs = (
        P(("blk", "grp"), None),
        P(("grp", "blk"), None),
        P(("blk", "grp"), None),
        P(("grp", "blk"), None),
    )
    out_specs = (P(("blk", "grp"), None), P(("grp", "blk"), None), P())
    run = functools.partial(local, mesh.shape["grp"], mesh.shape["blk"])
    return jax.shard_map(run, mesh=mesh, in_specs=in_specs, out_specs=out_specs, check_vma=False)
```

```python
import functools

import jax
import jax.numpy as jnp
from jax import lax
from jax.experimental import pallas as pl
from jax.experimental.pallas import tpu as pltpu
from jax.sharding import PartitionSpec as P

mix_weight = 0.4
very_low = -1e30
MESH = pl.DeviceIdType.MESH
f32 = jnp.float32
bf16 = jnp.bfloat16


def lines_of(grp, blk):
    fine = 1
    while fine * blk < grp // fine and grp % (2 * fine) == 0:
        fine *= 2
    return fine


def split_index(index, size):
    if size & (size - 1) == 0:
        return index >> (size.bit_length() - 1), index & (size - 1)
    return lax.div(index, size), lax.rem(index, size)


def kernel(
    grp, blk, fine, rows,
    image_ref, text_ref, mimage_ref, mtext_ref,
    grad_image_ref, grad_text_ref, loss_ref,
    images, texts, image_stats, text_stats, plane_partial, line_partial, image_out, text_out,
    image_in, text_in,
    plane_send, plane_recv, line_send, line_recv, fetched, fetch_sem,
):
    n_plane, n_line = fine * blk, grp // fine
    width = image_ref.shape[1]
    half = width // 2
    lanes = images.shape[0] * images.shape[1]
    text_rows = n_line * rows
    text_lanes = text_stats.shape[2]
    my_grp, my_blk = lax.axis_index("grp"), lax.axis_index("blk")
    my_line, my_fine = lax.div(my_grp, fine), lax.rem(my_grp, fine)
    my_plane = my_fine * blk + my_blk

    def plane_peer(step):
        rank = lax.rem(my_plane + step, n_plane)
        return rank, (my_line * fine + lax.div(rank, blk), lax.rem(rank, blk))

    def line_peer(step):
        rank = lax.rem(my_line + step, n_line)
        return rank, (rank * fine + my_fine, my_blk)

    def send_all(peer_of, count, sems, phase, ends):
        send_sem, recv_sem = sems

        def step(s, carry):
            rank, peer = peer_of(s + 1)
            source, target = ends(s, rank)
            pltpu.make_async_remote_copy(
                src_ref=source, dst_ref=target,
                send_sem=send_sem.at[phase], recv_sem=recv_sem.at[phase],
                device_id=peer, device_id_type=MESH,
            ).start()
            return carry

        lax.fori_loop(0, count - 1, step, 0)

    def wait_all(sem, phase, span):
        pltpu.make_async_copy(span, span, sem.at[phase]).wait()

    plane_sems, line_sems = (plane_send, plane_recv), (line_send, line_recv)

    def to_plane(phase, ends):
        send_all(plane_peer, n_plane, plane_sems, phase, ends)

    def to_line(phase, ends):
        send_all(line_peer, n_line, line_sems, phase, ends)

    other_planes, other_lines = pl.ds(0, n_plane - 1), pl.ds(0, n_line - 1)
    plane_spans = [
        images.at[other_planes], image_stats.at[other_planes], image_in,
    ]
    line_spans = [texts.at[other_lines], text_stats.at[other_lines], text_in]

    barrier = pltpu.get_barrier_semaphore()

    def greet(peer_of, count):
        def step(s, carry):
            pl.semaphore_signal(
                barrier, inc=1, device_id=peer_of(s + 1)[1], device_id_type=MESH
            )
            return carry

        lax.fori_loop(0, count - 1, step, 0)

    greet(line_peer, n_line)
    greet(plane_peer, n_plane)
    fetches = [
        pltpu.make_async_copy(ref, fetched.at[k], fetch_sem.at[k])
        for k, ref in enumerate((text_ref, mtext_ref, image_ref, mimage_ref))
    ]
    for copy in fetches:
        copy.start()

    def pair(first, second):
        return jnp.concatenate([first.astype(f32), second.astype(f32)], axis=0).astype(bf16)

    fetches[0].wait()
    fetches[1].wait()
    texts[my_line] = pair(fetched[0], fetched[1])
    pl.semaphore_wait(barrier, n_plane + n_line - 2)
    to_line(0, lambda s, rank: (texts.at[my_line], texts.at[my_line]))
    fetches[2].wait()
    fetches[3].wait()
    images[my_plane] = pair(fetched[2], fetched[3])
    to_plane(0, lambda s, rank: (images.at[my_plane], images.at[my_plane]))

    shape = (text_rows, lanes)
    text_slot, text_sub = split_index(lax.broadcasted_iota(jnp.int32, shape, 0), rows)
    lane_slot, lane_sub = split_index(lax.broadcasted_iota(jnp.int32, shape, 1), 2 * rows)
    online = lane_sub < rows
    lane_fine, lane_blk = split_index(lane_slot, blk)
    image_tile = lane_blk * grp + my_line * fine + lane_fine
    text_tile = (text_slot * fine + my_fine) * blk + my_blk
    same = (image_tile == text_tile) & (lane_sub == text_sub)
    diagonal = jnp.where(same, 1.0, 0.0)
    square = (text_rows, text_lanes)
    eye = lax.broadcasted_iota(jnp.int32, square, 0) == lax.broadcasted_iota(jnp.int32, square, 1)

    def to_lanes(column):
        return jnp.sum(jnp.where(eye, column, 0.0), axis=0, keepdims=True)

    def to_column(row):
        return jnp.sum(jnp.where(eye, row, 0.0), axis=1, keepdims=True)

    wait_all(line_recv, 0, line_spans[0])
    wait_all(plane_recv, 0, plane_spans[0])
    scores = lax.dot_general(
        texts[...].reshape(n_line * 2 * rows, width), images[...].reshape(lanes, width),
        (((1,), (1,)), ((), ())), preferred_element_type=f32,
    ) * (width ** -0.5)
    scores = scores.reshape(n_line, 2, rows, lanes)
    score_on = scores[:, 0].reshape(shape)
    score_mom = pltpu.roll(scores[:, 1].reshape(shape), lanes - rows, 1)
    masked_on = jnp.where(online, score_on, very_low)
    masked_mom = jnp.where(online, score_mom, very_low)

    def stats(on, mom, axis):
        top_on = jnp.max(on, axis=axis, keepdims=True)
        top_mom = jnp.max(mom, axis=axis, keepdims=True)
        spread = jnp.exp(mom - top_mom)
        return (
            top_on, jnp.sum(jnp.exp(on - top_on), axis=axis, keepdims=True),
            top_mom, jnp.sum(spread, axis=axis, keepdims=True),
            jnp.sum(spread * score_on, axis=axis, keepdims=True),
        )

    def message(top_on, sum_on, top_mom, sum_mom, cross, diag):
        line = lax.broadcasted_iota(jnp.int32, (8, top_on.shape[1]), 0)
        tile = diag
        for row, part in enumerate((top_on, top_mom, sum_on, sum_mom, cross)):
            tile = jnp.where(line == row, part, tile)
        return tile

    def joined(held, count):
        line = lax.broadcasted_iota(jnp.int32, held.shape[1:], 0)
        tiles = [held[k] for k in range(count)]
        tops = [
            jnp.where(line == 2, tile[0:1], jnp.where((line == 3) | (line == 4), tile[1:2], 0.0))
            for tile in tiles
        ]
        top = functools.reduce(jnp.maximum, tops)
        total = sum(tile * jnp.exp(mine - top) for tile, mine in zip(tiles, tops))
        return top[2:4] + jnp.log(total[2:4]), total

    text_part = [to_lanes(column) for column in stats(masked_on, masked_mom, 1)]
    in_text = lax.broadcasted_iota(jnp.int32, (1, text_lanes), 1) < text_rows
    for k in (1, 3):
        text_part[k] = jnp.where(in_text, text_part[k], 1.0)
    text_stats[my_line] = message(*text_part, jnp.zeros((1, text_lanes), f32))
    to_line(1, lambda s, rank: (text_stats.at[my_line], text_stats.at[my_line]))
    diag = jnp.sum(diagonal * score_on, axis=0, keepdims=True)
    image_stats[my_plane] = message(*stats(score_on, score_mom, 0), diag)
    to_plane(1, lambda s, rank: (image_stats.at[my_plane], image_stats.at[my_plane]))
    wait_all(line_recv, 1, line_spans[1])
    text_lse, text_total = joined(text_stats, n_line)
    col_on, col_mom = to_column(text_lse[0:1]), to_column(text_lse[1:2])
    prob_col = jnp.exp(masked_on - col_on)
    target_col = mix_weight * jnp.exp(masked_mom - col_mom) + (1.0 - mix_weight) * diagonal
    wait_all(plane_recv, 1, plane_spans[1])
    image_lse, image_total = joined(image_stats, n_plane)
    prob_row = jnp.exp(score_on - image_lse[0:1])
    target_row = (
        mix_weight * jnp.exp(score_mom - image_lse[1:2]) + (1.0 - mix_weight) * diagonal
    )
    grad = 0.5 * ((prob_row - target_row) + (prob_col - target_col))
    grad = jnp.where(online, grad, 0.0)

    def shares(lse, total, valid):
        share = lse[0:1] - mix_weight * (total[4:5] / total[3:4])
        return jnp.where(valid, share, 0.0)

    image_share = shares(image_lse, image_total, online[0:1])
    image_share = image_share - jnp.where(
        online[0:1], 2.0 * (1.0 - mix_weight) * image_total[5:6], 0.0
    )
    text_loss = shares(text_lse, text_total, in_text)

    def narrow(share):
        return sum(share[:, first:first + 128] for first in range(0, share.shape[1], 128))

    image_share, text_loss = narrow(image_share), narrow(text_loss)

    def rider(share):
        head = share.astype(bf16).astype(f32)
        middle = (share - head).astype(bf16).astype(f32)
        tail = share - head - middle
        line = lax.broadcasted_iota(jnp.int32, (2 * rows, 128), 0)
        return jnp.where(
            line == 0, head, jnp.where(line == 1, middle, jnp.where(line == 2, tail, 0.0))
        )

    image_rider, text_rider = rider(image_share), rider(text_loss)

    def folded(value):
        return jnp.concatenate([value[:, :half], value[:, half:]], axis=0)

    def put(target, value, extra):
        target[:, :half] = folded(value).astype(bf16)
        target[:, half:] = extra.astype(bf16)

    line_partial[...] = jnp.dot(
        grad.astype(bf16), images[...].reshape(lanes, width), preferred_element_type=f32
    ).reshape(n_line, rows, width)

    def text_ends(s, rank):
        put(text_out.at[s], line_partial[rank], image_rider)
        return text_out.at[s], text_in.at[s]

    to_line(2, text_ends)
    spaced = jnp.concatenate(
        [grad.reshape(n_line, 1, rows, lanes), jnp.zeros((n_line, 1, rows, lanes), f32)], axis=1
    ).reshape(n_line * 2 * rows, lanes)
    plane_partial[...] = lax.dot_general(
        spaced.astype(bf16), texts[...].reshape(n_line * 2 * rows, width),
        (((0,), (0,)), ((), ())), preferred_element_type=f32,
    ).reshape(n_plane, 2 * rows, width)

    def image_ends(s, rank):
        put(image_out.at[s], plane_partial[rank, :rows, :], text_rider)
        return image_out.at[s], image_in.at[s]

    to_plane(2, image_ends)

    def gathered(own, held, count, extra):
        total, share = folded(own), extra
        for s in range(count):
            total = total + held[s, :, :half].astype(f32)
            share = share + held[s, :, half:].astype(f32)
        return jnp.concatenate([total[:rows], total[rows:]], axis=1), share

    for phase in range(2):
        wait_all(line_send, phase, line_spans[phase])
        wait_all(plane_send, phase, plane_spans[phase])
    wait_all(line_recv, 2, line_spans[2])
    grad_text_ref[...], image_loss = gathered(
        line_partial[my_line], text_in, n_line - 1, image_rider
    )
    wait_all(plane_recv, 2, plane_spans[2])
    grad_image_ref[...], text_loss = gathered(
        plane_partial[my_plane, :rows, :], image_in, n_plane - 1, text_rider
    )
    loss_ref[...] = image_loss + text_loss

    wait_all(line_send, 2, line_spans[2])
    wait_all(plane_send, 2, plane_spans[2])


def hand_over(pairs, image_in, text_in, loss_in, image_out, text_out, loss_out, loss, sems):
    copies = [
        pltpu.make_async_copy(image_in, image_out, sems.at[0]),
        pltpu.make_async_copy(text_in, text_out, sems.at[1]),
        pltpu.make_async_copy(loss, loss_out, sems.at[2]),
    ]
    copies[0].start()
    copies[1].start()
    loss[...] = jnp.sum(loss_in[...], keepdims=True) / (2.0 * pairs)
    copies[2].start()
    for copy in copies:
        copy.wait()


def local(grp, blk, image, text, mimage, mtext):
    rows, width = image.shape
    fine = lines_of(grp, blk)
    n_plane, n_line = fine * blk, grp // fine
    lanes = n_plane * 2 * rows
    text_lanes = -(-n_line * rows // 128) * 128
    operands = [
        pltpu.with_memory_space_constraint(value, pltpu.HBM)
        for value in (image, text, mimage, mtext)
    ]
    in_hbm = pl.BlockSpec(memory_space=pltpu.HBM)
    in_vmem = pl.BlockSpec(memory_space=pltpu.VMEM)
    grad_image, grad_text, loss = pl.pallas_call(
        functools.partial(kernel, grp, blk, fine, rows),
        out_shape=(
            jax.ShapeDtypeStruct((rows, width), f32),
            jax.ShapeDtypeStruct((rows, width), f32),
            jax.ShapeDtypeStruct((2 * rows, 128), f32),
        ),
        in_specs=[in_hbm] * 4,
        out_specs=(in_vmem,) * 3,
        scratch_shapes=[
            pltpu.VMEM((n_plane, 2 * rows, width), bf16),
            pltpu.VMEM((n_line, 2 * rows, width), bf16),
            pltpu.VMEM((n_plane, 8, lanes), f32),
            pltpu.VMEM((n_line, 8, text_lanes), f32),
            pltpu.VMEM((n_plane, 2 * rows, width), f32),
            pltpu.VMEM((n_line, rows, width), f32),
            pltpu.VMEM((n_plane - 1, 2 * rows, width // 2 + 128), bf16),
            pltpu.VMEM((n_line - 1, 2 * rows, width // 2 + 128), bf16),
            pltpu.VMEM((n_plane - 1, 2 * rows, width // 2 + 128), bf16),
            pltpu.VMEM((n_line - 1, 2 * rows, width // 2 + 128), bf16),
            pltpu.SemaphoreType.DMA((3,)),
            pltpu.SemaphoreType.DMA((3,)),
            pltpu.SemaphoreType.DMA((3,)),
            pltpu.SemaphoreType.DMA((3,)),
            pltpu.VMEM((4, rows, width), bf16),
            pltpu.SemaphoreType.DMA((4,)),
        ],
        compiler_params=pltpu.CompilerParams(
            collective_id=0, has_side_effects=True, vmem_limit_bytes=32 * 1024 * 1024
        ),
    )(*operands)
    grad_image, grad_text, loss = pl.pallas_call(
        functools.partial(hand_over, rows * grp * blk),
        out_shape=(
            jax.ShapeDtypeStruct((rows, width), f32),
            jax.ShapeDtypeStruct((rows, width), f32),
            jax.ShapeDtypeStruct((1, 1), f32),
        ),
        in_specs=[in_vmem] * 3,
        out_specs=(in_hbm,) * 3,
        scratch_shapes=[pltpu.VMEM((1, 1), f32), pltpu.SemaphoreType.DMA((3,))],
        compiler_params=pltpu.CompilerParams(vmem_limit_bytes=32 * 1024 * 1024),
    )(grad_image, grad_text, loss)
    return grad_image, grad_text, loss.reshape(())


def solution(mesh):
    in_specs = (
        P(("blk", "grp"), None),
        P(("grp", "blk"), None),
        P(("blk", "grp"), None),
        P(("grp", "blk"), None),
    )
    out_specs = (P(("blk", "grp"), None), P(("grp", "blk"), None), P())
    run = functools.partial(local, mesh.shape["grp"], mesh.shape["blk"])
    return jax.shard_map(run, mesh=mesh, in_specs=in_specs, out_specs=out_specs, check_vma=False)
```

```python
import functools

import jax
import jax.numpy as jnp
from jax import lax
from jax.experimental import pallas as pl
from jax.experimental.pallas import tpu as pltpu
from jax.sharding import PartitionSpec as P

mix_weight = 0.4
very_low = -1e30
MESH = pl.DeviceIdType.MESH
f32 = jnp.float32
bf16 = jnp.bfloat16


def lines_of(grp, blk):
    fine = 1
    while fine * blk < grp // fine and grp % (2 * fine) == 0:
        fine *= 2
    return fine


def split_index(index, size):
    if size & (size - 1) == 0:
        return index >> (size.bit_length() - 1), index & (size - 1)
    return lax.div(index, size), lax.rem(index, size)


def kernel(
    grp, blk, fine, rows,
    image_ref, text_ref, mimage_ref, mtext_ref,
    grad_image_ref, grad_text_ref, loss_ref,
    images, texts, image_stats, text_stats, plane_partial, line_partial, image_out, text_out,
    image_in, text_in,
    plane_send, plane_recv, line_send, line_recv, fetched, fetch_sem,
):
    n_plane, n_line = fine * blk, grp // fine
    width = image_ref.shape[1]
    half = width // 2
    lanes = images.shape[0] * images.shape[1]
    text_rows = n_line * rows
    text_lanes = text_stats.shape[2]
    my_grp, my_blk = lax.axis_index("grp"), lax.axis_index("blk")
    my_line, my_fine = lax.div(my_grp, fine), lax.rem(my_grp, fine)
    my_plane = my_fine * blk + my_blk

    def plane_peer(step):
        rank = lax.rem(my_plane + step, n_plane)
        return rank, (my_line * fine + lax.div(rank, blk), lax.rem(rank, blk))

    def line_peer(step):
        rank = lax.rem(my_line + step, n_line)
        return rank, (rank * fine + my_fine, my_blk)

    def send_all(peer_of, count, sems, phase, ends):
        send_sem, recv_sem = sems

        def step(s, carry):
            rank, peer = peer_of(s + 1)
            source, target = ends(s, rank)
            pltpu.make_async_remote_copy(
                src_ref=source, dst_ref=target,
                send_sem=send_sem.at[phase], recv_sem=recv_sem.at[phase],
                device_id=peer, device_id_type=MESH,
            ).start()
            return carry

        lax.fori_loop(0, count - 1, step, 0, unroll=count <= 4)

    def wait_all(sem, phase, span):
        pltpu.make_async_copy(span, span, sem.at[phase]).wait()

    plane_sems, line_sems = (plane_send, plane_recv), (line_send, line_recv)

    def to_plane(phase, ends):
        send_all(plane_peer, n_plane, plane_sems, phase, ends)

    def to_line(phase, ends):
        send_all(line_peer, n_line, line_sems, phase, ends)

    other_planes, other_lines = pl.ds(0, n_plane - 1), pl.ds(0, n_line - 1)
    plane_spans = [
        images.at[other_planes], image_stats.at[other_planes], image_in,
    ]
    line_spans = [texts.at[other_lines], text_stats.at[other_lines], text_in]

    barrier = pltpu.get_barrier_semaphore()

    def greet(peer_of, count):
        def step(s, carry):
            pl.semaphore_signal(
                barrier, inc=1, device_id=peer_of(s + 1)[1], device_id_type=MESH
            )
            return carry

        lax.fori_loop(0, count - 1, step, 0, unroll=count <= 4)

    greet(line_peer, n_line)
    greet(plane_peer, n_plane)
    fetches = [
        pltpu.make_async_copy(ref, fetched.at[k], fetch_sem.at[k])
        for k, ref in enumerate((text_ref, mtext_ref, image_ref, mimage_ref))
    ]
    for copy in fetches:
        copy.start()

    def pair(first, second):
        return jnp.concatenate([first.astype(f32), second.astype(f32)], axis=0).astype(bf16)

    fetches[0].wait()
    fetches[1].wait()
    texts[my_line] = pair(fetched[0], fetched[1])
    pl.semaphore_wait(barrier, n_plane + n_line - 2)
    to_line(0, lambda s, rank: (texts.at[my_line], texts.at[my_line]))
    fetches[2].wait()
    fetches[3].wait()
    images[my_plane] = pair(fetched[2], fetched[3])
    to_plane(0, lambda s, rank: (images.at[my_plane], images.at[my_plane]))

    shape = (text_rows, lanes)
    text_slot, text_sub = split_index(lax.broadcasted_iota(jnp.int32, shape, 0), rows)
    lane_slot, lane_sub = split_index(lax.broadcasted_iota(jnp.int32, shape, 1), 2 * rows)
    online = lane_sub < rows
    lane_fine, lane_blk = split_index(lane_slot, blk)
    image_tile = lane_blk * grp + my_line * fine + lane_fine
    text_tile = (text_slot * fine + my_fine) * blk + my_blk
    same = (image_tile == text_tile) & (lane_sub == text_sub)
    diagonal = jnp.where(same, 1.0, 0.0)
    square = (text_rows, text_lanes)
    eye = lax.broadcasted_iota(jnp.int32, square, 0) == lax.broadcasted_iota(jnp.int32, square, 1)

    def to_lanes(column):
        return jnp.sum(jnp.where(eye, column, 0.0), axis=0, keepdims=True)

    def to_column(row):
        return jnp.sum(jnp.where(eye, row, 0.0), axis=1, keepdims=True)

    wait_all(line_recv, 0, line_spans[0])
    wait_all(plane_recv, 0, plane_spans[0])
    scores = lax.dot_general(
        texts[...].reshape(n_line * 2 * rows, width), images[...].reshape(lanes, width),
        (((1,), (1,)), ((), ())), preferred_element_type=f32,
    ) * (width ** -0.5)
    scores = scores.reshape(n_line, 2, rows, lanes)
    score_on = scores[:, 0].reshape(shape)
    score_mom = pltpu.roll(scores[:, 1].reshape(shape), lanes - rows, 1)
    masked_on = jnp.where(online, score_on, very_low)
    masked_mom = jnp.where(online, score_mom, very_low)

    def stats(on, mom, axis):
        top_on = jnp.max(on, axis=axis, keepdims=True)
        top_mom = jnp.max(mom, axis=axis, keepdims=True)
        spread = jnp.exp(mom - top_mom)
        return (
            top_on, jnp.sum(jnp.exp(on - top_on), axis=axis, keepdims=True),
            top_mom, jnp.sum(spread, axis=axis, keepdims=True),
            jnp.sum(spread * score_on, axis=axis, keepdims=True),
        )

    def message(top_on, sum_on, top_mom, sum_mom, cross, diag):
        line = lax.broadcasted_iota(jnp.int32, (8, top_on.shape[1]), 0)
        tile = diag
        for row, part in enumerate((top_on, top_mom, sum_on, sum_mom, cross)):
            tile = jnp.where(line == row, part, tile)
        return tile

    def joined(held, count):
        line = lax.broadcasted_iota(jnp.int32, held.shape[1:], 0)
        tiles = [held[k] for k in range(count)]
        tops = [
            jnp.where(line == 2, tile[0:1], jnp.where((line == 3) | (line == 4), tile[1:2], 0.0))
            for tile in tiles
        ]
        top = functools.reduce(jnp.maximum, tops)
        total = sum(tile * jnp.exp(mine - top) for tile, mine in zip(tiles, tops))
        return top[2:4] + jnp.log(total[2:4]), total

    text_part = [to_lanes(column) for column in stats(masked_on, masked_mom, 1)]
    in_text = lax.broadcasted_iota(jnp.int32, (1, text_lanes), 1) < text_rows
    for k in (1, 3):
        text_part[k] = jnp.where(in_text, text_part[k], 1.0)
    text_stats[my_line] = message(*text_part, jnp.zeros((1, text_lanes), f32))
    to_line(1, lambda s, rank: (text_stats.at[my_line], text_stats.at[my_line]))
    diag = jnp.sum(diagonal * score_on, axis=0, keepdims=True)
    image_stats[my_plane] = message(*stats(score_on, score_mom, 0), diag)
    to_plane(1, lambda s, rank: (image_stats.at[my_plane], image_stats.at[my_plane]))
    wait_all(line_recv, 1, line_spans[1])
    text_lse, text_total = joined(text_stats, n_line)
    col_on, col_mom = to_column(text_lse[0:1]), to_column(text_lse[1:2])
    prob_col = jnp.exp(masked_on - col_on)
    target_col = mix_weight * jnp.exp(masked_mom - col_mom) + (1.0 - mix_weight) * diagonal
    wait_all(plane_recv, 1, plane_spans[1])
    image_lse, image_total = joined(image_stats, n_plane)
    prob_row = jnp.exp(score_on - image_lse[0:1])
    target_row = (
        mix_weight * jnp.exp(score_mom - image_lse[1:2]) + (1.0 - mix_weight) * diagonal
    )
    grad = 0.5 * ((prob_row - target_row) + (prob_col - target_col))
    grad = jnp.where(online, grad, 0.0)

    def shares(lse, total, valid):
        share = lse[0:1] - mix_weight * (total[4:5] / total[3:4])
        return jnp.where(valid, share, 0.0)

    image_share = shares(image_lse, image_total, online[0:1])
    image_share = image_share - jnp.where(
        online[0:1], 2.0 * (1.0 - mix_weight) * image_total[5:6], 0.0
    )
    text_loss = shares(text_lse, text_total, in_text)

    def narrow(share):
        return sum(share[:, first:first + 128] for first in range(0, share.shape[1], 128))

    image_share, text_loss = narrow(image_share), narrow(text_loss)

    def rider(share):
        head = share.astype(bf16).astype(f32)
        middle = (share - head).astype(bf16).astype(f32)
        tail = share - head - middle
        line = lax.broadcasted_iota(jnp.int32, (2 * rows, 128), 0)
        return jnp.where(
            line == 0, head, jnp.where(line == 1, middle, jnp.where(line == 2, tail, 0.0))
        )

    image_rider, text_rider = rider(image_share), rider(text_loss)

    def folded(value):
        return jnp.concatenate([value[:, :half], value[:, half:]], axis=0)

    def put(target, value, extra):
        target[:, :half] = folded(value).astype(bf16)
        target[:, half:] = extra.astype(bf16)

    line_partial[...] = jnp.dot(
        grad.astype(bf16), images[...].reshape(lanes, width), preferred_element_type=f32
    ).reshape(n_line, rows, width)

    def text_ends(s, rank):
        put(text_out.at[s], line_partial[rank], image_rider)
        return text_out.at[s], text_in.at[s]

    to_line(2, text_ends)
    spaced = jnp.concatenate(
        [grad.reshape(n_line, 1, rows, lanes), jnp.zeros((n_line, 1, rows, lanes), f32)], axis=1
    ).reshape(n_line * 2 * rows, lanes)
    plane_partial[...] = lax.dot_general(
        spaced.astype(bf16), texts[...].reshape(n_line * 2 * rows, width),
        (((0,), (0,)), ((), ())), preferred_element_type=f32,
    ).reshape(n_plane, 2 * rows, width)

    def image_ends(s, rank):
        put(image_out.at[s], plane_partial[rank, :rows, :], text_rider)
        return image_out.at[s], image_in.at[s]

    to_plane(2, image_ends)

    def gathered(own, held, count, extra):
        total, share = folded(own), extra
        for s in range(count):
            total = total + held[s, :, :half].astype(f32)
            share = share + held[s, :, half:].astype(f32)
        return jnp.concatenate([total[:rows], total[rows:]], axis=1), share

    wait_all(line_recv, 2, line_spans[2])
    grad_text_ref[...], image_loss = gathered(
        line_partial[my_line], text_in, n_line - 1, image_rider
    )
    wait_all(plane_recv, 2, plane_spans[2])
    grad_image_ref[...], text_loss = gathered(
        plane_partial[my_plane, :rows, :], image_in, n_plane - 1, text_rider
    )
    loss_ref[...] = image_loss + text_loss

    for phase in range(3):
        wait_all(line_send, phase, line_spans[phase])
        wait_all(plane_send, phase, plane_spans[phase])


def hand_over(pairs, image_in, text_in, loss_in, image_out, text_out, loss_out, loss, sems):
    copies = [
        pltpu.make_async_copy(image_in, image_out, sems.at[0]),
        pltpu.make_async_copy(text_in, text_out, sems.at[1]),
        pltpu.make_async_copy(loss, loss_out, sems.at[2]),
    ]
    copies[0].start()
    copies[1].start()
    loss[...] = jnp.sum(loss_in[...], keepdims=True) / (2.0 * pairs)
    copies[2].start()
    for copy in copies:
        copy.wait()


def local(grp, blk, image, text, mimage, mtext):
    rows, width = image.shape
    fine = lines_of(grp, blk)
    n_plane, n_line = fine * blk, grp // fine
    lanes = n_plane * 2 * rows
    text_lanes = -(-n_line * rows // 128) * 128
    operands = [
        pltpu.with_memory_space_constraint(value, pltpu.HBM)
        for value in (image, text, mimage, mtext)
    ]
    in_hbm = pl.BlockSpec(memory_space=pltpu.HBM)
    in_vmem = pl.BlockSpec(memory_space=pltpu.VMEM)
    grad_image, grad_text, loss = pl.pallas_call(
        functools.partial(kernel, grp, blk, fine, rows),
        out_shape=(
            jax.ShapeDtypeStruct((rows, width), f32),
            jax.ShapeDtypeStruct((rows, width), f32),
            jax.ShapeDtypeStruct((2 * rows, 128), f32),
        ),
        in_specs=[in_hbm] * 4,
        out_specs=(in_vmem,) * 3,
        scratch_shapes=[
            pltpu.VMEM((n_plane, 2 * rows, width), bf16),
            pltpu.VMEM((n_line, 2 * rows, width), bf16),
            pltpu.VMEM((n_plane, 8, lanes), f32),
            pltpu.VMEM((n_line, 8, text_lanes), f32),
            pltpu.VMEM((n_plane, 2 * rows, width), f32),
            pltpu.VMEM((n_line, rows, width), f32),
            pltpu.VMEM((n_plane - 1, 2 * rows, width // 2 + 128), bf16),
            pltpu.VMEM((n_line - 1, 2 * rows, width // 2 + 128), bf16),
            pltpu.VMEM((n_plane - 1, 2 * rows, width // 2 + 128), bf16),
            pltpu.VMEM((n_line - 1, 2 * rows, width // 2 + 128), bf16),
            pltpu.SemaphoreType.DMA((3,)),
            pltpu.SemaphoreType.DMA((3,)),
            pltpu.SemaphoreType.DMA((3,)),
            pltpu.SemaphoreType.DMA((3,)),
            pltpu.VMEM((4, rows, width), bf16),
            pltpu.SemaphoreType.DMA((4,)),
        ],
        compiler_params=pltpu.CompilerParams(
            collective_id=0, has_side_effects=True, vmem_limit_bytes=32 * 1024 * 1024
        ),
    )(*operands)
    grad_image, grad_text, loss = pl.pallas_call(
        functools.partial(hand_over, rows * grp * blk),
        out_shape=(
            jax.ShapeDtypeStruct((rows, width), f32),
            jax.ShapeDtypeStruct((rows, width), f32),
            jax.ShapeDtypeStruct((1, 1), f32),
        ),
        in_specs=[in_vmem] * 3,
        out_specs=(in_hbm,) * 3,
        scratch_shapes=[pltpu.VMEM((1, 1), f32), pltpu.SemaphoreType.DMA((3,))],
        compiler_params=pltpu.CompilerParams(vmem_limit_bytes=32 * 1024 * 1024),
    )(grad_image, grad_text, loss)
    return grad_image, grad_text, loss.reshape(())


def solution(mesh):
    in_specs = (
        P(("blk", "grp"), None),
        P(("grp", "blk"), None),
        P(("blk", "grp"), None),
        P(("grp", "blk"), None),
    )
    out_specs = (P(("blk", "grp"), None), P(("grp", "blk"), None), P())
    run = functools.partial(local, mesh.shape["grp"], mesh.shape["blk"])
    return jax.shard_map(run, mesh=mesh, in_specs=in_specs, out_specs=out_specs, check_vma=False)
```
